128 devices in a mesh: slab: 32 (over z, x, core), depth: 4 (over y).
Axes of the slice: x: 4, y: 4, z: 4, core: 2. Of those that a mesh axis runs over, the one named last changes fastest.
Arguments:
- alpha: float32 [512, 256, 512], P('slab', 'depth'), may hold values from 0 to 1
- vel_x: float32 [512, 256, 512], P('slab', 'depth'), may hold values from -1 to 1
- vel_z: float32 [512, 256, 512], P('slab', 'depth'), may hold values from -1 to 1
- divergence: float32 [512, 256, 512], P('slab', 'depth'), may hold values from -6 to 6
- press_guess: float32 [512, 256, 512], P('slab', 'depth'), may hold values from -6 to 6
- panel_records: bfloat16 [32768, 128], P(('slab', 'depth')), may hold values from -6 to 6
- panel_dest: int32 [32768, 1], P(('slab', 'depth')), may hold values from 0 to 127; in each aligned block of 256 rows (0 to 255, 256 to 511, ...) at most 4 rows name the same one
- panel_segment: int32 [32768, 1], P(('slab', 'depth')), may hold values from 0 to 4095
Outputs:
- pressure: float32 [512, 256, 512], P('slab', 'depth')
- alpha_next: float32 [512, 256, 512], P('slab', 'depth')
- panel_pressure: bfloat16 [32768, 128], P(('slab', 'depth'))
The draws below stay inside these ranges and needn't reach their ends.
Inputs may be any that keep to these rules, and one draw needn't show every extreme that they name: `panel_dest`: among the 256 panels of one device no fluid device is named more than 4 times.
All inputs are finite; a program needn't handle non-finite values.
Results may differ from the reference program's by a relative error of at most 0.001.
Values may be sent and summed in bfloat16 or wider, within the bound.
A program may use at most 64 MiB of HBM per device.

```python
import math
import jax
import jax.numpy as jnp
import numpy as np

CX = 16
CZ = 64
NY = 512
PAN_DEV = 256
MORTAR = 128
NX = 512
NZ = 256
PANELS = 32768
CAP = 4
N_DEPTH = 4
DEVICES = 128


def touch_ends(result, rng, low, largest):
    extent = result.shape
    spot = [jax.random.randint(jax.random.fold_in(rng, axis), (), 0, extent[axis]) for axis in range(len(extent))]
    result = result.at[tuple(spot)].set(low)
    longest = extent.index(max(extent))
    spot[longest] = (spot[longest] + 1) % extent[longest]
    return result.at[tuple(spot)].set(largest)


def block_levels(stream_key, shape, split, low, top_value):
    factor_of, own = 1.0, jax.random.fold_in(stream_key, 6)
    for dim, shards_of in split:
        steps = jnp.exp(jax.random.uniform(jax.random.fold_in(own, dim), (shards_of,), jnp.float32, low / len(split), top_value / len(split)))
        factor_of = factor_of * jnp.repeat(steps, shape[dim] // shards_of).reshape([-1 if axis == dim else 1 for axis in range(len(shape))])
    return factor_of


def routed_block(rng, own, number, rows, amount, top, limit, slope):
    order = jax.random.permutation(rng, amount)
    packed, usual = portions_of(amount, rows * top, limit, slope, True), portions_of(amount, rows * top, limit, slope, False)
    places = jnp.arange(amount)

    def named(tallies, rotation):
        used = int((tallies > 0).sum())
        fixed = max(1, used // 4)
        passed = fixed + (places - fixed + rotation * (used - fixed)) % max(1, amount - fixed)
        return jnp.zeros((amount,), jnp.int32).at[order[jnp.where(places < fixed, places, passed)]].set(jnp.asarray(tallies, jnp.int32))

    tallies = jnp.where(number % 4 == 0, named(packed, number // 4), named(usual, number - number // 4 - 1))
    mixed = jax.random.permutation(jax.random.fold_in(own, 3), amount)
    donor, sink = mixed[0:amount // 2 * 2:2], mixed[1:amount // 2 * 2:2]
    margin = jnp.minimum(tallies[donor] - 1, limit - tallies[sink]) // 2
    margin = jnp.where((donor == order[0]) | (sink == order[0]) | (tallies[sink] == 0), 0, jnp.maximum(margin, 0))
    passed = jax.random.randint(jax.random.fold_in(own, 4), (amount // 2,), 0, 1 << 20) % (margin + 1)
    tallies = tallies.at[donor].add(-passed).at[sink].add(passed)
    items = jnp.searchsorted(jnp.cumsum(tallies), jnp.arange(rows * top), side="right").astype(jnp.int32)
    table = items.reshape(top, rows).T
    table = table[jax.random.permutation(jax.random.fold_in(own, 1), rows)]
    rotation = jax.random.randint(jax.random.fold_in(own, 2), (rows, 1), 0, top)
    return jnp.take_along_axis(table, (jnp.arange(top)[None, :] + rotation) % top, axis=1)


def portions_of(number_of, total, limit, slope, full):
    portions = [(1 << 20) // math.isqrt(standing ** slope) + 1 for standing in range(1, number_of + 1)]
    largest = limit if full else min(limit, max(-(-total // number_of), total * portions[0] // sum(portions)))
    least = 1 if total - largest >= number_of - 1 else 0
    given, surplus = [largest] + [least] * (number_of - 1), total - largest - least * (number_of - 1)
    while surplus > 0:
        free = [i for i in range(1, number_of) if given[i] < largest] or [i for i in range(1, number_of) if given[i] < limit]
        whole, budget = sum([portions[i] for i in free]), surplus
        for i in free:
            more = min(limit - given[i], max(1, budget * portions[i] // whole), surplus)
            given[i] = given[i] + more
            surplus = surplus - more
    return np.array(given)


def scatter_about(stream_key, shape, spread, bound, pieces=(), held_as=jnp.bfloat16):
    entries = jax.random.normal(stream_key, shape, jnp.float32) * spread
    if len(pieces) > 0:
        entries = block_levels(stream_key, shape, pieces, -0.22, 0.18) * entries
    return jnp.clip(entries, min=-bound, max=bound).astype(held_as)


def setup_inputs(seed: int = 0) -> dict:
    seeds = jax.random.split(jax.random.key(seed), 9)
    alpha = jnp.clip(1.0 * jax.random.uniform(seeds[0], (NX, NZ, NY), jnp.float32) ** block_levels(seeds[0], (NX, NZ, NY), ((0, 32), (1, 4)), -0.2, 0.2), 0.0, 1.0)
    vel_x = jnp.clip(jax.random.uniform(seeds[1], (NX, NZ, NY), jnp.float32, -1.0, 1.0) * block_levels(seeds[1], (NX, NZ, NY), ((0, 32), (1, 4)), -0.4, 0.0), -1.0, 1.0)
    vel_z = jnp.clip(jax.random.uniform(seeds[2], (NX, NZ, NY), jnp.float32, -1.0, 1.0) * block_levels(seeds[2], (NX, NZ, NY), ((0, 32), (1, 4)), -0.4, 0.0), -1.0, 1.0)
    divergence = scatter_about(seeds[3], (NX, NZ, NY), 1.0, 6.0, ((0, 32), (1, 4)), jnp.float32)
    press_guess = scatter_about(seeds[4], (NX, NZ, NY), 1.0, 6.0, ((0, 32), (1, 4)), jnp.float32)
    panel_records = scatter_about(seeds[5], (PANELS, MORTAR), 1.0, 6.0, ((0, 128),))
    panel_dest_keys = jax.random.split(jax.random.fold_in(seeds[6], 1), PANELS // PAN_DEV)
    panel_dest_turns = jax.random.permutation(jax.random.fold_in(seeds[6], 3), PANELS // PAN_DEV)
    panel_dest = jax.vmap(lambda own, number: routed_block(jax.random.fold_in(seeds[6], 2), own, number, PAN_DEV, DEVICES, 1, CAP, 2))(panel_dest_keys, panel_dest_turns).reshape((PANELS, 1))
    panel_segment = touch_ends(jax.random.randint(seeds[7], (PANELS, 1), 0, CX * CZ * NY // 128), jax.random.fold_in(seeds[7], 1), 0, (CX * CZ * NY // 128) - 1).astype(jnp.int32)
    return {"alpha": alpha, "vel_x": vel_x, "vel_z": vel_z, "divergence": divergence, "press_guess": press_guess, "panel_records": panel_records, "panel_dest": panel_dest, "panel_segment": panel_segment}


COURANT = 0.2


def advect_core(alpha_pad, velx_pad, velz_pad):
    face_x = velx_pad[1:, 1:-1] * jnp.where(velx_pad[1:, 1:-1] > 0, alpha_pad[:-1, 1:-1], alpha_pad[1:, 1:-1])
    face_z = velz_pad[1:-1, 1:] * jnp.where(velz_pad[1:-1, 1:] > 0, alpha_pad[1:-1, :-1], alpha_pad[1:-1, 1:])
    change = face_x[1:] - face_x[:-1] + face_z[:, 1:] - face_z[:, :-1]
    return alpha_pad[1:-1, 1:-1] - COURANT * change


def sweep(press_pad, dens_pad, rhs):
    press_pad = jnp.pad(press_pad, ((0, 0), (0, 0), (1, 1)))
    dens_pad = jnp.pad(dens_pad, ((0, 0), (0, 0), (1, 1)))
    rows_all = rhs.shape[0]
    cols_all = rhs.shape[1]
    beam = rhs.shape[2]
    own_rho = dens_pad[1:1 + rows_all, 1:1 + cols_all, 1:1 + beam]
    total = jnp.zeros_like(rhs)
    weight = jnp.zeros_like(rhs)
    for off_x, off_z, off_y in ((0, 1, 1), (2, 1, 1), (1, 0, 1), (1, 2, 1), (1, 1, 0), (1, 1, 2)):
        next_p = press_pad[off_x:off_x + rows_all, off_z:off_z + cols_all, off_y:off_y + beam]
        next_rho = dens_pad[off_x:off_x + rows_all, off_z:off_z + cols_all, off_y:off_y + beam]
        coeff = 2.0 / (own_rho + next_rho)
        total = total + coeff * next_p
        weight = weight + coeff
    return (total - rhs) / weight


def pad_two(field):
    return jnp.pad(field, ((1, 1), (1, 1), (0, 0)))


def reference(alpha, vel_x, vel_z, divergence, press_guess, panel_records, panel_dest, panel_segment):
    blocks = NY // 128
    target = panel_dest[:, 0]
    segment = panel_segment[:, 0]
    slab_of = target // N_DEPTH
    depth_of = target % N_DEPTH
    local_x = segment // (CZ * blocks)
    local_z = (segment // blocks) % CZ
    block_y = segment % blocks
    global_row = ((slab_of * CX + local_x) * NZ + depth_of * CZ + local_z) * blocks + block_y
    global_row = global_row.astype(jnp.int32)
    hull = jnp.zeros((NX * NZ * blocks, 128), jnp.float32).at[global_row].add(panel_records.astype(jnp.float32))
    hull = hull.reshape(NX, NZ, NY)
    alpha_next = advect_core(pad_two(alpha), pad_two(vel_x), pad_two(vel_z))
    density = 1.0 + 9.0 * alpha_next
    rhs = divergence + hull
    dens_pad = pad_two(density)
    pressure = press_guess
    for sweep_number in range(3):
        pressure = sweep(pad_two(pressure), dens_pad, rhs)
    panel_pressure = pressure.reshape(-1, 128).astype(jnp.bfloat16)[global_row]
    return pressure, alpha_next, panel_pressure
```

```python
import jax
import jax.numpy as jnp
from jax import lax
from jax.experimental import pallas as pl
from jax.experimental.pallas import tpu as pltpu
from jax.sharding import PartitionSpec as P

MESH = pl.DeviceIdType.MESH
F32, BF16, I32 = jnp.float32, jnp.bfloat16, jnp.int32
CX, CZ, BEAM, LANES = 16, 64, 512, 128
NB = BEAM // LANES
ROW0 = 8
PADZ = CZ + 16
SLABS, DEPTHS = 32, 4
GA, GB = 8, 16
CAP = 4
SLOTS = GA * GB * CAP
PAN = 256
REC_B, REC_A = GA * CAP, GB * CAP
META = 16


def iota(shape, dim):
    return lax.broadcasted_iota(I32, shape, dim)


def onehot(cond):
    return jnp.where(cond, 1.0, 0.0).astype(BF16)


def dot(a, b):
    return jnp.dot(a, b, preferred_element_type=F32)


def recip(d):
    r = pl.reciprocal(d, approx=True)
    return r * (2.0 - d * r)


def kernel(
    alpha_h, velx_h, velz_h, div_h, press_h, rec_ref, dest_ref, seg_ref,
    press_o, alpha_o, panel_o,
    al, vx, vz, div, rho, p0, p1, p2, an_s, pr_s,
    axm, axp, azm, azp, aym, ayp, rr,
    zs, zr,
    s1, r1, s2, r2, s3, t1, s4, t2,
    q_s, g_s, perm_s, rmat, pb,
    load_sem, out_sem, xs_sem, xr_sem, zs_sem, zr_sem,
    b1s, b1r, a1s, a1r, a2s, a2r, b2s, b2r,
):
    slab = lax.axis_index("slab")
    depth = lax.axis_index("depth")
    up_s, dn_s = (slab + 1) % SLABS, (slab + SLABS - 1) % SLABS
    up_d, dn_d = (depth + 1) % DEPTHS, (depth + DEPTHS - 1) % DEPTHS
    x_up, x_dn = (up_s, depth), (dn_s, depth)
    z_up, z_dn = (slab, up_d), (slab, dn_d)
    b_me, core = slab // 2, slab % 2
    a_me = core * DEPTHS + depth

    def b_peer(k):
        b = (b_me + k) % GB
        return b, (b * 2 + core, depth)

    def a_peer(k):
        a = (a_me + k) % GA
        return a, (b_me * 2 + a // DEPTHS, a % DEPTHS)

    loads = {}
    sem_i = 0
    for name, src, dst in (
        ("al", alpha_h, lambda y: al.at[pl.ds(1, CX), y, pl.ds(ROW0, CZ), :]),
        ("vx", velx_h, lambda y: vx.at[pl.ds(0, CX), y, :, :]),
        ("vz", velz_h, lambda y: vz.at[:, y, pl.ds(0, CZ), :]),
        ("p0", press_h, lambda y: p0.at[pl.ds(1, CX), y, pl.ds(ROW0, CZ), :]),
        ("div", div_h, lambda y: div.at[:, y, :, :]),
    ):
        loads[name] = []
        for y in range(NB):
            c = pltpu.make_async_copy(
                src.at[:, :, pl.ds(y * LANES, LANES)], dst(y), load_sem.at[sem_i]
            )
            c.start()
            sem_i += 1
            loads[name].append(c)

    barrier = pltpu.get_barrier_semaphore()
    for dev in (x_up, x_dn, z_up, z_dn):
        pl.semaphore_signal(barrier, inc=1, device_id=dev, device_id_type=MESH)

    def sig_b(k, c):
        pl.semaphore_signal(barrier, inc=1, device_id=b_peer(k)[1], device_id_type=MESH)
        return c

    def sig_a(k, c):
        pl.semaphore_signal(barrier, inc=1, device_id=a_peer(k)[1], device_id_type=MESH)
        return c

    lax.fori_loop(1, GB, sig_b, 0)
    lax.fori_loop(1, GA, sig_a, 0)

    dest, seg = dest_ref[...], seg_ref[...]
    own = onehot(iota((GA * GB, PAN), 0) == dest)
    before = dot(own, onehot(iota((PAN, PAN), 0) < iota((PAN, PAN), 1)))
    slot = jnp.sum(own.astype(F32) * before, axis=0, keepdims=True)
    place = dest * CAP + slot.astype(I32)
    packed = dot(onehot(iota((SLOTS, PAN), 0) == place), rec_ref[...]).astype(BF16)
    lane_of = place & (REC_B - 1)
    row = iota((LANES, PAN), 0)
    hi, lo = (seg >> 6).astype(F32), (seg & 63).astype(F32)
    bt = jnp.where(row == lane_of, hi, 0.0) + jnp.where(row == lane_of + REC_B, lo, 0.0)
    meta = lax.dot_general(
        onehot(iota((GB, PAN), 0) == (dest >> 3)), bt.astype(BF16),
        (((1,), (1,)), ((), ())), preferred_element_type=F32,
    )
    for b in range(GB):
        s1[b, 0:REC_B, :] = packed[b * REC_B : (b + 1) * REC_B]
        s1[b, REC_B:, :] = jnp.broadcast_to(meta[b : b + 1], (META, LANES)).astype(BF16)
    place_t = jnp.broadcast_to(place.astype(F32), (LANES, PAN)).T
    for c in range(SLOTS // LANES):
        q_s[:, c * LANES : (c + 1) * LANES] = onehot(
            place_t == (iota((PAN, LANES), 1) + c * LANES).astype(F32)
        )

    def rcopy(src, dst, ss, rs, dev):
        return pltpu.make_async_remote_copy(
            src_ref=src, dst_ref=dst, send_sem=ss, recv_sem=rs,
            device_id=dev, device_id_type=MESH,
        )

    def xcopy(i, src, src_x, dst_x, dev, padded=True):
        rows = pl.ds(ROW0, CZ) if padded else pl.ds(0, CZ)
        return rcopy(
            src.at[src_x, :, rows, :], src.at[dst_x, :, rows, :], xs_sem.at[i], xr_sem.at[i], dev
        )

    def zcopy(i, dev):
        return rcopy(zs.at[i], zr.at[i], zs_sem.at[i], zr_sem.at[i], dev)

    def xpair(i, ref):
        return [xcopy(i, ref, CX, 0, x_up), xcopy(i + 1, ref, 1, CX + 1, x_dn)]

    def zpair(i):
        return [zcopy(i, z_up), zcopy(i + 1, z_dn)]

    def pack_z(items):
        def step(x, c):
            for i, ref, xo, r in items:
                zs[i, x] = ref[x + xo, :, r, :]
            return c

        lax.fori_loop(0, CX, step, 0)

    def fill_z(items):
        def step(x, c):
            for i, ref, xo, r, edge in items:
                zero = depth == edge
                ref[x + xo, :, r, :] = jnp.where(zero, 0.0, zr[i, x])
            return c

        lax.fori_loop(0, CX, step, 0)

    def zero_x(ref):
        @pl.when(slab == 0)
        def _():
            ref[0, :, ROW0 : ROW0 + CZ, :] = jnp.zeros((NB, CZ, LANES), F32)

        @pl.when(slab == SLABS - 1)
        def _():
            ref[CX + 1, :, ROW0 : ROW0 + CZ, :] = jnp.zeros((NB, CZ, LANES), F32)

    sends = []

    def start(copies):
        for c in copies:
            c.start()
        sends.extend(copies)

    for name in ("al", "vx", "vz"):
        for c in loads[name]:
            c.wait()
    pack_z([(0, al, 1, ROW0 + CZ - 1), (1, al, 1, ROW0), (2, vz, 0, 0)])
    pl.semaphore_wait(barrier, 4 + (GB - 1) + (GA - 1))
    e_al, e_vx = xpair(0, al), [xcopy(2, vx, 0, CX, x_dn, padded=False)]
    ez_al, ez_vz = zpair(0), [zcopy(2, z_dn)]
    start(e_al + e_vx + ez_al + ez_vz)

    def b1_copy(k):
        b, dev = b_peer(k)
        return rcopy(s1.at[b], r1.at[b_me], b1s.at[k], b1r.at[k], dev)

    def b1_start(k, c):
        b1_copy(k).start()
        return c

    lax.fori_loop(1, GB, b1_start, 0)
    r1[b_me] = s1[b_me]

    for c in loads["p0"]:
        c.wait()
    pack_z([(3, p0, 1, ROW0 + CZ - 1), (4, p0, 1, ROW0)])
    e_p0, ez_p0 = xpair(3, p0), zpair(3)
    start(e_p0 + ez_p0)

    lane = iota((NB, 8, LANES), 2)
    zero1 = jnp.zeros((1, 8, LANES), F32)

    def y_minus(v):
        r = pltpu.roll(v, 1, 2)
        return jnp.where(lane == 0, jnp.concatenate([zero1, r[: NB - 1]], axis=0), r)

    def y_plus(v):
        r = pltpu.roll(v, LANES - 1, 2)
        return jnp.where(lane == LANES - 1, jnp.concatenate([r[1:], zero1], axis=0), r)

    def at(ref, x, z, shift=0):
        return ref[x, :, pl.ds(ROW0 + z * 8 + shift, 8), :]

    def raw(ref, x, z, shift=0):
        return ref[x, :, pl.ds(z * 8 + shift, 8), :]

    def to_out(ref, x, z, v):
        for y in range(NB):
            ref[x, pl.ds(z * 8, 8), y * LANES : (y + 1) * LANES] = v[y]

    def advect(x, z):
        a = at(al, x + 1, z)
        u0, u1 = raw(vx, x, z), raw(vx, x + 1, z)
        w0, w1 = raw(vz, x, z), raw(vz, x, z, 1)
        fx0 = u0 * jnp.where(u0 > 0, at(al, x, z), a)
        fx1 = u1 * jnp.where(u1 > 0, a, at(al, x + 2, z))
        fz0 = w0 * jnp.where(w0 > 0, at(al, x + 1, z, -1), a)
        fz1 = w1 * jnp.where(w1 > 0, a, at(al, x + 1, z, 1))
        new = a - 0.2 * (fx1 - fx0 + fz1 - fz0)
        to_out(an_s, x, z, new)
        rho[x + 1, :, pl.ds(ROW0 + z * 8, 8), :] = 1.0 + 9.0 * new

    def first(x, z):
        d = at(rho, x + 1, z)
        c = (
            recip(d + at(rho, x, z)), recip(d + at(rho, x + 2, z)),
            recip(d + at(rho, x + 1, z, -1)), recip(d + at(rho, x + 1, z, 1)),
            recip(d + y_minus(d)), recip(d + y_plus(d)),
        )
        inv = recip(c[0] + c[1] + c[2] + c[3] + c[4] + c[5])
        c = [v * inv for v in c]
        r = 0.5 * raw(div, x, z) * inv
        for ref, v in zip((axm, axp, azm, azp, aym, ayp, rr), c + [r]):
            ref[x, :, pl.ds(z * 8, 8), :] = v
        return apply(p0, c, r, x, z)

    def apply(p, c, r, x, z):
        q = at(p, x + 1, z)
        return (
            (c[0] * at(p, x, z) + c[1] * at(p, x + 2, z))
            + (c[2] * at(p, x + 1, z, -1) + c[3] * at(p, x + 1, z, 1))
            + (c[4] * y_minus(q) + c[5] * y_plus(q) - r)
        )

    def later(p, x, z):
        c = [raw(ref, x, z) for ref in (axm, axp, azm, azp, aym, ayp)]
        return apply(p, c, raw(rr, x, z), x, z)

    def sweep1(x, z):
        p1[x + 1, :, pl.ds(ROW0 + z * 8, 8), :] = first(x, z)

    def sweep2(x, z):
        p2[x + 1, :, pl.ds(ROW0 + z * 8, 8), :] = later(p1, x, z)

    def sweep3(x, z):
        to_out(pr_s, x, z, later(p2, x, z))

    tiles = CZ // 8

    def interior(fn, zs_):
        def step(x, c):
            for z in zs_:
                fn(x, z)
            return c

        lax.fori_loop(1, CX - 1, step, 0)

    def ends(fn):
        def step(z, c):
            fn(0, z)
            fn(CX - 1, z)
            return c

        lax.fori_loop(0, tiles, step, 0)

    inner, edge = range(1, tiles - 1), (0, tiles - 1)

    def recv(copies):
        for c in copies:
            c.wait_recv()

    interior(advect, inner)
    recv(ez_al + ez_vz)
    fill_z([(0, al, 1, ROW0 - 1, 0), (1, al, 1, ROW0 + CZ, DEPTHS - 1), (2, vz, 0, CZ, DEPTHS - 1)])
    interior(advect, edge)
    recv(e_al + e_vx)
    zero_x(al)

    @pl.when(slab == SLABS - 1)
    def _():
        vx[CX] = jnp.zeros((NB, CZ, LANES), F32)

    ends(advect)
    e_rho, ez_rho = xpair(5, rho), zpair(5)
    start(e_rho)
    pack_z([(5, rho, 1, ROW0 + CZ - 1), (6, rho, 1, ROW0)])
    start(ez_rho)
    out_alpha = pltpu.make_async_copy(an_s, alpha_o, out_sem.at[0])
    out_alpha.start()

    def b1_wait(k, c):
        src = (b_me + GB - k) % GB
        rcopy(s1.at[src], r1.at[src], b1s.at[k], b1r.at[k], b_peer(k)[1]).wait_recv()
        return c

    lax.fori_loop(1, GB, b1_wait, 0)
    pr, pc = iota((SLOTS, SLOTS), 0), iota((SLOTS, SLOTS), 1)
    perm_s[...] = onehot(
        pc == (((pr >> 2) & (GB - 1)) * REC_B + (pr >> 6) * CAP + (pr & 3))
    )
    got = dot(perm_s[...], r1[:, 0:REC_B, :].reshape(SLOTS, LANES)).astype(BF16)
    brow = iota((META, LANES), 0)
    m1 = jnp.zeros((META, LANES), F32)
    for b in range(GB):
        m1 = jnp.where(brow == b, r1[b, REC_B:, :].astype(F32), m1)
    m1 = m1.astype(BF16)
    for a in range(GA):
        s2[a, 0:REC_A, :] = got[a * REC_A : (a + 1) * REC_A]
        s2[a, REC_A:, :] = m1

    def a1_copy(k):
        a, dev = a_peer(k)
        return rcopy(s2.at[a], r2.at[a_me], a1s.at[k], a1r.at[k], dev)

    def a1_start(k, c):
        a1_copy(k).start()
        return c

    lax.fori_loop(1, GA, a1_start, 0)
    r2[a_me] = s2[a_me]
    perm_s[...] = onehot(
        pc == (((pr >> 2) & (GA - 1)) * REC_A + (pr >> 5) * CAP + (pr & 3))
    )
    for c in loads["div"]:
        c.wait()

    def a1_wait(k, c):
        src = (a_me + GA - k) % GA
        rcopy(s2.at[src], r2.at[src], a1s.at[k], a1r.at[k], a_peer(k)[1]).wait_recv()
        return c

    lax.fori_loop(1, GA, a1_wait, 0)

    m2 = r2[:, REC_A:, :].reshape(GA * GB, LANES)
    wide = dot(onehot((iota((SLOTS, LANES), 0) >> 2) == iota((SLOTS, LANES), 1)), m2)
    pick = iota((SLOTS, LANES), 1) - (iota((SLOTS, LANES), 0) & 3) - a_me * CAP
    hi_c = jnp.sum(jnp.where(pick == 0, wide, 0.0), axis=1, keepdims=True)
    lo_c = jnp.sum(jnp.where(pick == REC_B, wide, 0.0), axis=1, keepdims=True)
    seg_c = hi_c.astype(I32) * 64 + lo_c.astype(I32)
    block_c, key_c = seg_c & 3, seg_c >> 2
    key_f = jnp.broadcast_to(key_c, (SLOTS, LANES)).astype(F32)
    key_r = key_f.T[0:1]
    for c in range(CX * CZ // LANES):
        g_s[:, c * LANES : (c + 1) * LANES] = onehot(
            key_f == (iota((SLOTS, LANES), 1) + c * LANES).astype(F32)
        )
    recs = r2[:, 0:REC_A, :].reshape(SLOTS, LANES)
    for y in range(NB):
        rmat[:, y * LANES : (y + 1) * LANES] = jnp.where(
            block_c == y, recs.astype(F32), 0.0
        ).astype(BF16)

    def hull(x, c):
        cells = (iota((CZ, SLOTS), 0) + x * CZ).astype(F32)
        h = dot(onehot(cells == key_r), rmat[...])
        for y in range(NB):
            div[x, y] += h[:, y * LANES : (y + 1) * LANES]
        return c

    lax.fori_loop(0, CX, hull, 0)

    interior(sweep1, inner)
    recv(ez_p0 + ez_rho)
    fill_z([
        (3, p0, 1, ROW0 - 1, 0), (4, p0, 1, ROW0 + CZ, DEPTHS - 1),
        (5, rho, 1, ROW0 - 1, 0), (6, rho, 1, ROW0 + CZ, DEPTHS - 1),
    ])
    interior(sweep1, edge)
    recv(e_p0 + e_rho)
    zero_x(p0)
    zero_x(rho)
    ends(sweep1)
    e_p1, ez_p1 = xpair(7, p1), zpair(7)
    start(e_p1)
    pack_z([(7, p1, 1, ROW0 + CZ - 1), (8, p1, 1, ROW0)])
    start(ez_p1)
    interior(sweep2, inner)
    recv(ez_p1)
    fill_z([(7, p1, 1, ROW0 - 1, 0), (8, p1, 1, ROW0 + CZ, DEPTHS - 1)])
    interior(sweep2, edge)
    recv(e_p1)
    zero_x(p1)
    ends(sweep2)
    e_p2, ez_p2 = xpair(9, p2), zpair(9)
    start(e_p2)
    pack_z([(9, p2, 1, ROW0 + CZ - 1), (10, p2, 1, ROW0)])
    start(ez_p2)
    interior(sweep3, inner)
    recv(ez_p2)
    fill_z([(9, p2, 1, ROW0 - 1, 0), (10, p2, 1, ROW0 + CZ, DEPTHS - 1)])
    interior(sweep3, edge)
    recv(e_p2)
    zero_x(p2)
    ends(sweep3)
    out_press = pltpu.make_async_copy(pr_s, press_o, out_sem.at[1])
    out_press.start()

    for x in range(CX):
        pb[x * CZ : (x + 1) * CZ, :] = pr_s[x].astype(BF16)
    wet = dot(g_s[...], pb[...])
    back = jnp.zeros((SLOTS, LANES), F32)
    for y in range(NB):
        back = jnp.where(block_c == y, wet[:, y * LANES : (y + 1) * LANES], back)
    back = back.astype(BF16)
    for a in range(GA):
        s3[a] = back[a * REC_A : (a + 1) * REC_A]

    def a2_start(k, c):
        a, dev = a_peer(k)
        rcopy(s3.at[a], t1.at[a_me], a2s.at[k], a2r.at[k], dev).start()
        return c

    def a2_wait(k, c):
        src = (a_me + GA - k) % GA
        rcopy(s3.at[src], t1.at[src], a2s.at[k], a2r.at[k], a_peer(k)[1]).wait_recv()
        return c

    lax.fori_loop(1, GA, a2_start, 0)
    t1[a_me] = s3[a_me]
    lax.fori_loop(1, GA, a2_wait, 0)
    turned = dot(perm_s[...], t1[...].reshape(SLOTS, LANES)).astype(BF16)
    for b in range(GB):
        s4[b] = turned[b * REC_B : (b + 1) * REC_B]

    def b2_start(k, c):
        b, dev = b_peer(k)
        rcopy(s4.at[b], t2.at[b_me], b2s.at[k], b2r.at[k], dev).start()
        return c

    def b2_wait(k, c):
        src = (b_me + GB - k) % GB
        rcopy(s4.at[src], t2.at[src], b2s.at[k], b2r.at[k], b_peer(k)[1]).wait_recv()
        return c

    lax.fori_loop(1, GB, b2_start, 0)
    t2[b_me] = s4[b_me]
    lax.fori_loop(1, GB, b2_wait, 0)
    panel_o[...] = dot(q_s[...], t2[...].reshape(SLOTS, LANES)).astype(BF16)

    for c in sends:
        c.wait_send()

    def b_done(k, c):
        b, dev = b_peer(k)
        rcopy(s1.at[b], r1.at[b_me], b1s.at[k], b1r.at[k], dev).wait_send()
        rcopy(s4.at[b], t2.at[b_me], b2s.at[k], b2r.at[k], dev).wait_send()
        return c

    def a_done(k, c):
        a, dev = a_peer(k)
        rcopy(s2.at[a], r2.at[a_me], a1s.at[k], a1r.at[k], dev).wait_send()
        rcopy(s3.at[a], t1.at[a_me], a2s.at[k], a2r.at[k], dev).wait_send()
        return c

    lax.fori_loop(1, GB, b_done, 0)
    lax.fori_loop(1, GA, a_done, 0)
    out_alpha.wait()
    out_press.wait()


def body(alpha, vel_x, vel_z, divergence, press_guess, panel_records, panel_dest, panel_segment):
    padded = pltpu.VMEM((CX + 2, NB, PADZ, LANES), F32)
    plain = pltpu.VMEM((CX, NB, CZ, LANES), F32)
    natural = pltpu.VMEM((CX, CZ, BEAM), F32)
    hbm = pl.BlockSpec(memory_space=pl.ANY)
    vmem = pl.BlockSpec(memory_space=pltpu.VMEM)
    dma = lambda n: pltpu.SemaphoreType.DMA((n,))
    field = jax.ShapeDtypeStruct((CX, CZ, BEAM), F32)
    return pl.pallas_call(
        kernel,
        out_shape=(field, field, jax.ShapeDtypeStruct((PAN, LANES), BF16)),
        in_specs=[hbm] * 5 + [vmem] * 3,
        out_specs=(hbm, hbm, vmem),
        scratch_shapes=[
            padded,
            pltpu.VMEM((CX + 1, NB, CZ, LANES), F32),
            pltpu.VMEM((CX, NB, CZ + 8, LANES), F32),
            plain,
            padded, padded, padded, padded,
            natural, natural,
            plain, plain, plain, plain, plain, plain, plain,
            pltpu.VMEM((11, CX, NB, LANES), F32),
            pltpu.VMEM((11, CX, NB, LANES), F32),
            pltpu.VMEM((GB, REC_B + META, LANES), BF16),
            pltpu.VMEM((GB, REC_B + META, LANES), BF16),
            pltpu.VMEM((GA, REC_A + META, LANES), BF16),
            pltpu.VMEM((GA, REC_A + META, LANES), BF16),
            pltpu.VMEM((GA, REC_A, LANES), BF16),
            pltpu.VMEM((GA, REC_A, LANES), BF16),
            pltpu.VMEM((GB, REC_B, LANES), BF16),
            pltpu.VMEM((GB, REC_B, LANES), BF16),
            pltpu.VMEM((PAN, SLOTS), BF16),
            pltpu.VMEM((SLOTS, CX * CZ), BF16),
            pltpu.VMEM((SLOTS, SLOTS), BF16),
            pltpu.VMEM((SLOTS, BEAM), BF16),
            pltpu.VMEM((CX * CZ, BEAM), BF16),
            dma(20), dma(2), dma(11), dma(11), dma(11), dma(11),
            dma(GB), dma(GB), dma(GA), dma(GA), dma(GA), dma(GA), dma(GB), dma(GB),
        ],
        compiler_params=pltpu.CompilerParams(
            collective_id=0, has_side_effects=True, vmem_limit_bytes=60 * 1024 * 1024
        ),
    )(
        alpha, vel_x, vel_z, divergence, press_guess, panel_records,
        panel_dest.reshape(1, PAN), panel_segment.reshape(1, PAN),
    )


def solution(mesh):
    field = P("slab", "depth", None)
    rows = P(("slab", "depth"), None)
    return jax.shard_map(
        body, mesh=mesh, in_specs=(field,) * 5 + (rows,) * 3,
        out_specs=(field, field, rows), check_vma=False,
    )
```

```python
import jax
import jax.numpy as jnp
from jax import lax
from jax.experimental import pallas as pl
from jax.experimental.pallas import tpu as pltpu
from jax.sharding import PartitionSpec as P

MESH = pl.DeviceIdType.MESH
F32, BF16, I32 = jnp.float32, jnp.bfloat16, jnp.int32
CX, CZ, BEAM, LANES = 16, 64, 512, 128
NB = BEAM // LANES
ROW0 = 8
PADZ = CZ + 16
SLABS, DEPTHS = 32, 4
GA, GB = 8, 16
CAP = 4
SLOTS = GA * GB * CAP
PAN = 256
REC_B, REC_A = GA * CAP, GB * CAP
META = 16


def iota(shape, dim):
    return lax.broadcasted_iota(I32, shape, dim)


def onehot(cond):
    return jnp.where(cond, 1.0, 0.0).astype(BF16)


def dot(a, b):
    return jnp.dot(a, b, preferred_element_type=F32)


def recip(d):
    r = pl.reciprocal(d, approx=True)
    return r * (2.0 - d * r)


def kernel(
    alpha_h, velx_h, velz_h, div_h, press_h, rec_ref, dest_ref, seg_ref,
    press_o, alpha_o, panel_o,
    al, vx, vz, div, rho, p0, p1, p2,
    axm, axp, azm, azp, aym, ayp, rr,
    zs, zr,
    s1, r1, s2, r2, s3, t1, s4, t2,
    q_s, g_s, perm_s, rmat, pb,
    load_sem, xs_sem, xr_sem, zs_sem, zr_sem,
    b1s, b1r, a1s, a1r, a2s, a2r, b2s, b2r,
):
    slab = lax.axis_index("slab")
    depth = lax.axis_index("depth")
    up_s, dn_s = (slab + 1) % SLABS, (slab + SLABS - 1) % SLABS
    up_d, dn_d = (depth + 1) % DEPTHS, (depth + DEPTHS - 1) % DEPTHS
    x_up, x_dn = (up_s, depth), (dn_s, depth)
    z_up, z_dn = (slab, up_d), (slab, dn_d)
    b_me, core = slab // 2, slab % 2
    a_me = core * DEPTHS + depth

    def b_peer(k):
        b = (b_me + k) % GB
        return b, (b * 2 + core, depth)

    def a_peer(k):
        a = (a_me + k) % GA
        return a, (b_me * 2 + a // DEPTHS, a % DEPTHS)

    loads = {}
    sem_i = 0
    for name, src, dst in (
        ("al", alpha_h, lambda y: al.at[pl.ds(1, CX), y, pl.ds(ROW0, CZ), :]),
        ("vx", velx_h, lambda y: vx.at[pl.ds(0, CX), y, :, :]),
        ("vz", velz_h, lambda y: vz.at[:, y, pl.ds(0, CZ), :]),
        ("p0", press_h, lambda y: p0.at[pl.ds(1, CX), y, pl.ds(ROW0, CZ), :]),
        ("div", div_h, lambda y: div.at[:, y, :, :]),
    ):
        loads[name] = []
        for y in range(NB):
            c = pltpu.make_async_copy(
                src.at[:, :, pl.ds(y * LANES, LANES)], dst(y), load_sem.at[sem_i]
            )
            c.start()
            sem_i += 1
            loads[name].append(c)

    barrier = pltpu.get_barrier_semaphore()
    for dev in (x_up, x_dn, z_up, z_dn):
        pl.semaphore_signal(barrier, inc=1, device_id=dev, device_id_type=MESH)

    def sig_b(k, c):
        pl.semaphore_signal(barrier, inc=1, device_id=b_peer(k)[1], device_id_type=MESH)
        return c

    def sig_a(k, c):
        pl.semaphore_signal(barrier, inc=1, device_id=a_peer(k)[1], device_id_type=MESH)
        return c

    lax.fori_loop(1, GB, sig_b, 0)
    lax.fori_loop(1, GA, sig_a, 0)

    dest, seg = dest_ref[...], seg_ref[...]
    own = onehot(iota((GA * GB, PAN), 0) == dest)
    before = dot(own, onehot(iota((PAN, PAN), 0) < iota((PAN, PAN), 1)))
    slot = jnp.sum(own.astype(F32) * before, axis=0, keepdims=True)
    lane_of = (dest >> 3) * CAP + slot.astype(I32)
    place = (dest & (GA - 1)) * REC_A + lane_of
    packed = dot(onehot(iota((SLOTS, PAN), 0) == place), rec_ref[...]).astype(BF16)
    row = iota((LANES, PAN), 0)
    hi, lo = (seg >> 6).astype(F32), (seg & 63).astype(F32)
    bt = jnp.where(row == lane_of, hi, 0.0) + jnp.where(row == lane_of + REC_A, lo, 0.0)
    meta = lax.dot_general(
        onehot(iota((16, PAN), 0) == (dest & (GA - 1))), bt.astype(BF16),
        (((1,), (1,)), ((), ())), preferred_element_type=F32,
    )
    for a in range(GA):
        s1[a, 0:REC_A, :] = packed[a * REC_A : (a + 1) * REC_A]
        s1[a, REC_A:, :] = jnp.broadcast_to(meta[a : a + 1], (META, LANES)).astype(BF16)

    def rcopy(src, dst, ss, rs, dev):
        return pltpu.make_async_remote_copy(
            src_ref=src, dst_ref=dst, send_sem=ss, recv_sem=rs,
            device_id=dev, device_id_type=MESH,
        )

    def xcopy(i, src, src_x, dst_x, dev, padded=True):
        rows = pl.ds(ROW0, CZ) if padded else pl.ds(0, CZ)
        return rcopy(
            src.at[src_x, :, rows, :], src.at[dst_x, :, rows, :], xs_sem.at[i], xr_sem.at[i], dev
        )

    def zcopy(i, dev):
        return rcopy(zs.at[i], zr.at[i], zs_sem.at[i], zr_sem.at[i], dev)

    def xpair(i, ref):
        return [xcopy(i, ref, CX, 0, x_up), xcopy(i + 1, ref, 1, CX + 1, x_dn)]

    def zpair(i):
        return [zcopy(i, z_up), zcopy(i + 1, z_dn)]

    def pack_z(items):
        def step(g, c):
            for k in range(4):
                x = g * 4 + k
                for i, ref, xo, r in items:
                    zs[i, x] = ref[x + xo, :, r, :]
            return c

        lax.fori_loop(0, CX // 4, step, 0)

    def fill_z(items):
        def step(g, c):
            for k in range(4):
                x = g * 4 + k
                for i, ref, xo, r, edge in items:
                    ref[x + xo, :, r, :] = jnp.where(depth == edge, 0.0, zr[i, x])
            return c

        lax.fori_loop(0, CX // 4, step, 0)

    def zero_x(ref):
        @pl.when(slab == 0)
        def _():
            ref[0, :, ROW0 : ROW0 + CZ, :] = jnp.zeros((NB, CZ, LANES), F32)

        @pl.when(slab == SLABS - 1)
        def _():
            ref[CX + 1, :, ROW0 : ROW0 + CZ, :] = jnp.zeros((NB, CZ, LANES), F32)

    sends = []

    def start(copies):
        for c in copies:
            c.start()
        sends.extend(copies)

    for name in ("al", "vx", "vz"):
        for c in loads[name]:
            c.wait()
    pack_z([(0, al, 1, ROW0 + CZ - 1), (1, al, 1, ROW0), (2, vz, 0, 0)])
    pl.semaphore_wait(barrier, 4 + (GB - 1) + (GA - 1))
    e_al, e_vx = xpair(0, al), [xcopy(2, vx, 0, CX, x_dn, padded=False)]
    ez_al, ez_vz = zpair(0), [zcopy(2, z_dn)]
    start(e_al + e_vx + ez_al + ez_vz)

    def a1_start(k, c):
        a, dev = a_peer(k)
        rcopy(s1.at[a], r1.at[a_me], a1s.at[k], a1r.at[k], dev).start()
        return c

    lax.fori_loop(1, GA, a1_start, 0)
    r1[a_me] = s1[a_me]

    for c in loads["p0"]:
        c.wait()
    pack_z([(3, p0, 1, ROW0 + CZ - 1), (4, p0, 1, ROW0)])
    e_p0, ez_p0 = xpair(3, p0), zpair(3)
    start(e_p0 + ez_p0)

    place_t = jnp.broadcast_to(place.astype(F32), (LANES, PAN)).T
    for c in range(SLOTS // LANES):
        q_s[:, c * LANES : (c + 1) * LANES] = onehot(
            place_t == (iota((PAN, LANES), 1) + c * LANES).astype(F32)
        )
    pr, pc = iota((SLOTS, SLOTS), 0), iota((SLOTS, SLOTS), 1)
    perm_s[...] = onehot(
        pc == (((pr >> 2) & (GA - 1)) * REC_A + (pr >> 5) * CAP + (pr & 3))
    )

    lane = iota((NB, 8, LANES), 2)
    last = (lane == LANES - 1) & (iota((NB, 8, LANES), 0) == NB - 1)
    zero1 = jnp.zeros((1, 8, LANES), F32)

    def y_minus(v):
        r = pltpu.roll(v, 1, 2)
        return jnp.where(lane == 0, jnp.concatenate([zero1, r[: NB - 1]], axis=0), r)

    def y_plus(v):
        r = pltpu.roll(v, LANES - 1, 2)
        return jnp.where(lane == LANES - 1, jnp.concatenate([r[1:], zero1], axis=0), r)

    def at(ref, x, z, shift=0):
        return ref[x, :, pl.ds(ROW0 + z * 8 + shift, 8), :]

    def raw(ref, x, z, shift=0):
        return ref[x, :, pl.ds(z * 8 + shift, 8), :]

    def to_out(ref, x, z, v):
        for y in range(NB):
            ref[x, pl.ds(z * 8, 8), y * LANES : (y + 1) * LANES] = v[y]

    def advect(xs, z):
        a, right, fx1, u1 = at(al, xs[0] + 1, z), None, None, None
        left, u0 = at(al, xs[0], z), raw(vx, xs[0], z)
        fx0 = u0 * jnp.where(u0 > 0, left, a)
        for x in xs:
            right, u1 = at(al, x + 2, z), raw(vx, x + 1, z)
            w0, w1 = raw(vz, x, z), raw(vz, x, z, 1)
            fx1 = u1 * jnp.where(u1 > 0, a, right)
            fz0 = w0 * jnp.where(w0 > 0, at(al, x + 1, z, -1), a)
            fz1 = w1 * jnp.where(w1 > 0, a, at(al, x + 1, z, 1))
            new = a - 0.2 * (fx1 - fx0 + fz1 - fz0)
            to_out(alpha_o, x, z, new)
            rho[x + 1, :, pl.ds(ROW0 + z * 8, 8), :] = 1.0 + 9.0 * new
            a, fx0 = right, fx1

    def coefficients(xs, z):
        d = at(rho, xs[0] + 1, z)
        cm = recip(d + at(rho, xs[0], z))
        for x in xs:
            right = at(rho, x + 2, z)
            cp = recip(d + right)
            zm, zp = recip(d + at(rho, x + 1, z, -1)), recip(d + at(rho, x + 1, z, 1))
            ym = recip(d + y_minus(d))
            yp = y_plus(ym)
            yp = jnp.where(last, recip(d), yp)
            inv = recip((cm + cp) + (zm + zp) + (ym + yp))
            for ref, v in zip((axm, axp, azm, azp, aym, ayp), (cm, cp, zm, zp, ym, yp)):
                ref[x, :, pl.ds(z * 8, 8), :] = v * inv
            rr[x, :, pl.ds(z * 8, 8), :] = 0.5 * inv
            d, cm = right, cp

    def sweep(p, store, xs, z):
        left, mid = at(p, xs[0], z), at(p, xs[0] + 1, z)
        for x in xs:
            right = at(p, x + 2, z)
            store(
                x, z,
                (raw(axm, x, z) * left + raw(axp, x, z) * right)
                + (raw(azm, x, z) * at(p, x + 1, z, -1) + raw(azp, x, z) * at(p, x + 1, z, 1))
                + (raw(aym, x, z) * y_minus(mid) + raw(ayp, x, z) * y_plus(mid) - raw(rr, x, z)),
            )
            left, mid = mid, right

    def into(ref):
        def store(x, z, v):
            ref[x + 1, :, pl.ds(ROW0 + z * 8, 8), :] = v

        return store

    def sweep1(xs, z):
        sweep(p0, into(p1), xs, z)

    def sweep2(xs, z):
        sweep(p1, into(p2), xs, z)

    def sweep3(xs, z):
        sweep(p2, lambda x, z, v: to_out(press_o, x, z, v), xs, z)

    tiles = CZ // 8
    middle = tuple(range(1, CX - 1))

    def interior(fn, first, count):
        def step(i, c):
            fn(middle, first + i)
            return c

        lax.fori_loop(0, count, step, 0)

    def edges(fn):
        def step(i, c):
            fn(middle, i * (tiles - 1))
            return c

        lax.fori_loop(0, 2, step, 0)

    def ends(fn):
        def step(i, c):
            for k in range(4):
                fn((0,), i * 4 + k)
                fn((CX - 1,), i * 4 + k)
            return c

        lax.fori_loop(0, tiles // 4, step, 0)

    inside = tiles - 2

    def recv(copies):
        for c in copies:
            c.wait_recv()

    interior(advect, 1, inside)
    recv(ez_al + ez_vz)
    fill_z([(0, al, 1, ROW0 - 1, 0), (1, al, 1, ROW0 + CZ, DEPTHS - 1), (2, vz, 0, CZ, DEPTHS - 1)])
    edges(advect)

    def a1_wait(k, c):
        src = (a_me + GA - k) % GA
        rcopy(s1.at[src], r1.at[src], a1s.at[k], a1r.at[k], a_peer(k)[1]).wait_recv()
        return c

    lax.fori_loop(1, GA, a1_wait, 0)
    got = dot(perm_s[...], r1[:, 0:REC_A, :].reshape(SLOTS, LANES)).astype(BF16)
    perm_s[...] = onehot(
        pc == (((pr >> 2) & (GB - 1)) * REC_B + (pr >> 6) * CAP + (pr & 3))
    )
    mrow = iota((META, LANES), 0)
    m1 = jnp.zeros((META, LANES), F32)
    for a in range(GA):
        m1 = jnp.where(mrow == a, r1[a, REC_A:, :].astype(F32), m1)
    m1 = m1.astype(BF16)
    for b in range(GB):
        s2[b, 0:REC_B, :] = got[b * REC_B : (b + 1) * REC_B]
        s2[b, REC_B:, :] = m1

    recv(e_al + e_vx)
    zero_x(al)

    @pl.when(slab == SLABS - 1)
    def _():
        vx[CX] = jnp.zeros((NB, CZ, LANES), F32)

    ends(advect)
    e_rho, ez_rho = xpair(5, rho), zpair(5)
    start(e_rho)
    pack_z([(5, rho, 1, ROW0 + CZ - 1), (6, rho, 1, ROW0)])
    start(ez_rho)

    def b1_start(k, c):
        b, dev = b_peer(k)
        rcopy(s2.at[b], r2.at[b_me], b1s.at[k], b1r.at[k], dev).start()
        return c

    lax.fori_loop(1, GB, b1_start, 0)
    r2[b_me] = s2[b_me]

    interior(coefficients, 1, inside)
    recv(ez_p0 + ez_rho)
    fill_z([
        (3, p0, 1, ROW0 - 1, 0), (4, p0, 1, ROW0 + CZ, DEPTHS - 1),
        (5, rho, 1, ROW0 - 1, 0), (6, rho, 1, ROW0 + CZ, DEPTHS - 1),
    ])
    edges(coefficients)
    recv(e_p0 + e_rho)
    zero_x(p0)
    zero_x(rho)
    ends(coefficients)
    for c in loads["div"]:
        c.wait()

    def b1_wait(k, c):
        src = (b_me + GB - k) % GB
        rcopy(s2.at[src], r2.at[src], b1s.at[k], b1r.at[k], b_peer(k)[1]).wait_recv()
        return c

    lax.fori_loop(1, GB, b1_wait, 0)

    m2 = r2[:, REC_B:, :].reshape(GB * META, LANES)
    srow, scol = iota((SLOTS, GB * META), 0), iota((SLOTS, GB * META), 1)
    wide = dot(onehot(scol == (srow >> 5) * META + ((srow >> 2) & (GA - 1))), m2)
    pick = iota((SLOTS, LANES), 1) - (iota((SLOTS, LANES), 0) & 3) - b_me * CAP
    hi_c = jnp.sum(jnp.where(pick == 0, wide, 0.0), axis=1, keepdims=True)
    lo_c = jnp.sum(jnp.where(pick == REC_A, wide, 0.0), axis=1, keepdims=True)
    seg_c = hi_c.astype(I32) * 64 + lo_c.astype(I32)
    block_c, key_c = seg_c & 3, seg_c >> 2
    key_f = jnp.broadcast_to(key_c, (SLOTS, LANES)).astype(F32)
    key_r = key_f.T[0:1]
    recs = r2[:, 0:REC_B, :].reshape(SLOTS, LANES)
    for y in range(NB):
        rmat[:, y * LANES : (y + 1) * LANES] = jnp.where(
            block_c == y, recs.astype(F32), 0.0
        ).astype(BF16)

    def hull(i, c):
        cells = (iota((4 * CZ, SLOTS), 0) + i * (4 * CZ)).astype(F32)
        h = dot(onehot(cells == key_r), rmat[...])
        for k in range(4):
            x = i * 4 + k
            for y in range(NB):
                part = h[k * CZ : (k + 1) * CZ, y * LANES : (y + 1) * LANES]
                rr[x, y] = (div[x, y] + part) * rr[x, y]
        return c

    lax.fori_loop(0, CX // 4, hull, 0)

    ends(sweep1)
    e_p1, ez_p1 = xpair(7, p1), zpair(7)
    start(e_p1)
    edges(sweep1)
    pack_z([(7, p1, 1, ROW0 + CZ - 1), (8, p1, 1, ROW0)])
    start(ez_p1)
    interior(sweep1, 1, inside)
    for c in range(CX * CZ // LANES):
        g_s[:, c * LANES : (c + 1) * LANES] = onehot(
            key_f == (iota((SLOTS, LANES), 1) + c * LANES).astype(F32)
        )
    interior(sweep2, 1, inside // 2)
    recv(ez_p1)
    fill_z([(7, p1, 1, ROW0 - 1, 0), (8, p1, 1, ROW0 + CZ, DEPTHS - 1)])
    recv(e_p1)
    zero_x(p1)
    ends(sweep2)
    e_p2, ez_p2 = xpair(9, p2), zpair(9)
    start(e_p2)
    edges(sweep2)
    pack_z([(9, p2, 1, ROW0 + CZ - 1), (10, p2, 1, ROW0)])
    start(ez_p2)
    interior(sweep2, 1 + inside // 2, inside - inside // 2)
    interior(sweep3, 1, inside)
    recv(ez_p2)
    fill_z([(9, p2, 1, ROW0 - 1, 0), (10, p2, 1, ROW0 + CZ, DEPTHS - 1)])
    edges(sweep3)
    recv(e_p2)
    zero_x(p2)
    ends(sweep3)

    for x in range(CX):
        pb[x * CZ : (x + 1) * CZ, :] = press_o[x].astype(BF16)
    wet = dot(g_s[...], pb[...])
    back = jnp.zeros((SLOTS, LANES), F32)
    for y in range(NB):
        back = jnp.where(block_c == y, wet[:, y * LANES : (y + 1) * LANES], back)
    back = back.astype(BF16)
    for b in range(GB):
        s3[b] = back[b * REC_B : (b + 1) * REC_B]

    def b2_start(k, c):
        b, dev = b_peer(k)
        rcopy(s3.at[b], t1.at[b_me], b2s.at[k], b2r.at[k], dev).start()
        return c

    def b2_wait(k, c):
        src = (b_me + GB - k) % GB
        rcopy(s3.at[src], t1.at[src], b2s.at[k], b2r.at[k], b_peer(k)[1]).wait_recv()
        return c

    lax.fori_loop(1, GB, b2_start, 0)
    t1[b_me] = s3[b_me]
    lax.fori_loop(1, GB, b2_wait, 0)
    turned = dot(perm_s[...], t1[...].reshape(SLOTS, LANES)).astype(BF16)
    for a in range(GA):
        s4[a] = turned[a * REC_A : (a + 1) * REC_A]

    def a2_start(k, c):
        a, dev = a_peer(k)
        rcopy(s4.at[a], t2.at[a_me], a2s.at[k], a2r.at[k], dev).start()
        return c

    def a2_wait(k, c):
        src = (a_me + GA - k) % GA
        rcopy(s4.at[src], t2.at[src], a2s.at[k], a2r.at[k], a_peer(k)[1]).wait_recv()
        return c

    lax.fori_loop(1, GA, a2_start, 0)
    t2[a_me] = s4[a_me]
    lax.fori_loop(1, GA, a2_wait, 0)
    panel_o[...] = dot(q_s[...], t2[...].reshape(SLOTS, LANES)).astype(BF16)

    for c in sends:
        c.wait_send()

    def b_done(k, c):
        b, dev = b_peer(k)
        rcopy(s2.at[b], r2.at[b_me], b1s.at[k], b1r.at[k], dev).wait_send()
        rcopy(s3.at[b], t1.at[b_me], b2s.at[k], b2r.at[k], dev).wait_send()
        return c

    def a_done(k, c):
        a, dev = a_peer(k)
        rcopy(s1.at[a], r1.at[a_me], a1s.at[k], a1r.at[k], dev).wait_send()
        rcopy(s4.at[a], t2.at[a_me], a2s.at[k], a2r.at[k], dev).wait_send()
        return c

    lax.fori_loop(1, GB, b_done, 0)
    lax.fori_loop(1, GA, a_done, 0)


def body(alpha, vel_x, vel_z, divergence, press_guess, panel_records, panel_dest, panel_segment):
    padded = pltpu.VMEM((CX + 2, NB, PADZ, LANES), F32)
    plain = pltpu.VMEM((CX, NB, CZ, LANES), F32)
    hbm = pl.BlockSpec(memory_space=pl.ANY)
    vmem = pl.BlockSpec(memory_space=pltpu.VMEM)
    dma = lambda n: pltpu.SemaphoreType.DMA((n,))
    field = pltpu.VMEM((CX, CZ, BEAM), F32)
    return pl.pallas_call(
        kernel,
        out_shape=(field, field, pltpu.VMEM((PAN, LANES), BF16)),
        in_specs=[hbm] * 5 + [vmem] * 3,
        out_specs=(vmem, vmem, vmem),
        scratch_shapes=[
            padded,
            pltpu.VMEM((CX + 1, NB, CZ, LANES), F32),
            pltpu.VMEM((CX, NB, CZ + 8, LANES), F32),
            plain,
            padded, padded, padded, padded,
            plain, plain, plain, plain, plain, plain, plain,
            pltpu.VMEM((11, CX, NB, LANES), F32),
            pltpu.VMEM((11, CX, NB, LANES), F32),
            pltpu.VMEM((GA, REC_A + META, LANES), BF16),
            pltpu.VMEM((GA, REC_A + META, LANES), BF16),
            pltpu.VMEM((GB, REC_B + META, LANES), BF16),
            pltpu.VMEM((GB, REC_B + META, LANES), BF16),
            pltpu.VMEM((GB, REC_B, LANES), BF16),
            pltpu.VMEM((GB, REC_B, LANES), BF16),
            pltpu.VMEM((GA, REC_A, LANES), BF16),
            pltpu.VMEM((GA, REC_A, LANES), BF16),
            pltpu.VMEM((PAN, SLOTS), BF16),
            pltpu.VMEM((SLOTS, CX * CZ), BF16),
            pltpu.VMEM((SLOTS, SLOTS), BF16),
            pltpu.VMEM((SLOTS, BEAM), BF16),
            pltpu.VMEM((CX * CZ, BEAM), BF16),
            dma(20), dma(11), dma(11), dma(11), dma(11),
            dma(GB), dma(GB), dma(GA), dma(GA), dma(GA), dma(GA), dma(GB), dma(GB),
        ],
        compiler_params=pltpu.CompilerParams(
            collective_id=0, has_side_effects=True, vmem_limit_bytes=59 * 1024 * 1024 + 768 * 1024
        ),
    )(
        alpha, vel_x, vel_z, divergence, press_guess, panel_records,
        panel_dest.reshape(1, PAN), panel_segment.reshape(1, PAN),
    )


def solution(mesh):
    field = P("slab", "depth", None)
    rows = P(("slab", "depth"), None)
    return jax.shard_map(
        body, mesh=mesh, in_specs=(field,) * 5 + (rows,) * 3,
        out_specs=(field, field, rows), check_vma=False,
    )
```

```python
import jax
import jax.numpy as jnp
from jax import lax
from jax.experimental import pallas as pl
from jax.experimental.pallas import tpu as pltpu
from jax.sharding import PartitionSpec as P

MESH = pl.DeviceIdType.MESH
F32, BF16, I32 = jnp.float32, jnp.bfloat16, jnp.int32
CX, CZ, BEAM, LANES = 16, 64, 512, 128
NB = BEAM // LANES
ROW0 = 8
PADZ = CZ + 16
SLABS, DEPTHS = 32, 4
GA, GB = 8, 16
CAP = 4
SLOTS = GA * GB * CAP
PAN = 256
REC_B, REC_A = GA * CAP, GB * CAP
META = 16


def iota(shape, dim):
    return lax.broadcasted_iota(I32, shape, dim)


def onehot(cond):
    return jnp.where(cond, 1.0, 0.0).astype(BF16)


def dot(a, b):
    return jnp.dot(a, b, preferred_element_type=F32)


def recip(d):
    r = pl.reciprocal(d, approx=True)
    return r * (2.0 - d * r)


def kernel(
    alpha_h, velx_h, velz_h, div_h, press_h, rec_h, dest_h, seg_h,
    press_o, alpha_o, panel_o,
    rec_ref, dest_ref, seg_ref, al, vx, vz, div, rho, p0, p1, p2,
    axm, axp, azm, azp, aym, ayp, rr,
    zs, zr, xb, xr, acc,
    s1, r1, s2, r2, s3, t1, s4, t2,
    q_s, g_s, perm_s, rmat, pb,
    load_sem, xs_sem, xr_sem, zs_sem, zr_sem,
    b1s, b1r, a1s, a1r, a2s, a2r, b2s, b2r,
):
    slab = lax.axis_index("slab")
    depth = lax.axis_index("depth")
    up_s, dn_s = (slab + 1) % SLABS, (slab + SLABS - 1) % SLABS
    up_d, dn_d = (depth + 1) % DEPTHS, (depth + DEPTHS - 1) % DEPTHS
    x_up, x_dn = (up_s, depth), (dn_s, depth)
    z_up, z_dn = (slab, up_d), (slab, dn_d)
    b_me, core = slab // 2, slab % 2
    a_me = core * DEPTHS + depth

    def b_peer(k):
        b = (b_me + k) % GB
        return b, (b * 2 + core, depth)

    def a_peer(k):
        a = (a_me + k) % GA
        return a, (b_me * 2 + a // DEPTHS, a % DEPTHS)

    loads = {}
    sem_i = 0

    def load(name, pairs):
        nonlocal sem_i
        loads[name] = []
        for src, dst in pairs:
            c = pltpu.make_async_copy(src, dst, load_sem.at[sem_i])
            c.start()
            sem_i += 1
            loads[name].append(c)

    def loaded(name):
        for c in loads[name]:
            c.wait()

    def field(src, dst):
        return [(src.at[:, :, pl.ds(y * LANES, LANES)], dst(y)) for y in range(NB)]

    load("panels", [(dest_h, dest_ref), (seg_h, seg_ref), (rec_h, rec_ref)])
    load("al", field(alpha_h, lambda y: al.at[pl.ds(1, CX), y, pl.ds(ROW0, CZ), :]))
    load("vx", field(velx_h, lambda y: vx.at[pl.ds(0, CX), y, :, :]))
    load("vz", field(velz_h, lambda y: vz.at[:, y, pl.ds(0, CZ), :]))
    load("p0", field(press_h, lambda y: p0.at[pl.ds(1, CX), y, pl.ds(ROW0, CZ), :]))
    load("div", field(div_h, lambda y: div.at[:, y, :, :]))

    barrier = pltpu.get_barrier_semaphore()
    for dev in (x_up, x_dn, z_up, z_dn):
        pl.semaphore_signal(barrier, inc=1, device_id=dev, device_id_type=MESH)

    def sig_b(k, c):
        pl.semaphore_signal(barrier, inc=1, device_id=b_peer(k)[1], device_id_type=MESH)
        return c

    def sig_a(k, c):
        pl.semaphore_signal(barrier, inc=1, device_id=a_peer(k)[1], device_id_type=MESH)
        return c

    lax.fori_loop(1, GB, sig_b, 0)
    lax.fori_loop(1, GA, sig_a, 0)

    loaded("panels")
    dest, seg = dest_ref[...], seg_ref[...]
    own = onehot(iota((GA * GB, PAN), 0) == dest)
    before = dot(own, onehot(iota((PAN, PAN), 0) < iota((PAN, PAN), 1)))
    slot = jnp.sum(own.astype(F32) * before, axis=0, keepdims=True)
    lane_of = (dest >> 3) * CAP + slot.astype(I32)
    place = (dest & (GA - 1)) * REC_A + lane_of
    packed = dot(onehot(iota((SLOTS, PAN), 0) == place), rec_ref[...]).astype(BF16)
    row = iota((LANES, PAN), 0)
    hi, lo = (seg >> 6).astype(F32), (seg & 63).astype(F32)
    bt = jnp.where(row == lane_of, hi, 0.0) + jnp.where(row == lane_of + REC_A, lo, 0.0)
    meta = lax.dot_general(
        onehot(iota((16, PAN), 0) == (dest & (GA - 1))), bt.astype(BF16),
        (((1,), (1,)), ((), ())), preferred_element_type=F32,
    )
    for a in range(GA):
        s1[a, 0:REC_A, :] = packed[a * REC_A : (a + 1) * REC_A]
        s1[a, REC_A:, :] = jnp.broadcast_to(meta[a : a + 1], (META, LANES)).astype(BF16)

    def rcopy(src, dst, ss, rs, dev):
        return pltpu.make_async_remote_copy(
            src_ref=src, dst_ref=dst, send_sem=ss, recv_sem=rs,
            device_id=dev, device_id_type=MESH,
        )

    def xcopy(i, dev):
        return rcopy(xb.at[i], xr.at[i], xs_sem.at[i], xr_sem.at[i], dev)

    def zcopy(i, dev):
        return rcopy(zs.at[i], zr.at[i], zs_sem.at[i], zr_sem.at[i], dev)

    def xpair(i):
        return [xcopy(i, x_up), xcopy(i + 1, x_dn)]

    def pack_x(i, ref):
        xb[i] = ref[CX, :, ROW0 : ROW0 + CZ, :].astype(BF16)
        xb[i + 1] = ref[1, :, ROW0 : ROW0 + CZ, :].astype(BF16)

    def fill_x(i, ref):
        low, high = xr[i].astype(F32), xr[i + 1].astype(F32)
        ref[0, :, ROW0 : ROW0 + CZ, :] = jnp.where(slab == 0, 0.0, low)
        ref[CX + 1, :, ROW0 : ROW0 + CZ, :] = jnp.where(slab == SLABS - 1, 0.0, high)

    def zpair(i):
        return [zcopy(i, z_up), zcopy(i + 1, z_dn)]

    def pack_z(items):
        def step(g, c):
            for k in range(4):
                x = g * 4 + k
                for i, ref, xo, r in items:
                    zs[i, x] = ref[x + xo, :, r, :]
            return c

        lax.fori_loop(0, CX // 4, step, 0)

    def fill_z(items):
        def step(g, c):
            for k in range(4):
                x = g * 4 + k
                for i, ref, xo, r, edge in items:
                    ref[x + xo, :, r, :] = jnp.where(depth == edge, 0.0, zr[i, x])
            return c

        lax.fori_loop(0, CX // 4, step, 0)

    sends = []

    def start(copies):
        for c in copies:
            c.start()
        sends.extend(copies)

    loaded("al")
    pack_x(0, al)
    pack_z([(0, al, 1, ROW0 + CZ - 1), (1, al, 1, ROW0)])
    pl.semaphore_wait(barrier, 4 + (GB - 1) + (GA - 1))
    e_al, ez_al = xpair(0), zpair(0)
    start(e_al + ez_al)
    loaded("vx")
    loaded("vz")
    xb[2] = vx[0].astype(BF16)
    pack_z([(2, vz, 0, 0)])
    e_vx, ez_vz = [xcopy(2, x_dn)], [zcopy(2, z_dn)]
    start(e_vx + ez_vz)

    def a1_start(k, c):
        a, dev = a_peer(k)
        rcopy(s1.at[a], r1.at[a_me], a1s.at[k], a1r.at[k], dev).start()
        return c

    lax.fori_loop(1, GA, a1_start, 0)
    r1[a_me] = s1[a_me]
    loaded("p0")
    pack_x(3, p0)
    pack_z([(3, p0, 1, ROW0 + CZ - 1), (4, p0, 1, ROW0)])
    e_p0, ez_p0 = xpair(3), zpair(3)
    start(e_p0 + ez_p0)

    place_t = jnp.broadcast_to(place.astype(F32), (LANES, PAN)).T
    for c in range(SLOTS // LANES):
        q_s[:, c * LANES : (c + 1) * LANES] = onehot(
            place_t == (iota((PAN, LANES), 1) + c * LANES).astype(F32)
        )
    pr, pc = iota((SLOTS, SLOTS), 0), iota((SLOTS, SLOTS), 1)
    perm_s[...] = onehot(
        pc == (((pr >> 2) & (GA - 1)) * REC_A + (pr >> 5) * CAP + (pr & 3))
    )

    lane = iota((NB, 8, LANES), 2)
    last = (lane == LANES - 1) & (iota((NB, 8, LANES), 0) == NB - 1)
    zero1 = jnp.zeros((1, 8, LANES), F32)

    def y_minus(v):
        r = pltpu.roll(v, 1, 2)
        return jnp.where(lane == 0, jnp.concatenate([zero1, r[: NB - 1]], axis=0), r)

    def y_plus(v):
        r = pltpu.roll(v, LANES - 1, 2)
        return jnp.where(lane == LANES - 1, jnp.concatenate([r[1:], zero1], axis=0), r)

    def at(ref, x, z, shift=0):
        return ref[x, :, pl.ds(ROW0 + z * 8 + shift, 8), :]

    def raw(ref, x, z, shift=0):
        return ref[x, :, pl.ds(z * 8 + shift, 8), :]

    def to_out(ref, x, z, v):
        for y in range(NB):
            ref[x, pl.ds(z * 8, 8), y * LANES : (y + 1) * LANES] = v[y]

    def advect(xs, z):
        a, right, fx1, u1 = at(al, xs[0] + 1, z), None, None, None
        left, u0 = at(al, xs[0], z), raw(vx, xs[0], z)
        fx0 = u0 * jnp.where(u0 > 0, left, a)
        for x in xs:
            right, u1 = at(al, x + 2, z), raw(vx, x + 1, z)
            w0, w1 = raw(vz, x, z), raw(vz, x, z, 1)
            fx1 = u1 * jnp.where(u1 > 0, a, right)
            fz0 = w0 * jnp.where(w0 > 0, at(al, x + 1, z, -1), a)
            fz1 = w1 * jnp.where(w1 > 0, a, at(al, x + 1, z, 1))
            new = a - 0.2 * (fx1 - fx0 + fz1 - fz0)
            to_out(alpha_o, x, z, new)
            rho[x + 1, :, pl.ds(ROW0 + z * 8, 8), :] = 1.0 + 9.0 * new
            a, fx0 = right, fx1

    def coefficients(xs, z):
        d = at(rho, xs[0] + 1, z)
        cm = recip(d + at(rho, xs[0], z))
        for x in xs:
            right = at(rho, x + 2, z)
            cp = recip(d + right)
            zm, zp = recip(d + at(rho, x + 1, z, -1)), recip(d + at(rho, x + 1, z, 1))
            ym = recip(d + y_minus(d))
            yp = y_plus(ym)
            yp = jnp.where(last, recip(d), yp)
            inv = recip((cm + cp) + (zm + zp) + (ym + yp))
            for ref, v in zip((axm, axp, azm, azp, aym, ayp), (cm, cp, zm, zp, ym, yp)):
                ref[x, :, pl.ds(z * 8, 8), :] = v * inv
            rr[x, :, pl.ds(z * 8, 8), :] = 0.5 * inv
            d, cm = right, cp

    def sweep(p, store, source, xs, z):
        left, mid = at(p, xs[0], z), at(p, xs[0] + 1, z)
        for x in xs:
            right = at(p, x + 2, z)
            store(
                x, z,
                (raw(axm, x, z) * left + raw(axp, x, z) * right)
                + (raw(azm, x, z) * at(p, x + 1, z, -1) + raw(azp, x, z) * at(p, x + 1, z, 1))
                + (raw(aym, x, z) * y_minus(mid) + raw(ayp, x, z) * y_plus(mid) - source(x, z)),
            )
            left, mid = mid, right

    def scaled(x, z):
        r = raw(rr, x, z) * raw(div, x, z)
        rr[x, :, pl.ds(z * 8, 8), :] = r
        return r

    def kept(x, z):
        return raw(rr, x, z)

    def into(ref):
        def store(x, z, v):
            ref[x + 1, :, pl.ds(ROW0 + z * 8, 8), :] = v

        return store

    def sweep1(xs, z):
        sweep(p0, into(p1), scaled, xs, z)

    def sweep2(xs, z):
        sweep(p1, into(p2), kept, xs, z)

    def sweep3(xs, z):
        sweep(p2, lambda x, z, v: to_out(press_o, x, z, v), kept, xs, z)

    tiles = CZ // 8
    middle = tuple(range(1, CX - 1))

    def interior(fn, first, count):
        def step(i, c):
            fn(middle, first + i)
            return c

        lax.fori_loop(0, count, step, 0)

    def edges(fn):
        def step(i, c):
            fn(middle, i * (tiles - 1))
            return c

        lax.fori_loop(0, 2, step, 0)

    def ends(fn):
        def step(i, c):
            for k in range(4):
                fn((0,), i * 4 + k)
                fn((CX - 1,), i * 4 + k)
            return c

        lax.fori_loop(0, tiles // 4, step, 0)

    inside = tiles - 2

    def recv(copies):
        for c in copies:
            c.wait_recv()

    interior(advect, 1, inside)
    recv(ez_al + ez_vz)
    fill_z([(0, al, 1, ROW0 - 1, 0), (1, al, 1, ROW0 + CZ, DEPTHS - 1), (2, vz, 0, CZ, DEPTHS - 1)])
    edges(advect)

    def a1_wait(k, c):
        src = (a_me + GA - k) % GA
        rcopy(s1.at[src], r1.at[src], a1s.at[k], a1r.at[k], a_peer(k)[1]).wait_recv()
        return c

    lax.fori_loop(1, GA, a1_wait, 0)
    got = dot(perm_s[...], r1[:, 0:REC_A, :].reshape(SLOTS, LANES)).astype(BF16)
    perm_s[...] = onehot(
        pc == (((pr >> 2) & (GB - 1)) * REC_B + (pr >> 6) * CAP + (pr & 3))
    )
    mrow = iota((META, LANES), 0)
    m1 = jnp.zeros((META, LANES), F32)
    for a in range(GA):
        m1 = jnp.where(mrow == a, r1[a, REC_A:, :].astype(F32), m1)
    m1 = m1.astype(BF16)
    for b in range(GB):
        s2[b, 0:REC_B, :] = got[b * REC_B : (b + 1) * REC_B]
        s2[b, REC_B:, :] = m1

    def b1_start(k, c):
        b, dev = b_peer(k)
        rcopy(s2.at[b], r2.at[b_me], b1s.at[k], b1r.at[k], dev).start()
        return c

    lax.fori_loop(1, GB, b1_start, 0)
    r2[b_me] = s2[b_me]

    recv(e_al + e_vx)
    fill_x(0, al)
    vx[CX] = jnp.where(slab == SLABS - 1, 0.0, xr[2].astype(F32))
    ends(advect)
    pack_x(5, rho)
    e_rho, ez_rho = xpair(5), zpair(5)
    start(e_rho)
    pack_z([(5, rho, 1, ROW0 + CZ - 1), (6, rho, 1, ROW0)])
    start(ez_rho)

    interior(coefficients, 1, inside)
    loaded("div")

    def b1_wait(k, c):
        src = (b_me + GB - k) % GB
        rcopy(s2.at[src], r2.at[src], b1s.at[k], b1r.at[k], b_peer(k)[1]).wait_recv()
        return c

    lax.fori_loop(1, GB, b1_wait, 0)

    m2 = r2[:, REC_B:, :].reshape(GB * META, LANES)
    srow, scol = iota((SLOTS, GB * META), 0), iota((SLOTS, GB * META), 1)
    wide = dot(onehot(scol == (srow >> 5) * META + ((srow >> 2) & (GA - 1))), m2)
    pick = iota((SLOTS, LANES), 1) - (iota((SLOTS, LANES), 0) & 3) - b_me * CAP
    hi_c = jnp.sum(jnp.where(pick == 0, wide, 0.0), axis=1, keepdims=True)
    lo_c = jnp.sum(jnp.where(pick == REC_A, wide, 0.0), axis=1, keepdims=True)
    seg_c = hi_c.astype(I32) * 64 + lo_c.astype(I32)
    block_c, key_c = seg_c & 3, seg_c >> 2
    key_f = jnp.broadcast_to(key_c, (SLOTS, LANES)).astype(F32)
    key_r = key_f.T[0:1]
    recs = r2[:, 0:REC_B, :].reshape(SLOTS, LANES)
    for y in range(NB):
        rmat[:, y * LANES : (y + 1) * LANES] = jnp.where(
            block_c == y, recs.astype(F32), 0.0
        ).astype(BF16)

    def hull(i, c):
        cells = (iota((4 * CZ, SLOTS), 0) + i * (4 * CZ)).astype(F32)
        h = dot(onehot(cells == key_r), rmat[...])
        for k in range(4):
            x = i * 4 + k
            for y in range(NB):
                part = h[k * CZ : (k + 1) * CZ, y * LANES : (y + 1) * LANES]
                div[x, y] += part
        return c

    lax.fori_loop(0, CX // 4, hull, 0)

    recv(ez_p0 + ez_rho)
    fill_z([
        (3, p0, 1, ROW0 - 1, 0), (4, p0, 1, ROW0 + CZ, DEPTHS - 1),
        (5, rho, 1, ROW0 - 1, 0), (6, rho, 1, ROW0 + CZ, DEPTHS - 1),
    ])
    edges(coefficients)
    recv(e_p0 + e_rho)
    fill_x(3, p0)
    fill_x(5, rho)
    ends(coefficients)
    ends(sweep1)
    pack_x(7, p1)
    e_p1, ez_p1 = xpair(7), zpair(7)
    start(e_p1)
    edges(sweep1)
    pack_z([(7, p1, 1, ROW0 + CZ - 1), (8, p1, 1, ROW0)])
    start(ez_p1)
    interior(sweep1, 1, inside)
    for c in range(CX * CZ // LANES):
        g_s[:, c * LANES : (c + 1) * LANES] = onehot(
            key_f == (iota((SLOTS, LANES), 1) + c * LANES).astype(F32)
        )
    interior(sweep2, 1, inside // 2)
    recv(ez_p1)
    fill_z([(7, p1, 1, ROW0 - 1, 0), (8, p1, 1, ROW0 + CZ, DEPTHS - 1)])
    recv(e_p1)
    fill_x(7, p1)
    ends(sweep2)
    pack_x(9, p2)
    e_p2, ez_p2 = xpair(9), zpair(9)
    start(e_p2)
    edges(sweep2)
    pack_z([(9, p2, 1, ROW0 + CZ - 1), (10, p2, 1, ROW0)])
    start(ez_p2)
    interior(sweep2, 1 + inside // 2, inside - inside // 2)
    interior(sweep3, 1, inside)
    recv(ez_p2)
    fill_z([(9, p2, 1, ROW0 - 1, 0), (10, p2, 1, ROW0 + CZ, DEPTHS - 1)])
    edges(sweep3)
    for x in range(2, CX - 2):
        pb[x * CZ : (x + 1) * CZ, :] = press_o[x].astype(BF16)
    acc[...] = dot(g_s[:, 2 * CZ : (CX - 2) * CZ], pb[2 * CZ : (CX - 2) * CZ, :])
    recv(e_p2)
    fill_x(9, p2)
    ends(sweep3)

    for x in (0, 1, CX - 2, CX - 1):
        pb[x * CZ : (x + 1) * CZ, :] = press_o[x].astype(BF16)
    wet = acc[...] + (
        dot(g_s[:, 0 : 2 * CZ], pb[0 : 2 * CZ, :])
        + dot(g_s[:, (CX - 2) * CZ :], pb[(CX - 2) * CZ :, :])
    )
    back = jnp.zeros((SLOTS, LANES), F32)
    for y in range(NB):
        back = jnp.where(block_c == y, wet[:, y * LANES : (y + 1) * LANES], back)
    back = back.astype(BF16)
    for b in range(GB):
        s3[b] = back[b * REC_B : (b + 1) * REC_B]

    def b2_start(k, c):
        b, dev = b_peer(k)
        rcopy(s3.at[b], t1.at[b_me], b2s.at[k], b2r.at[k], dev).start()
        return c

    def b2_wait(k, c):
        src = (b_me + GB - k) % GB
        rcopy(s3.at[src], t1.at[src], b2s.at[k], b2r.at[k], b_peer(k)[1]).wait_recv()
        return c

    lax.fori_loop(1, GB, b2_start, 0)
    t1[b_me] = s3[b_me]
    lax.fori_loop(1, GB, b2_wait, 0)
    turned = dot(perm_s[...], t1[...].reshape(SLOTS, LANES)).astype(BF16)
    for a in range(GA):
        s4[a] = turned[a * REC_A : (a + 1) * REC_A]

    def a2_start(k, c):
        a, dev = a_peer(k)
        rcopy(s4.at[a], t2.at[a_me], a2s.at[k], a2r.at[k], dev).start()
        return c

    def a2_wait(k, c):
        src = (a_me + GA - k) % GA
        rcopy(s4.at[src], t2.at[src], a2s.at[k], a2r.at[k], a_peer(k)[1]).wait_recv()
        return c

    lax.fori_loop(1, GA, a2_start, 0)
    t2[a_me] = s4[a_me]
    lax.fori_loop(1, GA, a2_wait, 0)
    panel_o[...] = dot(q_s[...], t2[...].reshape(SLOTS, LANES)).astype(BF16)

    for c in sends:
        c.wait_send()

    def b_done(k, c):
        b, dev = b_peer(k)
        rcopy(s2.at[b], r2.at[b_me], b1s.at[k], b1r.at[k], dev).wait_send()
        rcopy(s3.at[b], t1.at[b_me], b2s.at[k], b2r.at[k], dev).wait_send()
        return c

    def a_done(k, c):
        a, dev = a_peer(k)
        rcopy(s1.at[a], r1.at[a_me], a1s.at[k], a1r.at[k], dev).wait_send()
        rcopy(s4.at[a], t2.at[a_me], a2s.at[k], a2r.at[k], dev).wait_send()
        return c

    lax.fori_loop(1, GB, b_done, 0)
    lax.fori_loop(1, GA, a_done, 0)


def deliver(press, alpha, panel, press_o, alpha_o, panel_o, sem):
    pairs = ((press, press_o), (alpha, alpha_o), (panel, panel_o))
    copies = [pltpu.make_async_copy(s, d, sem.at[i]) for i, (s, d) in enumerate(pairs)]
    for c in copies:
        c.start()
    for c in copies:
        c.wait()


def body(alpha, vel_x, vel_z, divergence, press_guess, panel_records, panel_dest, panel_segment):
    padded = pltpu.VMEM((CX + 2, NB, PADZ, LANES), F32)
    plain = pltpu.VMEM((CX, NB, CZ, LANES), F32)
    hbm = pl.BlockSpec(memory_space=pltpu.HBM)
    vmem = pl.BlockSpec(memory_space=pltpu.VMEM)
    dma = lambda n: pltpu.SemaphoreType.DMA((n,))
    field = pltpu.VMEM((CX, CZ, BEAM), F32)
    outs = pl.pallas_call(
        kernel,
        out_shape=(field, field, pltpu.VMEM((PAN, LANES), BF16)),
        in_specs=[hbm] * 8,
        out_specs=(vmem, vmem, vmem),
        scratch_shapes=[
            pltpu.VMEM((PAN, LANES), BF16), pltpu.VMEM((1, PAN), I32), pltpu.VMEM((1, PAN), I32),
            padded,
            pltpu.VMEM((CX + 1, NB, CZ, LANES), F32),
            pltpu.VMEM((CX, NB, CZ + 8, LANES), F32),
            plain,
            padded, padded, padded, padded,
            plain, plain, plain, plain, plain, plain, plain,
            pltpu.VMEM((11, CX, NB, LANES), F32),
            pltpu.VMEM((11, CX, NB, LANES), F32),
            pltpu.VMEM((11, NB, CZ, LANES), BF16),
            pltpu.VMEM((11, NB, CZ, LANES), BF16),
            pltpu.VMEM((SLOTS, BEAM), F32),
            pltpu.VMEM((GA, REC_A + META, LANES), BF16),
            pltpu.VMEM((GA, REC_A + META, LANES), BF16),
            pltpu.VMEM((GB, REC_B + META, LANES), BF16),
            pltpu.VMEM((GB, REC_B + META, LANES), BF16),
            pltpu.VMEM((GB, REC_B, LANES), BF16),
            pltpu.VMEM((GB, REC_B, LANES), BF16),
            pltpu.VMEM((GA, REC_A, LANES), BF16),
            pltpu.VMEM((GA, REC_A, LANES), BF16),
            pltpu.VMEM((PAN, SLOTS), BF16),
            pltpu.VMEM((SLOTS, CX * CZ), BF16),
            pltpu.VMEM((SLOTS, SLOTS), BF16),
            pltpu.VMEM((SLOTS, BEAM), BF16),
            pltpu.VMEM((CX * CZ, BEAM), BF16),
            dma(23), dma(11), dma(11), dma(11), dma(11),
            dma(GB), dma(GB), dma(GA), dma(GA), dma(GA), dma(GA), dma(GB), dma(GB),
        ],
        compiler_params=pltpu.CompilerParams(
            collective_id=0, has_side_effects=True, vmem_limit_bytes=50 * 1024 * 1024
        ),
    )(
        alpha, vel_x, vel_z, divergence, press_guess, panel_records,
        panel_dest.reshape(1, PAN), panel_segment.reshape(1, PAN),
    )
    outs = [pltpu.with_memory_space_constraint(o, pltpu.VMEM) for o in outs]
    return pl.pallas_call(
        deliver,
        out_shape=tuple(jax.ShapeDtypeStruct(o.shape, o.dtype) for o in outs),
        in_specs=[pl.BlockSpec(memory_space=pl.ANY)] * 3,
        out_specs=(hbm,) * 3,
        scratch_shapes=[dma(3)],
        compiler_params=pltpu.CompilerParams(vmem_limit_bytes=1024 * 1024),
    )(*outs)


def solution(mesh):
    field = P("slab", "depth", None)
    rows = P(("slab", "depth"), None)
    return jax.shard_map(
        body, mesh=mesh, in_specs=(field,) * 5 + (rows,) * 3,
        out_specs=(field, field, rows), check_vma=False,
    )
```

```python
import jax
import jax.numpy as jnp
from jax import lax
from jax.experimental import pallas as pl
from jax.experimental.pallas import tpu as pltpu
from jax.sharding import PartitionSpec as P

MESH = pl.DeviceIdType.MESH
F32, BF16, I32 = jnp.float32, jnp.bfloat16, jnp.int32
CX, CZ, BEAM, LANES = 16, 64, 512, 128
NB = BEAM // LANES
ROW0 = 8
PADZ = CZ + 16
SLABS, DEPTHS = 32, 4
GA, GB = 8, 16
CAP = 4
SLOTS = GA * GB * CAP
PAN = 256
REC_B, REC_A = GA * CAP, GB * CAP
META = 16


def iota(shape, dim):
    return lax.broadcasted_iota(I32, shape, dim)


def onehot(cond):
    return jnp.where(cond, 1.0, 0.0).astype(BF16)


def dot(a, b):
    return jnp.dot(a, b, preferred_element_type=F32)


def recip(d):
    r = pl.reciprocal(d, approx=True)
    return r * (2.0 - d * r)


def kernel(
    alpha_h, velx_h, velz_h, div_h, press_h, rec_h, dest_h, seg_h,
    press_o, alpha_o, panel_o,
    rec_ref, dest_ref, seg_ref, al, vx, vz, div, rho, p0, p1, p2,
    axm, axp, azm, azp, aym, ayp, rr,
    zs, zr, xb, xr, acc,
    s1, r1, s2, r2, wb, tb,
    q_s, g_s, perm_s, rmat, pb,
    load_sem, xs_sem, xr_sem, zs_sem, zr_sem,
    b1s, b1r, a1s, a1r, home_s, home_r,
):
    slab = lax.axis_index("slab")
    depth = lax.axis_index("depth")
    up_s, dn_s = (slab + 1) % SLABS, (slab + SLABS - 1) % SLABS
    up_d, dn_d = (depth + 1) % DEPTHS, (depth + DEPTHS - 1) % DEPTHS
    x_up, x_dn = (up_s, depth), (dn_s, depth)
    z_up, z_dn = (slab, up_d), (slab, dn_d)
    b_me, core = slab // 2, slab % 2
    a_me = core * DEPTHS + depth
    me = slab * DEPTHS + depth

    def b_peer(k):
        b = (b_me + k) % GB
        return b, (b * 2 + core, depth)

    def a_peer(k):
        a = (a_me + k) % GA
        return a, (b_me * 2 + a // DEPTHS, a % DEPTHS)

    loads = {}
    sem_i = 0

    def load(name, pairs):
        nonlocal sem_i
        loads[name] = []
        for src, dst in pairs:
            c = pltpu.make_async_copy(src, dst, load_sem.at[sem_i])
            c.start()
            sem_i += 1
            loads[name].append(c)

    def loaded(name):
        for c in loads[name]:
            c.wait()

    def field(src, dst):
        return [(src.at[:, :, pl.ds(y * LANES, LANES)], dst(y)) for y in range(NB)]

    load("panels", [(dest_h, dest_ref), (seg_h, seg_ref), (rec_h, rec_ref)])
    load("al", field(alpha_h, lambda y: al.at[pl.ds(1, CX), y, pl.ds(ROW0, CZ), :]))
    load("vx", field(velx_h, lambda y: vx.at[pl.ds(0, CX), y, :, :]))
    load("vz", field(velz_h, lambda y: vz.at[:, y, pl.ds(0, CZ), :]))
    load("p0", field(press_h, lambda y: p0.at[pl.ds(1, CX), y, pl.ds(ROW0, CZ), :]))
    load("div", field(div_h, lambda y: div.at[:, y, :, :]))

    barrier = pltpu.get_barrier_semaphore()
    for dev in (x_up, x_dn, z_up, z_dn):
        pl.semaphore_signal(barrier, inc=1, device_id=dev, device_id_type=MESH)

    def sig_b(k, c):
        pl.semaphore_signal(barrier, inc=1, device_id=b_peer(k)[1], device_id_type=MESH)
        return c

    def sig_a(k, c):
        pl.semaphore_signal(barrier, inc=1, device_id=a_peer(k)[1], device_id_type=MESH)
        return c

    lax.fori_loop(1, GB, sig_b, 0)
    lax.fori_loop(1, GA, sig_a, 0)

    loaded("panels")
    dest, seg = dest_ref[...], seg_ref[...]
    own = onehot(iota((GA * GB, PAN), 0) == dest)
    before = dot(own, onehot(iota((PAN, PAN), 0) < iota((PAN, PAN), 1)))
    slot = jnp.sum(own.astype(F32) * before, axis=0, keepdims=True)
    lane_of = (dest >> 3) * CAP + slot.astype(I32)
    place = (dest & (GA - 1)) * REC_A + lane_of
    packed = dot(onehot(iota((SLOTS, PAN), 0) == place), rec_ref[...]).astype(BF16)
    row = iota((LANES, PAN), 0)
    hi, lo = (seg >> 6).astype(F32), (seg & 63).astype(F32)
    bt = jnp.where(row == lane_of, hi, 0.0) + jnp.where(row == lane_of + REC_A, lo, 0.0)
    meta = lax.dot_general(
        onehot(iota((16, PAN), 0) == (dest & (GA - 1))), bt.astype(BF16),
        (((1,), (1,)), ((), ())), preferred_element_type=F32,
    )
    for a in range(GA):
        s1[a, 0:REC_A, :] = packed[a * REC_A : (a + 1) * REC_A]
        s1[a, REC_A:, :] = jnp.broadcast_to(meta[a : a + 1], (META, LANES)).astype(BF16)

    def rcopy(src, dst, ss, rs, dev):
        return pltpu.make_async_remote_copy(
            src_ref=src, dst_ref=dst, send_sem=ss, recv_sem=rs,
            device_id=dev, device_id_type=MESH,
        )

    def xcopy(i, dev):
        return rcopy(xb.at[i], xr.at[i], xs_sem.at[i], xr_sem.at[i], dev)

    def zcopy(i, dev):
        return rcopy(zs.at[i], zr.at[i], zs_sem.at[i], zr_sem.at[i], dev)

    def xpair(i):
        return [xcopy(i, x_up), xcopy(i + 1, x_dn)]

    def pack_x(i, ref):
        xb[i] = ref[CX, :, ROW0 : ROW0 + CZ, :].astype(BF16)
        xb[i + 1] = ref[1, :, ROW0 : ROW0 + CZ, :].astype(BF16)

    def fill_x(i, ref):
        low, high = xr[i].astype(F32), xr[i + 1].astype(F32)
        ref[0, :, ROW0 : ROW0 + CZ, :] = jnp.where(slab == 0, 0.0, low)
        ref[CX + 1, :, ROW0 : ROW0 + CZ, :] = jnp.where(slab == SLABS - 1, 0.0, high)

    def zpair(i):
        return [zcopy(i, z_up), zcopy(i + 1, z_dn)]

    def pack_z(items):
        def step(g, c):
            for k in range(4):
                x = g * 4 + k
                for i, ref, xo, r in items:
                    zs[i, x] = ref[x + xo, :, r, :]
            return c

        lax.fori_loop(0, CX // 4, step, 0)

    def fill_z(items):
        def step(g, c):
            for k in range(4):
                x = g * 4 + k
                for i, ref, xo, r, edge in items:
                    ref[x + xo, :, r, :] = jnp.where(depth == edge, 0.0, zr[i, x])
            return c

        lax.fori_loop(0, CX // 4, step, 0)

    sends = []

    def start(copies):
        for c in copies:
            c.start()
        sends.extend(copies)

    pl.semaphore_wait(barrier, 4 + (GB - 1) + (GA - 1))

    def a1_start(k, c):
        a, dev = a_peer(k)
        rcopy(s1.at[a], r1.at[a_me], a1s.at[k], a1r.at[k], dev).start()
        return c

    lax.fori_loop(1, GA, a1_start, 0)
    r1[a_me] = s1[a_me]

    loaded("al")
    pack_x(0, al)
    pack_z([(0, al, 1, ROW0 + CZ - 1), (1, al, 1, ROW0)])
    e_al, ez_al = xpair(0), zpair(0)
    start(e_al + ez_al)
    loaded("vx")
    loaded("vz")
    xb[2] = vx[0].astype(BF16)
    pack_z([(2, vz, 0, 0)])
    e_vx, ez_vz = [xcopy(2, x_dn)], [zcopy(2, z_dn)]
    start(e_vx + ez_vz)

    loaded("p0")
    pack_x(3, p0)
    pack_z([(3, p0, 1, ROW0 + CZ - 1), (4, p0, 1, ROW0)])
    e_p0, ez_p0 = xpair(3), zpair(3)
    start(e_p0 + ez_p0)

    answer = dest * CAP + slot.astype(I32)
    place_t = jnp.broadcast_to(answer.astype(F32), (LANES, PAN)).T
    for c in range(SLOTS // LANES):
        q_s[:, c * LANES : (c + 1) * LANES] = onehot(
            place_t == (iota((PAN, LANES), 1) + c * LANES).astype(F32)
        )
    pr, pc = iota((SLOTS, SLOTS), 0), iota((SLOTS, SLOTS), 1)
    perm_s[...] = onehot(
        pc == (((pr >> 2) & (GA - 1)) * REC_A + (pr >> 5) * CAP + (pr & 3))
    )

    lane = iota((NB, 8, LANES), 2)
    last = (lane == LANES - 1) & (iota((NB, 8, LANES), 0) == NB - 1)
    zero1 = jnp.zeros((1, 8, LANES), F32)

    def y_minus(v):
        r = pltpu.roll(v, 1, 2)
        return jnp.where(lane == 0, jnp.concatenate([zero1, r[: NB - 1]], axis=0), r)

    def y_plus(v):
        r = pltpu.roll(v, LANES - 1, 2)
        return jnp.where(lane == LANES - 1, jnp.concatenate([r[1:], zero1], axis=0), r)

    def at(ref, x, z, shift=0):
        return ref[x, :, pl.ds(ROW0 + z * 8 + shift, 8), :]

    def raw(ref, x, z, shift=0):
        return ref[x, :, pl.ds(z * 8 + shift, 8), :]

    def to_out(ref, x, z, v):
        for y in range(NB):
            ref[x, pl.ds(z * 8, 8), y * LANES : (y + 1) * LANES] = v[y]

    def advect(xs, z):
        a, right, fx1, u1 = at(al, xs[0] + 1, z), None, None, None
        left, u0 = at(al, xs[0], z), raw(vx, xs[0], z)
        fx0 = u0 * jnp.where(u0 > 0, left, a)
        for x in xs:
            right, u1 = at(al, x + 2, z), raw(vx, x + 1, z)
            w0, w1 = raw(vz, x, z), raw(vz, x, z, 1)
            fx1 = u1 * jnp.where(u1 > 0, a, right)
            fz0 = w0 * jnp.where(w0 > 0, at(al, x + 1, z, -1), a)
            fz1 = w1 * jnp.where(w1 > 0, a, at(al, x + 1, z, 1))
            new = a - 0.2 * (fx1 - fx0 + fz1 - fz0)
            to_out(alpha_o, x, z, new)
            rho[x + 1, :, pl.ds(ROW0 + z * 8, 8), :] = 1.0 + 9.0 * new
            a, fx0 = right, fx1

    def coefficients(xs, z):
        d = at(rho, xs[0] + 1, z)
        cm = recip(d + at(rho, xs[0], z))
        for x in xs:
            right = at(rho, x + 2, z)
            cp = recip(d + right)
            zm, zp = recip(d + at(rho, x + 1, z, -1)), recip(d + at(rho, x + 1, z, 1))
            ym = recip(d + y_minus(d))
            yp = y_plus(ym)
            yp = jnp.where(last, recip(d), yp)
            inv = recip((cm + cp) + (zm + zp) + (ym + yp))
            for ref, v in zip((axm, axp, azm, azp, aym, ayp), (cm, cp, zm, zp, ym, yp)):
                ref[x, :, pl.ds(z * 8, 8), :] = v * inv
            rr[x, :, pl.ds(z * 8, 8), :] = 0.5 * inv
            d, cm = right, cp

    def sweep(p, store, source, xs, z):
        left, mid = at(p, xs[0], z), at(p, xs[0] + 1, z)
        for x in xs:
            right = at(p, x + 2, z)
            store(
                x, z,
                (raw(axm, x, z) * left + raw(axp, x, z) * right)
                + (raw(azm, x, z) * at(p, x + 1, z, -1) + raw(azp, x, z) * at(p, x + 1, z, 1))
                + (raw(aym, x, z) * y_minus(mid) + raw(ayp, x, z) * y_plus(mid) - source(x, z)),
            )
            left, mid = mid, right

    def scaled(x, z):
        r = raw(rr, x, z) * raw(div, x, z)
        rr[x, :, pl.ds(z * 8, 8), :] = r
        return r

    def kept(x, z):
        return raw(rr, x, z)

    def into(ref):
        def store(x, z, v):
            ref[x + 1, :, pl.ds(ROW0 + z * 8, 8), :] = v

        return store

    def sweep1(xs, z):
        sweep(p0, into(p1), scaled, xs, z)

    def sweep2(xs, z):
        sweep(p1, into(p2), kept, xs, z)

    def sweep3(xs, z):
        sweep(p2, lambda x, z, v: to_out(press_o, x, z, v), kept, xs, z)

    tiles = CZ // 8
    middle = tuple(range(1, CX - 1))

    def interior(fn, first, count):
        def step(i, c):
            fn(middle, first + i)
            return c

        lax.fori_loop(0, count, step, 0)

    def edges(fn):
        def step(i, c):
            fn(middle, i * (tiles - 1))
            return c

        lax.fori_loop(0, 2, step, 0)

    def ends(fn):
        def step(i, c):
            for k in range(4):
                fn((0,), i * 4 + k)
                fn((CX - 1,), i * 4 + k)
            return c

        lax.fori_loop(0, tiles // 4, step, 0)

    inside = tiles - 2

    def recv(copies):
        for c in copies:
            c.wait_recv()

    interior(advect, 1, inside)
    def a1_wait(k, c):
        src = (a_me + GA - k) % GA
        rcopy(s1.at[src], r1.at[src], a1s.at[k], a1r.at[k], a_peer(k)[1]).wait_recv()
        return c

    lax.fori_loop(1, GA, a1_wait, 0)
    got = dot(perm_s[...], r1[:, 0:REC_A, :].reshape(SLOTS, LANES)).astype(BF16)
    mrow = iota((META, LANES), 0)
    m1 = jnp.zeros((META, LANES), F32)
    for a in range(GA):
        m1 = jnp.where(mrow == a, r1[a, REC_A:, :].astype(F32), m1)
    m1 = m1.astype(BF16)
    for b in range(GB):
        s2[b, 0:REC_B, :] = got[b * REC_B : (b + 1) * REC_B]
        s2[b, REC_B:, :] = m1

    def b1_start(k, c):
        b, dev = b_peer(k)
        rcopy(s2.at[b], r2.at[b_me], b1s.at[k], b1r.at[k], dev).start()
        return c

    lax.fori_loop(1, GB, b1_start, 0)
    r2[b_me] = s2[b_me]

    recv(ez_al + ez_vz)
    fill_z([(0, al, 1, ROW0 - 1, 0), (1, al, 1, ROW0 + CZ, DEPTHS - 1), (2, vz, 0, CZ, DEPTHS - 1)])
    edges(advect)

    recv(e_al + e_vx)
    fill_x(0, al)
    vx[CX] = jnp.where(slab == SLABS - 1, 0.0, xr[2].astype(F32))
    ends(advect)
    pack_x(5, rho)
    e_rho, ez_rho = xpair(5), zpair(5)
    start(e_rho)
    pack_z([(5, rho, 1, ROW0 + CZ - 1), (6, rho, 1, ROW0)])
    start(ez_rho)

    interior(coefficients, 1, inside)
    loaded("div")

    def b1_wait(k, c):
        src = (b_me + GB - k) % GB
        rcopy(s2.at[src], r2.at[src], b1s.at[k], b1r.at[k], b_peer(k)[1]).wait_recv()
        return c

    lax.fori_loop(1, GB, b1_wait, 0)

    m2 = r2[:, REC_B:, :].reshape(GB * META, LANES)
    srow, scol = iota((SLOTS, GB * META), 0), iota((SLOTS, GB * META), 1)
    wide = dot(onehot(scol == (srow >> 5) * META + ((srow >> 2) & (GA - 1))), m2)
    pick = iota((SLOTS, LANES), 1) - (iota((SLOTS, LANES), 0) & 3) - b_me * CAP
    hi_c = jnp.sum(jnp.where(pick == 0, wide, 0.0), axis=1, keepdims=True)
    lo_c = jnp.sum(jnp.where(pick == REC_A, wide, 0.0), axis=1, keepdims=True)
    seg_c = hi_c.astype(I32) * 64 + lo_c.astype(I32)
    block_c, key_c = seg_c & 3, seg_c >> 2
    key_f = jnp.broadcast_to(key_c, (SLOTS, LANES)).astype(F32)
    key_r = key_f.T[0:1]
    recs = r2[:, 0:REC_B, :].reshape(SLOTS, LANES)
    for y in range(NB):
        rmat[:, y * LANES : (y + 1) * LANES] = jnp.where(
            block_c == y, recs.astype(F32), 0.0
        ).astype(BF16)

    def hull(planes):
        z = iota((CZ, SLOTS), 0)
        cells = jnp.concatenate([z + x * CZ for x in planes], axis=0).astype(F32)
        h = dot(onehot(cells == key_r), rmat[...])
        for k, x in enumerate(planes):
            for y in range(NB):
                div[x, y] += h[k * CZ : (k + 1) * CZ, y * LANES : (y + 1) * LANES]

    hull((0, CX - 1))
    recv(ez_p0 + ez_rho)
    fill_z([
        (3, p0, 1, ROW0 - 1, 0), (4, p0, 1, ROW0 + CZ, DEPTHS - 1),
        (5, rho, 1, ROW0 - 1, 0), (6, rho, 1, ROW0 + CZ, DEPTHS - 1),
    ])
    edges(coefficients)
    recv(e_p0 + e_rho)
    fill_x(3, p0)
    fill_x(5, rho)
    ends(coefficients)
    ends(sweep1)
    pack_x(7, p1)
    e_p1, ez_p1 = xpair(7), zpair(7)
    start(e_p1)
    for i in range(1, CX - 1, 7):
        hull(tuple(range(i, i + 7)))
    edges(sweep1)
    pack_z([(7, p1, 1, ROW0 + CZ - 1), (8, p1, 1, ROW0)])
    start(ez_p1)
    interior(sweep1, 1, inside)
    for c in range(CX * CZ // LANES):
        g_s[:, c * LANES : (c + 1) * LANES] = onehot(
            key_f == (iota((SLOTS, LANES), 1) + c * LANES).astype(F32)
        )
    interior(sweep2, 1, inside // 2)
    recv(ez_p1)
    fill_z([(7, p1, 1, ROW0 - 1, 0), (8, p1, 1, ROW0 + CZ, DEPTHS - 1)])
    recv(e_p1)
    fill_x(7, p1)
    ends(sweep2)
    pack_x(9, p2)
    e_p2, ez_p2 = xpair(9), zpair(9)
    start(e_p2)
    edges(sweep2)
    pack_z([(9, p2, 1, ROW0 + CZ - 1), (10, p2, 1, ROW0)])
    start(ez_p2)
    interior(sweep2, 1 + inside // 2, inside - inside // 2)
    interior(sweep3, 1, inside)
    recv(ez_p2)
    fill_z([(9, p2, 1, ROW0 - 1, 0), (10, p2, 1, ROW0 + CZ, DEPTHS - 1)])
    edges(sweep3)
    for x in range(2, CX - 2):
        pb[x * CZ : (x + 1) * CZ, :] = press_o[x].astype(BF16)
    acc[...] = dot(g_s[:, 2 * CZ : (CX - 2) * CZ], pb[2 * CZ : (CX - 2) * CZ, :])
    recv(e_p2)
    fill_x(9, p2)
    ends(sweep3)

    for x in (0, 1, CX - 2, CX - 1):
        pb[x * CZ : (x + 1) * CZ, :] = press_o[x].astype(BF16)
    wet = acc[...] + (
        dot(g_s[:, 0 : 2 * CZ], pb[0 : 2 * CZ, :])
        + dot(g_s[:, (CX - 2) * CZ :], pb[(CX - 2) * CZ :, :])
    )
    back = jnp.zeros((SLOTS, LANES), F32)
    for y in range(NB):
        back = jnp.where(block_c == y, wet[:, y * LANES : (y + 1) * LANES], back)
    back = back.astype(BF16).astype(F32)
    wb[...] = back.reshape(GA * GB, CAP, LANES)

    def home(k, c):
        d = (me + k) % (GA * GB)
        rcopy(wb.at[d], tb.at[me], home_s, home_r, (d // DEPTHS, d % DEPTHS)).start()
        return c

    lax.fori_loop(1, GA * GB, home, 0)
    others = pl.ds(0, GA * GB - 1)
    tb[me] = wb[me]
    pltpu.make_async_copy(wb.at[others], tb.at[others], home_r).wait()
    panel_o[...] = dot(q_s[...], tb[...].reshape(SLOTS, LANES).astype(BF16)).astype(BF16)
    pltpu.make_async_copy(wb.at[others], tb.at[others], home_s).wait()

    for c in sends:
        c.wait_send()

    def b_done(k, c):
        b, dev = b_peer(k)
        rcopy(s2.at[b], r2.at[b_me], b1s.at[k], b1r.at[k], dev).wait_send()
        return c

    def a_done(k, c):
        a, dev = a_peer(k)
        rcopy(s1.at[a], r1.at[a_me], a1s.at[k], a1r.at[k], dev).wait_send()
        return c

    lax.fori_loop(1, GB, b_done, 0)
    lax.fori_loop(1, GA, a_done, 0)


def deliver(press, alpha, panel, press_o, alpha_o, panel_o, sem):
    pairs = ((press, press_o), (alpha, alpha_o), (panel, panel_o))
    copies = [pltpu.make_async_copy(s, d, sem.at[i]) for i, (s, d) in enumerate(pairs)]
    for c in copies:
        c.start()
    for c in copies:
        c.wait()


def body(alpha, vel_x, vel_z, divergence, press_guess, panel_records, panel_dest, panel_segment):
    padded = pltpu.VMEM((CX + 2, NB, PADZ, LANES), F32)
    plain = pltpu.VMEM((CX, NB, CZ, LANES), F32)
    hbm = pl.BlockSpec(memory_space=pltpu.HBM)
    vmem = pl.BlockSpec(memory_space=pltpu.VMEM)
    dma = lambda n: pltpu.SemaphoreType.DMA((n,))
    field = pltpu.VMEM((CX, CZ, BEAM), F32)
    outs = pl.pallas_call(
        kernel,
        out_shape=(field, field, pltpu.VMEM((PAN, LANES), BF16)),
        in_specs=[hbm] * 8,
        out_specs=(vmem, vmem, vmem),
        scratch_shapes=[
            pltpu.VMEM((PAN, LANES), BF16), pltpu.VMEM((1, PAN), I32), pltpu.VMEM((1, PAN), I32),
            padded,
            pltpu.VMEM((CX + 1, NB, CZ, LANES), F32),
            pltpu.VMEM((CX, NB, CZ + 8, LANES), F32),
            plain,
            padded, padded, padded, padded,
            plain, plain, plain, plain, plain, plain, plain,
            pltpu.VMEM((11, CX, NB, LANES), F32),
            pltpu.VMEM((11, CX, NB, LANES), F32),
            pltpu.VMEM((11, NB, CZ, LANES), BF16),
            pltpu.VMEM((11, NB, CZ, LANES), BF16),
            pltpu.VMEM((SLOTS, BEAM), F32),
            pltpu.VMEM((GA, REC_A + META, LANES), BF16),
            pltpu.VMEM((GA, REC_A + META, LANES), BF16),
            pltpu.VMEM((GB, REC_B + META, LANES), BF16),
            pltpu.VMEM((GB, REC_B + META, LANES), BF16),
            pltpu.VMEM((GA * GB, CAP, LANES), F32),
            pltpu.VMEM((GA * GB, CAP, LANES), F32),
            pltpu.VMEM((PAN, SLOTS), BF16),
            pltpu.VMEM((SLOTS, CX * CZ), BF16),
            pltpu.VMEM((SLOTS, SLOTS), BF16),
            pltpu.VMEM((SLOTS, BEAM), BF16),
            pltpu.VMEM((CX * CZ, BEAM), BF16),
            dma(23), dma(11), dma(11), dma(11), dma(11),
            dma(GB), dma(GB), dma(GA), dma(GA), pltpu.SemaphoreType.DMA, pltpu.SemaphoreType.DMA,
        ],
        compiler_params=pltpu.CompilerParams(
            collective_id=0, has_side_effects=True, vmem_limit_bytes=50 * 1024 * 1024
        ),
    )(
        alpha, vel_x, vel_z, divergence, press_guess, panel_records,
        panel_dest.reshape(1, PAN), panel_segment.reshape(1, PAN),
    )
    outs = [pltpu.with_memory_space_constraint(o, pltpu.VMEM) for o in outs]
    return pl.pallas_call(
        deliver,
        out_shape=tuple(jax.ShapeDtypeStruct(o.shape, o.dtype) for o in outs),
        in_specs=[pl.BlockSpec(memory_space=pl.ANY)] * 3,
        out_specs=(hbm,) * 3,
        scratch_shapes=[dma(3)],
        compiler_params=pltpu.CompilerParams(vmem_limit_bytes=1024 * 1024),
    )(*outs)


def solution(mesh):
    field = P("slab", "depth", None)
    rows = P(("slab", "depth"), None)
    return jax.shard_map(
        body, mesh=mesh, in_specs=(field,) * 5 + (rows,) * 3,
        out_specs=(field, field, rows), check_vma=False,
    )
```

```python
import jax
import jax.numpy as jnp
from jax import lax
from jax.experimental import pallas as pl
from jax.experimental.pallas import tpu as pltpu
from jax.sharding import PartitionSpec as P

MESH = pl.DeviceIdType.MESH
F32, BF16, I32 = jnp.float32, jnp.bfloat16, jnp.int32
CX, CZ, BEAM, LANES = 16, 64, 512, 128
NB = BEAM // LANES
ROW0 = 8
PADZ = CZ + 16
SLABS, DEPTHS = 32, 4
GA, GB = 8, 16
CAP = 4
SLOTS = GA * GB * CAP
PAN = 256
REC_B, REC_A = GA * CAP, GB * CAP
META = 16


def iota(shape, dim):
    return lax.broadcasted_iota(I32, shape, dim)


def onehot(cond):
    return jnp.where(cond, 1.0, 0.0).astype(BF16)


def dot(a, b):
    return jnp.dot(a, b, preferred_element_type=F32)


def recip(d):
    r = pl.reciprocal(d, approx=True)
    return r * (2.0 - d * r)


def kernel(
    alpha_h, velx_h, velz_h, div_h, press_h, rec_h, dest_h, seg_h,
    press_o, alpha_o, panel_o,
    rec_ref, dest_ref, seg_ref, al, vx, vz, div, rho, p0, p1, p2,
    axm, axp, azm, azp, aym, ayp, rr,
    zs, zr, xb, xr, acc,
    s1, r1, s2, r2, wb, tb,
    q_s, g_s, perm_s, rmat, pb,
    load_sem, xs_sem, xr_sem, zs_sem, zr_sem,
    b1s, b1r, a1s, a1r, home_s, home_r,
):
    slab = lax.axis_index("slab")
    depth = lax.axis_index("depth")
    up_s, dn_s = (slab + 1) % SLABS, (slab + SLABS - 1) % SLABS
    up_d, dn_d = (depth + 1) % DEPTHS, (depth + DEPTHS - 1) % DEPTHS
    x_up, x_dn = (up_s, depth), (dn_s, depth)
    z_up, z_dn = (slab, up_d), (slab, dn_d)
    b_me, core = slab // 2, slab % 2
    a_me = core * DEPTHS + depth
    me = slab * DEPTHS + depth

    def b_peer(k):
        b = (b_me + k) % GB
        return b, (b * 2 + core, depth)

    def a_peer(k):
        a = (a_me + k) % GA
        return a, (b_me * 2 + a // DEPTHS, a % DEPTHS)

    loads = {}
    sem_i = 0

    def load(name, pairs):
        nonlocal sem_i
        loads[name] = []
        for src, dst in pairs:
            c = pltpu.make_async_copy(src, dst, load_sem.at[sem_i])
            c.start()
            sem_i += 1
            loads[name].append(c)

    def loaded(name):
        for c in loads[name]:
            c.wait()

    def field(src, dst):
        return [(src.at[:, :, pl.ds(y * LANES, LANES)], dst(y)) for y in range(NB)]

    load("panels", [(dest_h, dest_ref), (seg_h, seg_ref), (rec_h, rec_ref)])
    load("al", field(alpha_h, lambda y: al.at[pl.ds(1, CX), y, pl.ds(ROW0, CZ), :]))
    load("vx", field(velx_h, lambda y: vx.at[pl.ds(0, CX), y, :, :]))
    load("vz", field(velz_h, lambda y: vz.at[:, y, pl.ds(0, CZ), :]))
    load("p0", field(press_h, lambda y: p0.at[pl.ds(1, CX), y, pl.ds(ROW0, CZ), :]))
    load("div", field(div_h, lambda y: div.at[:, y, :, :]))

    barrier = pltpu.get_barrier_semaphore()
    for dev in (x_up, x_dn, z_up, z_dn):
        pl.semaphore_signal(barrier, inc=1, device_id=dev, device_id_type=MESH)

    def sig_b(k, c):
        pl.semaphore_signal(barrier, inc=1, device_id=b_peer(k)[1], device_id_type=MESH)
        return c

    def sig_a(k, c):
        pl.semaphore_signal(barrier, inc=1, device_id=a_peer(k)[1], device_id_type=MESH)
        return c

    lax.fori_loop(1, GB, sig_b, 0)
    lax.fori_loop(1, GA, sig_a, 0)

    loaded("panels")
    dest, seg = dest_ref[...], seg_ref[...]
    own = onehot(iota((GA * GB, PAN), 0) == dest)
    before = dot(own, onehot(iota((PAN, PAN), 0) < iota((PAN, PAN), 1)))
    slot = jnp.sum(own.astype(F32) * before, axis=0, keepdims=True)
    lane_of = (dest >> 3) * CAP + slot.astype(I32)
    place = (dest & (GA - 1)) * REC_A + lane_of
    packed = dot(onehot(iota((SLOTS, PAN), 0) == place), rec_ref[...]).astype(BF16)
    row = iota((LANES, PAN), 0)
    hi, lo = (seg >> 6).astype(F32), (seg & 63).astype(F32)
    bt = jnp.where(row == lane_of, hi, 0.0) + jnp.where(row == lane_of + REC_A, lo, 0.0)
    meta = lax.dot_general(
        onehot(iota((16, PAN), 0) == (dest & (GA - 1))), bt.astype(BF16),
        (((1,), (1,)), ((), ())), preferred_element_type=F32,
    )
    for a in range(GA):
        s1[a, 0:REC_A, :] = packed[a * REC_A : (a + 1) * REC_A]
        s1[a, REC_A:, :] = jnp.broadcast_to(meta[a : a + 1], (META, LANES)).astype(BF16)

    def rcopy(src, dst, ss, rs, dev):
        return pltpu.make_async_remote_copy(
            src_ref=src, dst_ref=dst, send_sem=ss, recv_sem=rs,
            device_id=dev, device_id_type=MESH,
        )

    def xcopy(i, dev):
        return rcopy(xb.at[i], xr.at[i], xs_sem.at[i], xr_sem.at[i], dev)

    def zcopy(i, dev):
        return rcopy(zs.at[i], zr.at[i], zs_sem.at[i], zr_sem.at[i], dev)

    def xpair(i):
        return [xcopy(i, x_up), xcopy(i + 1, x_dn)]

    def pack_x(i, ref):
        xb[i] = ref[CX, :, ROW0 : ROW0 + CZ, :].astype(BF16)
        xb[i + 1] = ref[1, :, ROW0 : ROW0 + CZ, :].astype(BF16)

    def fill_x(i, ref):
        low, high = xr[i].astype(F32), xr[i + 1].astype(F32)
        ref[0, :, ROW0 : ROW0 + CZ, :] = jnp.where(slab == 0, 0.0, low)
        ref[CX + 1, :, ROW0 : ROW0 + CZ, :] = jnp.where(slab == SLABS - 1, 0.0, high)

    def zpair(i):
        return [zcopy(i, z_up), zcopy(i + 1, z_dn)]

    def pack_z(items):
        def step(g, c):
            for k in range(4):
                x = g * 4 + k
                for i, ref, xo, r in items:
                    zs[i, x] = ref[x + xo, :, r, :]
            return c

        lax.fori_loop(0, CX // 4, step, 0)

    def fill_z(items):
        def step(g, c):
            for k in range(4):
                x = g * 4 + k
                for i, ref, xo, r, edge in items:
                    ref[x + xo, :, r, :] = jnp.where(depth == edge, 0.0, zr[i, x])
            return c

        lax.fori_loop(0, CX // 4, step, 0)

    sends = []

    def start(copies):
        for c in copies:
            c.start()
        sends.extend(copies)

    pl.semaphore_wait(barrier, 4 + (GB - 1) + (GA - 1))

    def a1_start(k, c):
        a, dev = a_peer(k)
        rcopy(s1.at[a], r1.at[a_me], a1s.at[k], a1r.at[k], dev).start()
        return c

    lax.fori_loop(1, GA, a1_start, 0)
    r1[a_me] = s1[a_me]

    loaded("al")
    pack_x(0, al)
    pack_z([(0, al, 1, ROW0 + CZ - 1), (1, al, 1, ROW0)])
    e_al, ez_al = xpair(0), zpair(0)
    start(e_al + ez_al)
    loaded("vx")
    loaded("vz")
    xb[2] = vx[0].astype(BF16)
    pack_z([(2, vz, 0, 0)])
    e_vx, ez_vz = [xcopy(2, x_dn)], [zcopy(2, z_dn)]
    start(e_vx + ez_vz)

    loaded("p0")
    pack_x(3, p0)
    pack_z([(3, p0, 1, ROW0 + CZ - 1), (4, p0, 1, ROW0)])
    e_p0, ez_p0 = xpair(3), zpair(3)
    start(e_p0 + ez_p0)

    answer = dest * CAP + slot.astype(I32)
    place_t = jnp.broadcast_to(answer.astype(F32), (LANES, PAN)).T
    for c in range(SLOTS // LANES):
        q_s[:, c * LANES : (c + 1) * LANES] = onehot(
            place_t == (iota((PAN, LANES), 1) + c * LANES).astype(F32)
        )
    pr, pc = iota((SLOTS, SLOTS), 0), iota((SLOTS, SLOTS), 1)
    perm_s[...] = onehot(
        pc == (((pr >> 2) & (GA - 1)) * REC_A + (pr >> 5) * CAP + (pr & 3))
    )

    lane = iota((NB, 8, LANES), 2)
    zero1 = jnp.zeros((1, 8, LANES), F32)

    def y_minus(v):
        r = pltpu.roll(v, 1, 2)
        return jnp.where(lane == 0, jnp.concatenate([zero1, r[: NB - 1]], axis=0), r)

    def y_plus(v):
        r = pltpu.roll(v, LANES - 1, 2)
        return jnp.where(lane == LANES - 1, jnp.concatenate([r[1:], zero1], axis=0), r)

    def at(ref, x, z, shift=0):
        return ref[x, :, pl.ds(ROW0 + z * 8 + shift, 8), :]

    def raw(ref, x, z, shift=0):
        return ref[x, :, pl.ds(z * 8 + shift, 8), :]

    def to_out(ref, x, z, v):
        for y in range(NB):
            ref[x, pl.ds(z * 8, 8), y * LANES : (y + 1) * LANES] = v[y]

    def advect(xs, z):
        a, right, fx1, u1 = at(al, xs[0] + 1, z), None, None, None
        left, u0 = at(al, xs[0], z), raw(vx, xs[0], z)
        fx0 = u0 * jnp.where(u0 > 0, left, a)
        for x in xs:
            right, u1 = at(al, x + 2, z), raw(vx, x + 1, z)
            w0, w1 = raw(vz, x, z), raw(vz, x, z, 1)
            fx1 = u1 * jnp.where(u1 > 0, a, right)
            fz0 = w0 * jnp.where(w0 > 0, at(al, x + 1, z, -1), a)
            fz1 = w1 * jnp.where(w1 > 0, a, at(al, x + 1, z, 1))
            new = a - 0.2 * (fx1 - fx0 + fz1 - fz0)
            to_out(alpha_o, x, z, new)
            rho[x + 1, :, pl.ds(ROW0 + z * 8, 8), :] = 1.0 + 9.0 * new
            a, fx0 = right, fx1

    def first(xs, z):
        d = at(rho, xs[0] + 1, z)
        cm = recip(d + at(rho, xs[0], z))
        left, mid = at(p0, xs[0], z), at(p0, xs[0] + 1, z)
        for x in xs:
            beyond, right = at(rho, x + 2, z), at(p0, x + 2, z)
            cp = recip(d + beyond)
            zm, zp = recip(d + at(rho, x + 1, z, -1)), recip(d + at(rho, x + 1, z, 1))
            ym = recip(d + y_minus(d))
            yp = y_plus(ym)
            wall = jnp.where(lane[:1] == LANES - 1, recip(d[NB - 1 :]), yp[NB - 1 :])
            yp = jnp.concatenate([yp[: NB - 1], wall], axis=0)
            inv = recip((cm + cp) + (zm + zp) + (ym + yp))
            c = [v * inv for v in (cm, cp, zm, zp, ym, yp)]
            for ref, v in zip((axm, axp, azm, azp, aym, ayp), c):
                ref[x, :, pl.ds(z * 8, 8), :] = v
            half = 0.5 * inv
            r = raw(div, x, z) * half
            rr[x, :, pl.ds(z * 8, 8), :] = r
            div[x, :, pl.ds(z * 8, 8), :] = half
            p1[x + 1, :, pl.ds(ROW0 + z * 8, 8), :] = (
                (c[0] * left + c[1] * right)
                + (c[2] * at(p0, x + 1, z, -1) + c[3] * at(p0, x + 1, z, 1))
                + (c[4] * y_minus(mid) + c[5] * y_plus(mid) - r)
            )
            d, cm, left, mid = beyond, cp, mid, right

    def sweep(p, store, xs, z):
        left, mid = at(p, xs[0], z), at(p, xs[0] + 1, z)
        for x in xs:
            right = at(p, x + 2, z)
            store(
                x, z,
                (raw(axm, x, z) * left + raw(axp, x, z) * right)
                + (raw(azm, x, z) * at(p, x + 1, z, -1) + raw(azp, x, z) * at(p, x + 1, z, 1))
                + (raw(aym, x, z) * y_minus(mid) + raw(ayp, x, z) * y_plus(mid) - raw(rr, x, z)),
            )
            left, mid = mid, right

    def into(ref):
        def store(x, z, v):
            ref[x + 1, :, pl.ds(ROW0 + z * 8, 8), :] = v

        return store

    def sweep2(xs, z):
        sweep(p1, into(p2), xs, z)

    def sweep3(xs, z):
        sweep(p2, lambda x, z, v: to_out(press_o, x, z, v), xs, z)

    tiles = CZ // 8
    middle = tuple(range(1, CX - 1))

    def interior(fn, first, count):
        def step(i, c):
            fn(middle, first + i)
            return c

        lax.fori_loop(0, count, step, 0)

    def edges(fn):
        def step(i, c):
            fn(middle, i * (tiles - 1))
            return c

        lax.fori_loop(0, 2, step, 0)

    def ends(fn):
        def step(i, c):
            for k in range(4):
                fn((0,), i * 4 + k)
                fn((CX - 1,), i * 4 + k)
            return c

        lax.fori_loop(0, tiles // 4, step, 0)

    inside, early = tiles - 2, 5

    def recv(copies):
        for c in copies:
            c.wait_recv()

    interior(advect, 1, inside)
    def a1_wait(k, c):
        src = (a_me + GA - k) % GA
        rcopy(s1.at[src], r1.at[src], a1s.at[k], a1r.at[k], a_peer(k)[1]).wait_recv()
        return c

    lax.fori_loop(1, GA, a1_wait, 0)
    got = dot(perm_s[...], r1[:, 0:REC_A, :].reshape(SLOTS, LANES)).astype(BF16)
    mrow = iota((META, LANES), 0)
    m1 = jnp.zeros((META, LANES), F32)
    for a in range(GA):
        m1 = jnp.where(mrow == a, r1[a, REC_A:, :].astype(F32), m1)
    m1 = m1.astype(BF16)
    for b in range(GB):
        s2[b, 0:REC_B, :] = got[b * REC_B : (b + 1) * REC_B]
        s2[b, REC_B:, :] = m1

    def b1_start(k, c):
        b, dev = b_peer(k)
        rcopy(s2.at[b], r2.at[b_me], b1s.at[k], b1r.at[k], dev).start()
        return c

    lax.fori_loop(1, GB, b1_start, 0)
    r2[b_me] = s2[b_me]

    recv(ez_al + ez_vz)
    fill_z([(0, al, 1, ROW0 - 1, 0), (1, al, 1, ROW0 + CZ, DEPTHS - 1), (2, vz, 0, CZ, DEPTHS - 1)])
    edges(advect)

    recv(e_al + e_vx)
    fill_x(0, al)
    vx[CX] = jnp.where(slab == SLABS - 1, 0.0, xr[2].astype(F32))
    ends(advect)
    pack_x(5, rho)
    e_rho, ez_rho = xpair(5), zpair(5)
    start(e_rho)
    pack_z([(5, rho, 1, ROW0 + CZ - 1), (6, rho, 1, ROW0)])
    start(ez_rho)

    loaded("div")
    interior(first, 1, inside)
    recv(ez_p0 + ez_rho)
    fill_z([
        (3, p0, 1, ROW0 - 1, 0), (4, p0, 1, ROW0 + CZ, DEPTHS - 1),
        (5, rho, 1, ROW0 - 1, 0), (6, rho, 1, ROW0 + CZ, DEPTHS - 1),
    ])
    edges(first)

    def b1_wait(k, c):
        src = (b_me + GB - k) % GB
        rcopy(s2.at[src], r2.at[src], b1s.at[k], b1r.at[k], b_peer(k)[1]).wait_recv()
        return c

    lax.fori_loop(1, GB, b1_wait, 0)

    m2 = r2[:, REC_B:, :].reshape(GB * META, LANES)
    srow, scol = iota((SLOTS, GB * META), 0), iota((SLOTS, GB * META), 1)
    wide = dot(onehot(scol == (srow >> 5) * META + ((srow >> 2) & (GA - 1))), m2)
    pick = iota((SLOTS, LANES), 1) - (iota((SLOTS, LANES), 0) & 3) - b_me * CAP
    own_meta = jnp.where((pick == 0) | (pick == REC_A), wide, 0.0).astype(BF16)
    weight_c = jnp.where(iota((LANES, LANES), 0) < REC_A, 64.0, 1.0).astype(BF16)
    weight_r = jnp.where(iota((META, LANES), 1) < REC_A, 64.0, 1.0).astype(BF16)
    seg_c = dot(own_meta, weight_c).astype(I32)
    seg_r = lax.dot_general(
        weight_r, own_meta, (((1,), (1,)), ((), ())), preferred_element_type=F32
    )[0:1].astype(I32)
    block_c, key_f = seg_c & 3, (seg_c >> 2).astype(F32)
    key_r = (seg_r >> 2).astype(F32)
    recs = r2[:, 0:REC_B, :].reshape(SLOTS, LANES)
    for y in range(NB):
        rmat[:, y * LANES : (y + 1) * LANES] = jnp.where(
            block_c == y, recs.astype(F32), 0.0
        ).astype(BF16)

    def hull(planes):
        z = iota((CZ, SLOTS), 0)
        cells = jnp.concatenate([z + x * CZ for x in planes], axis=0).astype(F32)
        h = dot(onehot(cells == key_r), rmat[...])
        for k, x in enumerate(planes):
            for y in range(NB):
                part = h[k * CZ : (k + 1) * CZ, y * LANES : (y + 1) * LANES] * div[x, y]
                rr[x, y] += part
                p1[x + 1, y, ROW0 : ROW0 + CZ, :] -= part

    recv(e_p0 + e_rho)
    fill_x(3, p0)
    fill_x(5, rho)
    ends(first)
    hull((0, CX - 1))
    pack_x(7, p1)
    e_p1, ez_p1 = xpair(7), zpair(7)
    start(e_p1)
    for i in range(1, CX - 1, 7):
        hull(tuple(range(i, i + 7)))
    pack_z([(7, p1, 1, ROW0 + CZ - 1), (8, p1, 1, ROW0)])
    start(ez_p1)
    for c in range(CX * CZ // LANES):
        g_s[:, c * LANES : (c + 1) * LANES] = onehot(
            key_f == (iota((SLOTS, LANES), 1) + c * LANES).astype(F32)
        )
    interior(sweep2, 1, early)
    recv(ez_p1)
    fill_z([(7, p1, 1, ROW0 - 1, 0), (8, p1, 1, ROW0 + CZ, DEPTHS - 1)])
    recv(e_p1)
    fill_x(7, p1)
    ends(sweep2)
    pack_x(9, p2)
    e_p2, ez_p2 = xpair(9), zpair(9)
    start(e_p2)
    edges(sweep2)
    pack_z([(9, p2, 1, ROW0 + CZ - 1), (10, p2, 1, ROW0)])
    start(ez_p2)
    interior(sweep2, 1 + early, inside - early)
    interior(sweep3, 1, inside)
    recv(ez_p2)
    fill_z([(9, p2, 1, ROW0 - 1, 0), (10, p2, 1, ROW0 + CZ, DEPTHS - 1)])
    edges(sweep3)
    for x in range(2, CX - 2):
        pb[x * CZ : (x + 1) * CZ, :] = press_o[x].astype(BF16)
    acc[...] = dot(g_s[:, 2 * CZ : (CX - 2) * CZ], pb[2 * CZ : (CX - 2) * CZ, :])
    recv(e_p2)
    fill_x(9, p2)
    ends(sweep3)

    for x in (0, 1, CX - 2, CX - 1):
        pb[x * CZ : (x + 1) * CZ, :] = press_o[x].astype(BF16)
    wet = acc[...] + (
        dot(g_s[:, 0 : 2 * CZ], pb[0 : 2 * CZ, :])
        + dot(g_s[:, (CX - 2) * CZ :], pb[(CX - 2) * CZ :, :])
    )
    back = jnp.zeros((SLOTS, LANES), F32)
    for y in range(NB):
        back = jnp.where(block_c == y, wet[:, y * LANES : (y + 1) * LANES], back)
    back = back.astype(BF16).astype(F32)
    wb[...] = back.reshape(GA * GB, CAP, LANES)

    far = (2, 1, 3, 0)
    for dz in far:
        for dx in far:
            b = (b_me // 4 + dz) % 4 * 4 + (b_me % 4 + dx) % 4

            def home(k, c, b=b):
                a = (a_me + k) % GA
                d = b * GA + a
                dev = (b * 2 + a // DEPTHS, a % DEPTHS)
                rcopy(wb.at[d], tb.at[me], home_s, home_r, dev).start()
                return c

            lax.fori_loop(1 if dz == dx == 0 else 0, GA, home, 0)
    others = pl.ds(0, GA * GB - 1)
    tb[me] = wb[me]
    pltpu.make_async_copy(wb.at[others], tb.at[others], home_r).wait()
    panel_o[...] = dot(q_s[...], tb[...].reshape(SLOTS, LANES).astype(BF16)).astype(BF16)
    pltpu.make_async_copy(wb.at[others], tb.at[others], home_s).wait()

    for c in sends:
        c.wait_send()

    def b_done(k, c):
        b, dev = b_peer(k)
        rcopy(s2.at[b], r2.at[b_me], b1s.at[k], b1r.at[k], dev).wait_send()
        return c

    def a_done(k, c):
        a, dev = a_peer(k)
        rcopy(s1.at[a], r1.at[a_me], a1s.at[k], a1r.at[k], dev).wait_send()
        return c

    lax.fori_loop(1, GB, b_done, 0)
    lax.fori_loop(1, GA, a_done, 0)


def deliver(press, alpha, panel, press_o, alpha_o, panel_o, sem):
    pairs = ((press, press_o), (alpha, alpha_o), (panel, panel_o))
    copies = [pltpu.make_async_copy(s, d, sem.at[i]) for i, (s, d) in enumerate(pairs)]
    for c in copies:
        c.start()
    for c in copies:
        c.wait()


def body(alpha, vel_x, vel_z, divergence, press_guess, panel_records, panel_dest, panel_segment):
    padded = pltpu.VMEM((CX + 2, NB, PADZ, LANES), F32)
    plain = pltpu.VMEM((CX, NB, CZ, LANES), F32)
    hbm = pl.BlockSpec(memory_space=pltpu.HBM)
    vmem = pl.BlockSpec(memory_space=pltpu.VMEM)
    dma = lambda n: pltpu.SemaphoreType.DMA((n,))
    field = pltpu.VMEM((CX, CZ, BEAM), F32)
    outs = pl.pallas_call(
        kernel,
        out_shape=(field, field, pltpu.VMEM((PAN, LANES), BF16)),
        in_specs=[hbm] * 8,
        out_specs=(vmem, vmem, vmem),
        scratch_shapes=[
            pltpu.VMEM((PAN, LANES), BF16), pltpu.VMEM((1, PAN), I32), pltpu.VMEM((1, PAN), I32),
            padded,
            pltpu.VMEM((CX + 1, NB, CZ, LANES), F32),
            pltpu.VMEM((CX, NB, CZ + 8, LANES), F32),
            plain,
            padded, padded, padded, padded,
            plain, plain, plain, plain, plain, plain, plain,
            pltpu.VMEM((11, CX, NB, LANES), F32),
            pltpu.VMEM((11, CX, NB, LANES), F32),
            pltpu.VMEM((11, NB, CZ, LANES), BF16),
            pltpu.VMEM((11, NB, CZ, LANES), BF16),
            pltpu.VMEM((SLOTS, BEAM), F32),
            pltpu.VMEM((GA, REC_A + META, LANES), BF16),
            pltpu.VMEM((GA, REC_A + META, LANES), BF16),
            pltpu.VMEM((GB, REC_B + META, LANES), BF16),
            pltpu.VMEM((GB, REC_B + META, LANES), BF16),
            pltpu.VMEM((GA * GB, CAP, LANES), F32),
            pltpu.VMEM((GA * GB, CAP, LANES), F32),
            pltpu.VMEM((PAN, SLOTS), BF16),
            pltpu.VMEM((SLOTS, CX * CZ), BF16),
            pltpu.VMEM((SLOTS, SLOTS), BF16),
            pltpu.VMEM((SLOTS, BEAM), BF16),
            pltpu.VMEM((CX * CZ, BEAM), BF16),
            dma(23), dma(11), dma(11), dma(11), dma(11),
            dma(GB), dma(GB), dma(GA), dma(GA), pltpu.SemaphoreType.DMA, pltpu.SemaphoreType.DMA,
        ],
        compiler_params=pltpu.CompilerParams(
            collective_id=0, has_side_effects=True, vmem_limit_bytes=50 * 1024 * 1024
        ),
    )(
        alpha, vel_x, vel_z, divergence, press_guess, panel_records,
        panel_dest.reshape(1, PAN), panel_segment.reshape(1, PAN),
    )
    outs = [pltpu.with_memory_space_constraint(o, pltpu.VMEM) for o in outs]
    return pl.pallas_call(
        deliver,
        out_shape=tuple(jax.ShapeDtypeStruct(o.shape, o.dtype) for o in outs),
        in_specs=[pl.BlockSpec(memory_space=pl.ANY)] * 3,
        out_specs=(hbm,) * 3,
        scratch_shapes=[dma(3)],
        compiler_params=pltpu.CompilerParams(vmem_limit_bytes=1024 * 1024),
    )(*outs)


def solution(mesh):
    field = P("slab", "depth", None)
    rows = P(("slab", "depth"), None)
    return jax.shard_map(
        body, mesh=mesh, in_specs=(field,) * 5 + (rows,) * 3,
        out_specs=(field, field, rows), check_vma=False,
    )
```

```python
import jax
import jax.numpy as jnp
from jax import lax
from jax.experimental import pallas as pl
from jax.experimental.pallas import tpu as pltpu
from jax.sharding import PartitionSpec as P

MESH = pl.DeviceIdType.MESH
F32, BF16, I32 = jnp.float32, jnp.bfloat16, jnp.int32
CX, CZ, BEAM, LANES = 16, 64, 512, 128
NB = BEAM // LANES
ROW0 = 8
PADZ = CZ + 16
SLABS, DEPTHS = 32, 4
GA, GB = 8, 16
CAP = 4
SLOTS = GA * GB * CAP
PAN = 256
REC_B, REC_A = GA * CAP, GB * CAP
META = 16


def iota(shape, dim):
    return lax.broadcasted_iota(I32, shape, dim)


def onehot(cond):
    return jnp.where(cond, 1.0, 0.0).astype(BF16)


def dot(a, b):
    return jnp.dot(a, b, preferred_element_type=F32)


def recip(d):
    r = pl.reciprocal(d, approx=True)
    return r * (2.0 - d * r)


def kernel(
    alpha_h, velx_h, velz_h, div_h, press_h, rec_h, dest_h, seg_h,
    press_o, alpha_o, panel_o,
    stage, rec_ref, dest_ref, seg_ref, al, vx, vz, div, rho, p0, p1, p2,
    axm, axp, azm, azp, aym, ayp, rr,
    zs, zr, xb, xr, acc,
    s1, r1, s2, r2, wb, tb,
    q_s, g_s, perm_s, rmat, pb,
    load_sem, xs_sem, xr_sem, zs_sem, zr_sem,
    b1s, b1r, a1s, a1r, home_s, home_r,
):
    slab = lax.axis_index("slab")
    depth = lax.axis_index("depth")
    up_s, dn_s = (slab + 1) % SLABS, (slab + SLABS - 1) % SLABS
    up_d, dn_d = (depth + 1) % DEPTHS, (depth + DEPTHS - 1) % DEPTHS
    x_up, x_dn = (up_s, depth), (dn_s, depth)
    z_up, z_dn = (slab, up_d), (slab, dn_d)
    b_me, core = slab // 2, slab % 2
    a_me = core * DEPTHS + depth
    me = slab * DEPTHS + depth

    def b_peer(k):
        b = (b_me + k) % GB
        return b, (b * 2 + core, depth)

    def a_peer(k):
        a = (a_me + k) % GA
        return a, (b_me * 2 + a // DEPTHS, a % DEPTHS)

    loads = {}
    sem_i = 0

    def load(name, pairs):
        nonlocal sem_i
        loads[name] = []
        for src, dst in pairs:
            c = pltpu.make_async_copy(src, dst, load_sem.at[sem_i])
            c.start()
            sem_i += 1
            loads[name].append(c)

    def loaded(name):
        for c in loads[name]:
            c.wait()

    def field(src, dst):
        return [(src.at[:, :, pl.ds(y * LANES, LANES)], dst(y)) for y in range(NB)]

    load("planes", [
        (alpha_h.at[CX - 1], stage.at[0]), (alpha_h.at[0], stage.at[1]), (velx_h.at[0], stage.at[2]),
    ])
    load("panels", [(dest_h, dest_ref), (seg_h, seg_ref), (rec_h, rec_ref)])
    load("al", field(alpha_h, lambda y: al.at[pl.ds(1, CX), y, pl.ds(ROW0, CZ), :]))
    load("vz", field(velz_h, lambda y: vz.at[:, y, pl.ds(0, CZ), :]))
    load("vx", field(velx_h, lambda y: vx.at[pl.ds(0, CX), y, :, :]))
    load("p0", field(press_h, lambda y: p0.at[pl.ds(1, CX), y, pl.ds(ROW0, CZ), :]))
    load("div", field(div_h, lambda y: div.at[:, y, :, :]))

    barrier = pltpu.get_barrier_semaphore()
    for dev in (x_up, x_dn, z_up, z_dn):
        pl.semaphore_signal(barrier, inc=1, device_id=dev, device_id_type=MESH)

    def sig_b(k, c):
        pl.semaphore_signal(barrier, inc=1, device_id=b_peer(k)[1], device_id_type=MESH)
        return c

    def sig_a(k, c):
        pl.semaphore_signal(barrier, inc=1, device_id=a_peer(k)[1], device_id_type=MESH)
        return c

    lax.fori_loop(1, GB, sig_b, 0)
    lax.fori_loop(1, GA, sig_a, 0)

    def rcopy(src, dst, ss, rs, dev):
        return pltpu.make_async_remote_copy(
            src_ref=src, dst_ref=dst, send_sem=ss, recv_sem=rs,
            device_id=dev, device_id_type=MESH,
        )

    def xcopy(i, dev):
        return rcopy(xb.at[i], xr.at[i], xs_sem.at[i], xr_sem.at[i], dev)

    def zcopy(i, dev):
        return rcopy(zs.at[i], zr.at[i], zs_sem.at[i], zr_sem.at[i], dev)

    def xpair(i):
        return [xcopy(i, x_up), xcopy(i + 1, x_dn)]

    def pack_x(i, ref):
        xb[i] = ref[CX, :, ROW0 : ROW0 + CZ, :].astype(BF16)
        xb[i + 1] = ref[1, :, ROW0 : ROW0 + CZ, :].astype(BF16)

    def fill_x(i, ref):
        low, high = xr[i].astype(F32), xr[i + 1].astype(F32)
        ref[0, :, ROW0 : ROW0 + CZ, :] = jnp.where(slab == 0, 0.0, low)
        ref[CX + 1, :, ROW0 : ROW0 + CZ, :] = jnp.where(slab == SLABS - 1, 0.0, high)

    def zpair(i):
        return [zcopy(i, z_up), zcopy(i + 1, z_dn)]

    def pack_z(items):
        def step(g, c):
            for k in range(4):
                x = g * 4 + k
                for i, ref, xo, r in items:
                    zs[i, x] = ref[x + xo, :, r, :]
            return c

        lax.fori_loop(0, CX // 4, step, 0)

    def fill_z(items):
        def step(g, c):
            for k in range(4):
                x = g * 4 + k
                for i, ref, xo, r, edge in items:
                    ref[x + xo, :, r, :] = jnp.where(depth == edge, 0.0, zr[i, x])
            return c

        lax.fori_loop(0, CX // 4, step, 0)

    sends = []

    def start(copies):
        for c in copies:
            c.start()
        sends.extend(copies)

    loaded("planes")
    for i in range(3):
        for y in range(NB):
            xb[i, y] = stage[i, :, y * LANES : (y + 1) * LANES].astype(BF16)
    pl.semaphore_wait(barrier, 4 + (GB - 1) + (GA - 1))
    e_al, e_vx = xpair(0), [xcopy(2, x_dn)]
    start(e_al + e_vx)

    loaded("panels")
    dest, seg = dest_ref[...], seg_ref[...]
    own = onehot(iota((GA * GB, PAN), 0) == dest)
    before = dot(own, onehot(iota((PAN, PAN), 0) < iota((PAN, PAN), 1)))
    slot = jnp.sum(own.astype(F32) * before, axis=0, keepdims=True)
    lane_of = (dest >> 3) * CAP + slot.astype(I32)
    place = (dest & (GA - 1)) * REC_A + lane_of
    packed = dot(onehot(iota((SLOTS, PAN), 0) == place), rec_ref[...]).astype(BF16)
    row = iota((LANES, PAN), 0)
    hi, lo = (seg >> 6).astype(F32), (seg & 63).astype(F32)
    bt = jnp.where(row == lane_of, hi, 0.0) + jnp.where(row == lane_of + REC_A, lo, 0.0)
    meta = lax.dot_general(
        onehot(iota((16, PAN), 0) == (dest & (GA - 1))), bt.astype(BF16),
        (((1,), (1,)), ((), ())), preferred_element_type=F32,
    )
    for a in range(GA):
        s1[a, 0:REC_A, :] = packed[a * REC_A : (a + 1) * REC_A]
        s1[a, REC_A:, :] = jnp.broadcast_to(meta[a : a + 1], (META, LANES)).astype(BF16)

    def a1_start(k, c):
        a, dev = a_peer(k)
        rcopy(s1.at[a], r1.at[a_me], a1s.at[k], a1r.at[k], dev).start()
        return c

    lax.fori_loop(1, GA, a1_start, 0)
    r1[a_me] = s1[a_me]

    loaded("al")
    loaded("vz")
    pack_z([(0, al, 1, ROW0 + CZ - 1), (1, al, 1, ROW0), (2, vz, 0, 0)])
    ez_al, ez_vz = zpair(0), [zcopy(2, z_dn)]
    start(ez_al + ez_vz)
    loaded("vx")
    loaded("p0")
    pack_x(3, p0)
    pack_z([(3, p0, 1, ROW0 + CZ - 1), (4, p0, 1, ROW0)])
    e_p0, ez_p0 = xpair(3), zpair(3)
    start(e_p0 + ez_p0)

    answer = dest * CAP + slot.astype(I32)
    place_t = jnp.broadcast_to(answer.astype(F32), (LANES, PAN)).T
    for c in range(SLOTS // LANES):
        q_s[:, c * LANES : (c + 1) * LANES] = onehot(
            place_t == (iota((PAN, LANES), 1) + c * LANES).astype(F32)
        )
    pr, pc = iota((SLOTS, SLOTS), 0), iota((SLOTS, SLOTS), 1)
    perm_s[...] = onehot(
        pc == (((pr >> 2) & (GA - 1)) * REC_A + (pr >> 5) * CAP + (pr & 3))
    )

    lane = iota((NB, 8, LANES), 2)
    zero1 = jnp.zeros((1, 8, LANES), F32)

    def y_minus(v):
        r = pltpu.roll(v, 1, 2)
        return jnp.where(lane == 0, jnp.concatenate([zero1, r[: NB - 1]], axis=0), r)

    def y_plus(v):
        r = pltpu.roll(v, LANES - 1, 2)
        return jnp.where(lane == LANES - 1, jnp.concatenate([r[1:], zero1], axis=0), r)

    def at(ref, x, z, shift=0):
        return ref[x, :, pl.ds(ROW0 + z * 8 + shift, 8), :]

    def raw(ref, x, z, shift=0):
        return ref[x, :, pl.ds(z * 8 + shift, 8), :]

    def to_out(ref, x, z, v):
        for y in range(NB):
            ref[x, pl.ds(z * 8, 8), y * LANES : (y + 1) * LANES] = v[y]

    def advect(xs, z):
        a, right, fx1, u1 = at(al, xs[0] + 1, z), None, None, None
        left, u0 = at(al, xs[0], z), raw(vx, xs[0], z)
        fx0 = u0 * jnp.where(u0 > 0, left, a)
        for x in xs:
            right, u1 = at(al, x + 2, z), raw(vx, x + 1, z)
            w0, w1 = raw(vz, x, z), raw(vz, x, z, 1)
            fx1 = u1 * jnp.where(u1 > 0, a, right)
            fz0 = w0 * jnp.where(w0 > 0, at(al, x + 1, z, -1), a)
            fz1 = w1 * jnp.where(w1 > 0, a, at(al, x + 1, z, 1))
            new = a - 0.2 * (fx1 - fx0 + fz1 - fz0)
            to_out(alpha_o, x, z, new)
            rho[x + 1, :, pl.ds(ROW0 + z * 8, 8), :] = 1.0 + 9.0 * new
            a, fx0 = right, fx1

    def first(xs, z):
        d = at(rho, xs[0] + 1, z)
        cm = recip(d + at(rho, xs[0], z))
        left, mid = at(p0, xs[0], z), at(p0, xs[0] + 1, z)
        for x in xs:
            beyond, right = at(rho, x + 2, z), at(p0, x + 2, z)
            cp = recip(d + beyond)
            zm, zp = recip(d + at(rho, x + 1, z, -1)), recip(d + at(rho, x + 1, z, 1))
            ym = recip(d + y_minus(d))
            yp = y_plus(ym)
            wall = jnp.where(lane[:1] == LANES - 1, recip(d[NB - 1 :]), yp[NB - 1 :])
            yp = jnp.concatenate([yp[: NB - 1], wall], axis=0)
            inv = recip((cm + cp) + (zm + zp) + (ym + yp))
            c = [v * inv for v in (cm, cp, zm, zp, ym, yp)]
            for ref, v in zip((axm, axp, azm, azp, aym, ayp), c):
                ref[x, :, pl.ds(z * 8, 8), :] = v
            half = 0.5 * inv
            r = raw(div, x, z) * half
            rr[x, :, pl.ds(z * 8, 8), :] = r
            div[x, :, pl.ds(z * 8, 8), :] = half
            p1[x + 1, :, pl.ds(ROW0 + z * 8, 8), :] = (
                (c[0] * left + c[1] * right)
                + (c[2] * at(p0, x + 1, z, -1) + c[3] * at(p0, x + 1, z, 1))
                + (c[4] * y_minus(mid) + c[5] * y_plus(mid) - r)
            )
            d, cm, left, mid = beyond, cp, mid, right

    def sweep(p, store, xs, z):
        left, mid = at(p, xs[0], z), at(p, xs[0] + 1, z)
        for x in xs:
            right = at(p, x + 2, z)
            store(
                x, z,
                (raw(axm, x, z) * left + raw(axp, x, z) * right)
                + (raw(azm, x, z) * at(p, x + 1, z, -1) + raw(azp, x, z) * at(p, x + 1, z, 1))
                + (raw(aym, x, z) * y_minus(mid) + raw(ayp, x, z) * y_plus(mid) - raw(rr, x, z)),
            )
            left, mid = mid, right

    def into(ref):
        def store(x, z, v):
            ref[x + 1, :, pl.ds(ROW0 + z * 8, 8), :] = v

        return store

    def sweep2(xs, z):
        sweep(p1, into(p2), xs, z)

    def sweep3(xs, z):
        sweep(p2, lambda x, z, v: to_out(press_o, x, z, v), xs, z)

    tiles = CZ // 8
    middle = tuple(range(1, CX - 1))

    def interior(fn, first, count):
        def step(i, c):
            fn(middle, first + i)
            return c

        lax.fori_loop(0, count, step, 0)

    def edges(fn):
        def step(i, c):
            fn(middle, i * (tiles - 1))
            return c

        lax.fori_loop(0, 2, step, 0)

    def ends(fn):
        def step(i, c):
            for k in range(4):
                fn((0,), i * 4 + k)
                fn((CX - 1,), i * 4 + k)
            return c

        lax.fori_loop(0, tiles // 4, step, 0)

    inside, early = tiles - 2, 5

    def recv(copies):
        for c in copies:
            c.wait_recv()

    interior(advect, 1, inside)
    def a1_wait(k, c):
        src = (a_me + GA - k) % GA
        rcopy(s1.at[src], r1.at[src], a1s.at[k], a1r.at[k], a_peer(k)[1]).wait_recv()
        return c

    lax.fori_loop(1, GA, a1_wait, 0)
    got = dot(perm_s[...], r1[:, 0:REC_A, :].reshape(SLOTS, LANES)).astype(BF16)
    mrow = iota((META, LANES), 0)
    m1 = jnp.zeros((META, LANES), F32)
    for a in range(GA):
        m1 = jnp.where(mrow == a, r1[a, REC_A:, :].astype(F32), m1)
    m1 = m1.astype(BF16)
    for b in range(GB):
        s2[b, 0:REC_B, :] = got[b * REC_B : (b + 1) * REC_B]
        s2[b, REC_B:, :] = m1

    def b1_start(k, c):
        b, dev = b_peer(k)
        rcopy(s2.at[b], r2.at[b_me], b1s.at[k], b1r.at[k], dev).start()
        return c

    lax.fori_loop(1, GB, b1_start, 0)
    r2[b_me] = s2[b_me]

    recv(ez_al + ez_vz)
    fill_z([(0, al, 1, ROW0 - 1, 0), (1, al, 1, ROW0 + CZ, DEPTHS - 1), (2, vz, 0, CZ, DEPTHS - 1)])
    edges(advect)

    recv(e_al + e_vx)
    fill_x(0, al)
    vx[CX] = jnp.where(slab == SLABS - 1, 0.0, xr[2].astype(F32))
    ends(advect)
    pack_x(5, rho)
    e_rho, ez_rho = xpair(5), zpair(5)
    start(e_rho)
    pack_z([(5, rho, 1, ROW0 + CZ - 1), (6, rho, 1, ROW0)])
    start(ez_rho)

    loaded("div")
    interior(first, 1, inside)
    recv(ez_p0 + ez_rho)
    fill_z([
        (3, p0, 1, ROW0 - 1, 0), (4, p0, 1, ROW0 + CZ, DEPTHS - 1),
        (5, rho, 1, ROW0 - 1, 0), (6, rho, 1, ROW0 + CZ, DEPTHS - 1),
    ])
    edges(first)

    def b1_wait(k, c):
        src = (b_me + GB - k) % GB
        rcopy(s2.at[src], r2.at[src], b1s.at[k], b1r.at[k], b_peer(k)[1]).wait_recv()
        return c

    lax.fori_loop(1, GB, b1_wait, 0)

    m2 = r2[:, REC_B:, :].reshape(GB * META, LANES)
    srow, scol = iota((SLOTS, GB * META), 0), iota((SLOTS, GB * META), 1)
    wide = dot(onehot(scol == (srow >> 5) * META + ((srow >> 2) & (GA - 1))), m2)
    pick = iota((SLOTS, LANES), 1) - (iota((SLOTS, LANES), 0) & 3) - b_me * CAP
    own_meta = jnp.where((pick == 0) | (pick == REC_A), wide, 0.0).astype(BF16)
    weight_c = jnp.where(iota((LANES, LANES), 0) < REC_A, 64.0, 1.0).astype(BF16)
    weight_r = jnp.where(iota((META, LANES), 1) < REC_A, 64.0, 1.0).astype(BF16)
    seg_c = dot(own_meta, weight_c).astype(I32)
    seg_r = lax.dot_general(
        weight_r, own_meta, (((1,), (1,)), ((), ())), preferred_element_type=F32
    )[0:1].astype(I32)
    block_c, key_f = seg_c & 3, (seg_c >> 2).astype(F32)
    key_r = (seg_r >> 2).astype(F32)
    recs = r2[:, 0:REC_B, :].reshape(SLOTS, LANES)
    for y in range(NB):
        rmat[:, y * LANES : (y + 1) * LANES] = jnp.where(
            block_c == y, recs.astype(F32), 0.0
        ).astype(BF16)

    def hull(planes):
        z = iota((CZ, SLOTS), 0)
        cells = jnp.concatenate([z + x * CZ for x in planes], axis=0).astype(F32)
        h = dot(onehot(cells == key_r), rmat[...])
        for k, x in enumerate(planes):
            for y in range(NB):
                part = h[k * CZ : (k + 1) * CZ, y * LANES : (y + 1) * LANES] * div[x, y]
                rr[x, y] += part
                p1[x + 1, y, ROW0 : ROW0 + CZ, :] -= part

    recv(e_p0 + e_rho)
    fill_x(3, p0)
    fill_x(5, rho)
    ends(first)
    hull((0, CX - 1))
    pack_x(7, p1)
    e_p1, ez_p1 = xpair(7), zpair(7)
    start(e_p1)
    for i in range(1, CX - 1, 7):
        hull(tuple(range(i, i + 7)))
    pack_z([(7, p1, 1, ROW0 + CZ - 1), (8, p1, 1, ROW0)])
    start(ez_p1)
    tail = (CX - 2) * CZ
    column = iota((SLOTS, LANES), 1)
    for c in range(tail // LANES):
        g_s[:, c * LANES : (c + 1) * LANES] = onehot(
            key_f == (column + (c * LANES + CZ)).astype(F32)
        )
    outer = jnp.where(column < CZ, column, column + tail)
    g_s[:, tail:] = onehot(key_f == outer.astype(F32))
    interior(sweep2, 1, early)
    recv(ez_p1)
    fill_z([(7, p1, 1, ROW0 - 1, 0), (8, p1, 1, ROW0 + CZ, DEPTHS - 1)])
    recv(e_p1)
    fill_x(7, p1)
    ends(sweep2)
    pack_x(9, p2)
    e_p2, ez_p2 = xpair(9), zpair(9)
    start(e_p2)
    edges(sweep2)
    pack_z([(9, p2, 1, ROW0 + CZ - 1), (10, p2, 1, ROW0)])
    start(ez_p2)
    interior(sweep2, 1 + early, inside - early)
    interior(sweep3, 1, inside)
    recv(ez_p2)
    fill_z([(9, p2, 1, ROW0 - 1, 0), (10, p2, 1, ROW0 + CZ, DEPTHS - 1)])
    edges(sweep3)
    for x in range(1, CX - 1):
        pb[(x - 1) * CZ : x * CZ, :] = press_o[x].astype(BF16)
    acc[...] = dot(g_s[:, 0:tail], pb[0:tail, :])
    recv(e_p2)
    fill_x(9, p2)
    ends(sweep3)

    pb[tail : tail + CZ, :] = press_o[0].astype(BF16)
    pb[tail + CZ :, :] = press_o[CX - 1].astype(BF16)
    wet = acc[...] + dot(g_s[:, tail:], pb[tail:, :])
    back = jnp.zeros((SLOTS, LANES), F32)
    for y in range(NB):
        back = jnp.where(block_c == y, wet[:, y * LANES : (y + 1) * LANES], back)
    back = back.astype(BF16).astype(F32)
    wb[...] = back.reshape(GA * GB, CAP, LANES)

    far = (2, 1, 3, 0)
    for dz in far:
        for dx in far:
            b = (b_me // 4 + dz) % 4 * 4 + (b_me % 4 + dx) % 4

            def home(k, c, b=b):
                a = (a_me + k) % GA
                d = b * GA + a
                dev = (b * 2 + a // DEPTHS, a % DEPTHS)
                rcopy(wb.at[d], tb.at[me], home_s, home_r, dev).start()
                return c

            lax.fori_loop(1 if dz == dx == 0 else 0, GA, home, 0)
    others = pl.ds(0, GA * GB - 1)
    tb[me] = wb[me]
    pltpu.make_async_copy(wb.at[others], tb.at[others], home_r).wait()
    panel_o[...] = dot(q_s[...], tb[...].reshape(SLOTS, LANES).astype(BF16)).astype(BF16)
    pltpu.make_async_copy(wb.at[others], tb.at[others], home_s).wait()

    for c in sends:
        c.wait_send()

    def b_done(k, c):
        b, dev = b_peer(k)
        rcopy(s2.at[b], r2.at[b_me], b1s.at[k], b1r.at[k], dev).wait_send()
        return c

    def a_done(k, c):
        a, dev = a_peer(k)
        rcopy(s1.at[a], r1.at[a_me], a1s.at[k], a1r.at[k], dev).wait_send()
        return c

    lax.fori_loop(1, GB, b_done, 0)
    lax.fori_loop(1, GA, a_done, 0)


def deliver(press, alpha, panel, press_o, alpha_o, panel_o, sem):
    pairs = ((press, press_o), (alpha, alpha_o), (panel, panel_o))
    copies = [pltpu.make_async_copy(s, d, sem.at[i]) for i, (s, d) in enumerate(pairs)]
    for c in copies:
        c.start()
    for c in copies:
        c.wait()


def body(alpha, vel_x, vel_z, divergence, press_guess, panel_records, panel_dest, panel_segment):
    padded = pltpu.VMEM((CX + 2, NB, PADZ, LANES), F32)
    plain = pltpu.VMEM((CX, NB, CZ, LANES), F32)
    hbm = pl.BlockSpec(memory_space=pltpu.HBM)
    vmem = pl.BlockSpec(memory_space=pltpu.VMEM)
    dma = lambda n: pltpu.SemaphoreType.DMA((n,))
    field = pltpu.VMEM((CX, CZ, BEAM), F32)
    outs = pl.pallas_call(
        kernel,
        out_shape=(field, field, pltpu.VMEM((PAN, LANES), BF16)),
        in_specs=[hbm] * 8,
        out_specs=(vmem, vmem, vmem),
        scratch_shapes=[
            pltpu.VMEM((3, CZ, BEAM), F32),
            pltpu.VMEM((PAN, LANES), BF16), pltpu.VMEM((1, PAN), I32), pltpu.VMEM((1, PAN), I32),
            padded,
            pltpu.VMEM((CX + 1, NB, CZ, LANES), F32),
            pltpu.VMEM((CX, NB, CZ + 8, LANES), F32),
            plain,
            padded, padded, padded, padded,
            plain, plain, plain, plain, plain, plain, plain,
            pltpu.VMEM((11, CX, NB, LANES), F32),
            pltpu.VMEM((11, CX, NB, LANES), F32),
            pltpu.VMEM((11, NB, CZ, LANES), BF16),
            pltpu.VMEM((11, NB, CZ, LANES), BF16),
            pltpu.VMEM((SLOTS, BEAM), F32),
            pltpu.VMEM((GA, REC_A + META, LANES), BF16),
            pltpu.VMEM((GA, REC_A + META, LANES), BF16),
            pltpu.VMEM((GB, REC_B + META, LANES), BF16),
            pltpu.VMEM((GB, REC_B + META, LANES), BF16),
            pltpu.VMEM((GA * GB, CAP, LANES), F32),
            pltpu.VMEM((GA * GB, CAP, LANES), F32),
            pltpu.VMEM((PAN, SLOTS), BF16),
            pltpu.VMEM((SLOTS, CX * CZ), BF16),
            pltpu.VMEM((SLOTS, SLOTS), BF16),
            pltpu.VMEM((SLOTS, BEAM), BF16),
            pltpu.VMEM((CX * CZ, BEAM), BF16),
            dma(26), dma(11), dma(11), dma(11), dma(11),
            dma(GB), dma(GB), dma(GA), dma(GA), pltpu.SemaphoreType.DMA, pltpu.SemaphoreType.DMA,
        ],
        compiler_params=pltpu.CompilerParams(
            collective_id=0, has_side_effects=True, vmem_limit_bytes=50 * 1024 * 1024
        ),
    )(
        alpha, vel_x, vel_z, divergence, press_guess, panel_records,
        panel_dest.reshape(1, PAN), panel_segment.reshape(1, PAN),
    )
    outs = [pltpu.with_memory_space_constraint(o, pltpu.VMEM) for o in outs]
    return pl.pallas_call(
        deliver,
        out_shape=tuple(jax.ShapeDtypeStruct(o.shape, o.dtype) for o in outs),
        in_specs=[pl.BlockSpec(memory_space=pl.ANY)] * 3,
        out_specs=(hbm,) * 3,
        scratch_shapes=[dma(3)],
        compiler_params=pltpu.CompilerParams(vmem_limit_bytes=1024 * 1024),
    )(*outs)


def solution(mesh):
    field = P("slab", "depth", None)
    rows = P(("slab", "depth"), None)
    return jax.shard_map(
        body, mesh=mesh, in_specs=(field,) * 5 + (rows,) * 3,
        out_specs=(field, field, rows), check_vma=False,
    )
```

```python
import jax
import jax.numpy as jnp
from jax import lax
from jax.experimental import pallas as pl
from jax.experimental.pallas import tpu as pltpu
from jax.sharding import PartitionSpec as P

MESH = pl.DeviceIdType.MESH
F32, BF16, I32 = jnp.float32, jnp.bfloat16, jnp.int32
CX, CZ, BEAM, LANES = 16, 64, 512, 128
NB = BEAM // LANES
ROW0 = 8
PADZ = CZ + 16
SLABS, DEPTHS = 32, 4
GA, GB = 8, 16
CAP = 4
SLOTS = GA * GB * CAP
PAN = 256
REC_B, REC_A = GA * CAP, GB * CAP
META = 16


def iota(shape, dim):
    return lax.broadcasted_iota(I32, shape, dim)


def onehot(cond):
    return jnp.where(cond, 1.0, 0.0).astype(BF16)


def dot(a, b):
    return jnp.dot(a, b, preferred_element_type=F32)


def recip(d):
    r = pl.reciprocal(d, approx=True)
    return r * (2.0 - d * r)


def kernel(
    alpha_h, velx_h, velz_h, div_h, press_h, rec_h, dest_h, seg_h,
    press_o, alpha_o, panel_o,
    stage, rec_ref, dest_ref, seg_ref, al, vx, vz, div, rho, p0, p1, p2,
    axm, axp, azm, azp, aym, ayp, rr,
    zs, zr, xb, xr, acc,
    s1, r1, s2, r2, wb, tb,
    q_s, g_s, perm_s, spread, rmat, pb,
    load_sem, xs_sem, xr_sem, zs_sem, zr_sem,
    b1s, b1r, a1s, a1r, home_s, home_r,
):
    slab = lax.axis_index("slab")
    depth = lax.axis_index("depth")
    up_s, dn_s = (slab + 1) % SLABS, (slab + SLABS - 1) % SLABS
    up_d, dn_d = (depth + 1) % DEPTHS, (depth + DEPTHS - 1) % DEPTHS
    x_up, x_dn = (up_s, depth), (dn_s, depth)
    z_up, z_dn = (slab, up_d), (slab, dn_d)
    b_me, core = slab // 2, slab % 2
    a_me = core * DEPTHS + depth
    me = slab * DEPTHS + depth

    def b_peer(k):
        b = (b_me + k) % GB
        return b, (b * 2 + core, depth)

    def a_peer(k):
        a = (a_me + k) % GA
        return a, (b_me * 2 + a // DEPTHS, a % DEPTHS)

    loads = {}
    sem_i = 0

    def load(name, pairs):
        nonlocal sem_i
        loads[name] = []
        for src, dst in pairs:
            c = pltpu.make_async_copy(src, dst, load_sem.at[sem_i])
            c.start()
            sem_i += 1
            loads[name].append(c)

    def loaded(name):
        for c in loads[name]:
            c.wait()

    def field(src, dst):
        return [(src.at[:, :, pl.ds(y * LANES, LANES)], dst(y)) for y in range(NB)]

    load("panels", [(dest_h, dest_ref), (seg_h, seg_ref), (rec_h, rec_ref)])
    load("planes", [
        (alpha_h.at[CX - 1], stage.at[0]), (alpha_h.at[0], stage.at[1]), (velx_h.at[0], stage.at[2]),
    ])
    load("al", field(alpha_h, lambda y: al.at[pl.ds(1, CX), y, pl.ds(ROW0, CZ), :]))
    load("vz", field(velz_h, lambda y: vz.at[:, y, pl.ds(0, CZ), :]))
    load("vx", field(velx_h, lambda y: vx.at[pl.ds(0, CX), y, :, :]))
    load("p0", field(press_h, lambda y: p0.at[pl.ds(1, CX), y, pl.ds(ROW0, CZ), :]))
    load("div", field(div_h, lambda y: div.at[:, y, :, :]))

    barrier = pltpu.get_barrier_semaphore()
    for dev in (x_up, x_dn, z_up, z_dn):
        pl.semaphore_signal(barrier, inc=1, device_id=dev, device_id_type=MESH)

    def sig_b(k, c):
        pl.semaphore_signal(barrier, inc=1, device_id=b_peer(k)[1], device_id_type=MESH)
        return c

    def sig_a(k, c):
        pl.semaphore_signal(barrier, inc=1, device_id=a_peer(k)[1], device_id_type=MESH)
        return c

    lax.fori_loop(1, GB, sig_b, 0)
    lax.fori_loop(1, GA, sig_a, 0)

    def rcopy(src, dst, ss, rs, dev):
        return pltpu.make_async_remote_copy(
            src_ref=src, dst_ref=dst, send_sem=ss, recv_sem=rs,
            device_id=dev, device_id_type=MESH,
        )

    def xcopy(i, dev):
        return rcopy(xb.at[i], xr.at[i], xs_sem.at[i], xr_sem.at[i], dev)

    def zcopy(i, dev):
        return rcopy(zs.at[i], zr.at[i], zs_sem.at[i], zr_sem.at[i], dev)

    def xpair(i):
        return [xcopy(i, x_up), xcopy(i + 1, x_dn)]

    def pack_x(i, ref):
        xb[i] = ref[CX, :, ROW0 : ROW0 + CZ, :].astype(BF16)
        xb[i + 1] = ref[1, :, ROW0 : ROW0 + CZ, :].astype(BF16)

    def fill_x(i, ref):
        low, high = xr[i].astype(F32), xr[i + 1].astype(F32)
        ref[0, :, ROW0 : ROW0 + CZ, :] = jnp.where(slab == 0, 0.0, low)
        ref[CX + 1, :, ROW0 : ROW0 + CZ, :] = jnp.where(slab == SLABS - 1, 0.0, high)

    def zpair(i):
        return [zcopy(i, z_up), zcopy(i + 1, z_dn)]

    def pack_z(items):
        def step(g, c):
            for k in range(4):
                x = g * 4 + k
                for i, ref, xo, r in items:
                    zs[i, x] = ref[x + xo, :, r, :]
            return c

        lax.fori_loop(0, CX // 4, step, 0)

    def fill_z(items):
        def step(g, c):
            for k in range(4):
                x = g * 4 + k
                for i, ref, xo, r, edge in items:
                    ref[x + xo, :, r, :] = jnp.where(depth == edge, 0.0, zr[i, x])
            return c

        lax.fori_loop(0, CX // 4, step, 0)

    sends = []

    def start(copies):
        for c in copies:
            c.start()
        sends.extend(copies)

    loaded("panels")
    dest, seg = dest_ref[...], seg_ref[...]
    own = onehot(iota((GA * GB, PAN), 0) == dest)
    before = dot(own, onehot(iota((PAN, PAN), 0) < iota((PAN, PAN), 1)))
    slot = jnp.sum(own.astype(F32) * before, axis=0, keepdims=True)
    lane_of = (dest >> 3) * CAP + slot.astype(I32)
    place = (dest & (GA - 1)) * REC_A + lane_of
    packed = dot(onehot(iota((SLOTS, PAN), 0) == place), rec_ref[...]).astype(BF16)
    row = iota((LANES, PAN), 0)
    hi, lo = (seg >> 6).astype(F32), (seg & 63).astype(F32)
    bt = jnp.where(row == lane_of, hi, 0.0) + jnp.where(row == lane_of + REC_A, lo, 0.0)
    meta = lax.dot_general(
        onehot(iota((16, PAN), 0) == (dest & (GA - 1))), bt.astype(BF16),
        (((1,), (1,)), ((), ())), preferred_element_type=F32,
    )
    for a in range(GA):
        s1[a, 0:REC_A, :] = packed[a * REC_A : (a + 1) * REC_A]
        s1[a, REC_A:, :] = jnp.broadcast_to(meta[a : a + 1], (META, LANES)).astype(BF16)

    pl.semaphore_wait(barrier, 4 + (GB - 1) + (GA - 1))

    def a1_start(k, c):
        a, dev = a_peer(k)
        rcopy(s1.at[a], r1.at[a_me], a1s.at[k], a1r.at[k], dev).start()
        return c

    lax.fori_loop(1, GA, a1_start, 0)
    loaded("planes")
    for i in range(3):
        for y in range(NB):
            xb[i, y] = stage[i, :, y * LANES : (y + 1) * LANES].astype(BF16)
    e_al, e_vx = xpair(0), [xcopy(2, x_dn)]
    start(e_al + e_vx)

    r1[a_me] = s1[a_me]

    loaded("al")
    loaded("vz")
    pack_z([(0, al, 1, ROW0 + CZ - 1), (1, al, 1, ROW0), (2, vz, 0, 0)])
    ez_al, ez_vz = zpair(0), [zcopy(2, z_dn)]
    start(ez_al + ez_vz)
    loaded("vx")
    loaded("p0")
    pack_x(3, p0)
    pack_z([(3, p0, 1, ROW0 + CZ - 1), (4, p0, 1, ROW0)])
    e_p0, ez_p0 = xpair(3), zpair(3)
    start(e_p0 + ez_p0)

    answer = dest * CAP + slot.astype(I32)
    place_t = jnp.broadcast_to(answer.astype(F32), (LANES, PAN)).T
    for c in range(SLOTS // LANES):
        q_s[:, c * LANES : (c + 1) * LANES] = onehot(
            place_t == (iota((PAN, LANES), 1) + c * LANES).astype(F32)
        )
    pr, pc = iota((SLOTS, SLOTS), 0), iota((SLOTS, SLOTS), 1)
    perm_s[...] = onehot(
        pc == (((pr >> 2) & (GA - 1)) * REC_A + (pr >> 5) * CAP + (pr & 3))
    )

    lane = iota((NB, 8, LANES), 2)
    zero1 = jnp.zeros((1, 8, LANES), F32)

    def y_minus(v):
        r = pltpu.roll(v, 1, 2)
        return jnp.where(lane == 0, jnp.concatenate([zero1, r[: NB - 1]], axis=0), r)

    def y_plus(v):
        r = pltpu.roll(v, LANES - 1, 2)
        return jnp.where(lane == LANES - 1, jnp.concatenate([r[1:], zero1], axis=0), r)

    def at(ref, x, z, shift=0):
        return ref[x, :, pl.ds(ROW0 + z * 8 + shift, 8), :]

    def raw(ref, x, z, shift=0):
        return ref[x, :, pl.ds(z * 8 + shift, 8), :]

    def to_out(ref, x, z, v):
        for y in range(NB):
            ref[x, pl.ds(z * 8, 8), y * LANES : (y + 1) * LANES] = v[y]

    def advect(xs, z):
        a, right, fx1, u1 = at(al, xs[0] + 1, z), None, None, None
        left, u0 = at(al, xs[0], z), raw(vx, xs[0], z)
        fx0 = u0 * jnp.where(u0 > 0, left, a)
        for x in xs:
            right, u1 = at(al, x + 2, z), raw(vx, x + 1, z)
            w0, w1 = raw(vz, x, z), raw(vz, x, z, 1)
            fx1 = u1 * jnp.where(u1 > 0, a, right)
            fz0 = w0 * jnp.where(w0 > 0, at(al, x + 1, z, -1), a)
            fz1 = w1 * jnp.where(w1 > 0, a, at(al, x + 1, z, 1))
            new = a - 0.2 * (fx1 - fx0 + fz1 - fz0)
            to_out(alpha_o, x, z, new)
            rho[x + 1, :, pl.ds(ROW0 + z * 8, 8), :] = 1.0 + 9.0 * new
            a, fx0 = right, fx1

    def first(xs, z):
        d = at(rho, xs[0] + 1, z)
        cm = recip(d + at(rho, xs[0], z))
        left, mid = at(p0, xs[0], z), at(p0, xs[0] + 1, z)
        for x in xs:
            beyond, right = at(rho, x + 2, z), at(p0, x + 2, z)
            cp = recip(d + beyond)
            zm, zp = recip(d + at(rho, x + 1, z, -1)), recip(d + at(rho, x + 1, z, 1))
            ym = recip(d + y_minus(d))
            yp = y_plus(ym)
            wall = jnp.where(lane[:1] == LANES - 1, recip(d[NB - 1 :]), yp[NB - 1 :])
            yp = jnp.concatenate([yp[: NB - 1], wall], axis=0)
            inv = recip((cm + cp) + (zm + zp) + (ym + yp))
            c = [v * inv for v in (cm, cp, zm, zp, ym, yp)]
            for ref, v in zip((axm, axp, azm, azp, aym, ayp), c):
                ref[x, :, pl.ds(z * 8, 8), :] = v
            half = 0.5 * inv
            r = raw(div, x, z) * half
            rr[x, :, pl.ds(z * 8, 8), :] = r
            div[x, :, pl.ds(z * 8, 8), :] = half
            p1[x + 1, :, pl.ds(ROW0 + z * 8, 8), :] = (
                (c[0] * left + c[1] * right)
                + (c[2] * at(p0, x + 1, z, -1) + c[3] * at(p0, x + 1, z, 1))
                + (c[4] * y_minus(mid) + c[5] * y_plus(mid) - r)
            )
            d, cm, left, mid = beyond, cp, mid, right

    def sweep(p, store, xs, z):
        left, mid = at(p, xs[0], z), at(p, xs[0] + 1, z)
        for x in xs:
            right = at(p, x + 2, z)
            store(
                x, z,
                (raw(axm, x, z) * left + raw(axp, x, z) * right)
                + (raw(azm, x, z) * at(p, x + 1, z, -1) + raw(azp, x, z) * at(p, x + 1, z, 1))
                + (raw(aym, x, z) * y_minus(mid) + raw(ayp, x, z) * y_plus(mid) - raw(rr, x, z)),
            )
            left, mid = mid, right

    def into(ref):
        def store(x, z, v):
            ref[x + 1, :, pl.ds(ROW0 + z * 8, 8), :] = v

        return store

    def sweep2(xs, z):
        sweep(p1, into(p2), xs, z)

    def sweep3(xs, z):
        sweep(p2, lambda x, z, v: to_out(press_o, x, z, v), xs, z)

    tiles = CZ // 8
    middle = tuple(range(1, CX - 1))

    def interior(fn, first, count):
        def step(i, c):
            fn(middle, first + i)
            return c

        lax.fori_loop(0, count, step, 0)

    def edges(fn):
        def step(i, c):
            fn(middle, i * (tiles - 1))
            return c

        lax.fori_loop(0, 2, step, 0)

    def ends(fn):
        def step(i, c):
            for k in range(4):
                fn((0,), i * 4 + k)
                fn((CX - 1,), i * 4 + k)
            return c

        lax.fori_loop(0, tiles // 4, step, 0)

    inside, early = tiles - 2, 5

    def recv(copies):
        for c in copies:
            c.wait_recv()

    interior(advect, 1, inside)
    def a1_wait(k, c):
        src = (a_me + GA - k) % GA
        rcopy(s1.at[src], r1.at[src], a1s.at[k], a1r.at[k], a_peer(k)[1]).wait_recv()
        return c

    lax.fori_loop(1, GA, a1_wait, 0)
    got = dot(perm_s[...], r1[:, 0:REC_A, :].reshape(SLOTS, LANES)).astype(BF16)
    mrow = iota((META, LANES), 0)
    m1 = jnp.zeros((META, LANES), F32)
    for a in range(GA):
        m1 = jnp.where(mrow == a, r1[a, REC_A:, :].astype(F32), m1)
    m1 = m1.astype(BF16)
    for b in range(GB):
        s2[b, 0:REC_B, :] = got[b * REC_B : (b + 1) * REC_B]
        s2[b, REC_B:, :] = m1

    def b1_start(k, c):
        b, dev = b_peer(k)
        rcopy(s2.at[b], r2.at[b_me], b1s.at[k], b1r.at[k], dev).start()
        return c

    for first_k, last_k in ((5, 12), (1, 5), (12, GB)):
        lax.fori_loop(first_k, last_k, b1_start, 0)
    r2[b_me] = s2[b_me]

    recv(ez_al + ez_vz)
    fill_z([(0, al, 1, ROW0 - 1, 0), (1, al, 1, ROW0 + CZ, DEPTHS - 1), (2, vz, 0, CZ, DEPTHS - 1)])
    edges(advect)

    recv(e_al + e_vx)
    fill_x(0, al)
    vx[CX] = jnp.where(slab == SLABS - 1, 0.0, xr[2].astype(F32))
    ends(advect)
    pack_x(5, rho)
    e_rho, ez_rho = xpair(5), zpair(5)
    start(e_rho)
    pack_z([(5, rho, 1, ROW0 + CZ - 1), (6, rho, 1, ROW0)])
    start(ez_rho)

    srow, scol = iota((SLOTS, GB * META), 0), iota((SLOTS, GB * META), 1)
    spread[...] = onehot(scol == (srow >> 5) * META + ((srow >> 2) & (GA - 1)))
    loaded("div")
    interior(first, 1, inside)
    recv(ez_p0 + ez_rho)
    fill_z([
        (3, p0, 1, ROW0 - 1, 0), (4, p0, 1, ROW0 + CZ, DEPTHS - 1),
        (5, rho, 1, ROW0 - 1, 0), (6, rho, 1, ROW0 + CZ, DEPTHS - 1),
    ])
    edges(first)
    recv(e_p0 + e_rho)
    fill_x(3, p0)
    fill_x(5, rho)
    ends(first)

    def b1_wait(k, c):
        src = (b_me + GB - k) % GB
        rcopy(s2.at[src], r2.at[src], b1s.at[k], b1r.at[k], b_peer(k)[1]).wait_recv()
        return c

    lax.fori_loop(1, GB, b1_wait, 0)

    m2 = r2[:, REC_B:, :].reshape(GB * META, LANES)
    wide = dot(spread[...], m2)
    pick = iota((SLOTS, LANES), 1) - (iota((SLOTS, LANES), 0) & 3) - b_me * CAP
    own_meta = jnp.where((pick == 0) | (pick == REC_A), wide, 0.0).astype(BF16)
    weight_c = jnp.where(iota((LANES, LANES), 0) < REC_A, 64.0, 1.0).astype(BF16)
    weight_r = jnp.where(iota((META, LANES), 1) < REC_A, 64.0, 1.0).astype(BF16)
    seg_c = dot(own_meta, weight_c).astype(I32)
    seg_r = lax.dot_general(
        weight_r, own_meta, (((1,), (1,)), ((), ())), preferred_element_type=F32
    )[0:1].astype(I32)
    block_c, key_f = seg_c & 3, (seg_c >> 2).astype(F32)
    key_r = (seg_r >> 2).astype(F32)
    recs = r2[:, 0:REC_B, :].reshape(SLOTS, LANES)
    for y in range(NB):
        rmat[:, y * LANES : (y + 1) * LANES] = jnp.where(
            block_c == y, recs.astype(F32), 0.0
        ).astype(BF16)

    def hull(planes):
        z = iota((CZ, SLOTS), 0)
        cells = jnp.concatenate([z + x * CZ for x in planes], axis=0).astype(F32)
        h = dot(onehot(cells == key_r), rmat[...])
        for k, x in enumerate(planes):
            for y in range(NB):
                part = h[k * CZ : (k + 1) * CZ, y * LANES : (y + 1) * LANES] * div[x, y]
                rr[x, y] += part
                p1[x + 1, y, ROW0 : ROW0 + CZ, :] -= part

    hull((0, CX - 1))
    pack_x(7, p1)
    e_p1, ez_p1 = xpair(7), zpair(7)
    start(e_p1)
    for i in range(1, CX - 1, 7):
        hull(tuple(range(i, i + 7)))
    pack_z([(7, p1, 1, ROW0 + CZ - 1), (8, p1, 1, ROW0)])
    start(ez_p1)
    tail = (CX - 2) * CZ
    column = iota((SLOTS, LANES), 1)
    for c in range(tail // LANES):
        g_s[:, c * LANES : (c + 1) * LANES] = onehot(
            key_f == (column + (c * LANES + CZ)).astype(F32)
        )
    outer = jnp.where(column < CZ, column, column + tail)
    g_s[:, tail:] = onehot(key_f == outer.astype(F32))
    interior(sweep2, 1, early)
    recv(ez_p1)
    fill_z([(7, p1, 1, ROW0 - 1, 0), (8, p1, 1, ROW0 + CZ, DEPTHS - 1)])
    recv(e_p1)
    fill_x(7, p1)
    ends(sweep2)
    pack_x(9, p2)
    e_p2, ez_p2 = xpair(9), zpair(9)
    start(e_p2)
    edges(sweep2)
    pack_z([(9, p2, 1, ROW0 + CZ - 1), (10, p2, 1, ROW0)])
    start(ez_p2)
    interior(sweep2, 1 + early, inside - early)
    interior(sweep3, 1, inside)
    recv(ez_p2)
    fill_z([(9, p2, 1, ROW0 - 1, 0), (10, p2, 1, ROW0 + CZ, DEPTHS - 1)])
    edges(sweep3)
    for x in range(1, CX - 1):
        pb[(x - 1) * CZ : x * CZ, :] = press_o[x].astype(BF16)
    acc[...] = dot(g_s[:, 0:tail], pb[0:tail, :])
    recv(e_p2)
    fill_x(9, p2)
    ends(sweep3)

    pb[tail : tail + CZ, :] = press_o[0].astype(BF16)
    pb[tail + CZ :, :] = press_o[CX - 1].astype(BF16)
    wet = acc[...] + dot(g_s[:, tail:], pb[tail:, :])
    back = jnp.zeros((SLOTS, LANES), F32)
    for y in range(NB):
        back = jnp.where(block_c == y, wet[:, y * LANES : (y + 1) * LANES], back)
    back = back.astype(BF16).astype(F32)
    wb[...] = back.reshape(GA * GB, CAP, LANES)

    far = (2, 1, 3, 0)
    for dz in far:
        for dx in far:
            b = (b_me // 4 + dz) % 4 * 4 + (b_me % 4 + dx) % 4

            def home(k, c, b=b):
                a = (a_me + k) % GA
                d = b * GA + a
                dev = (b * 2 + a // DEPTHS, a % DEPTHS)
                rcopy(wb.at[d], tb.at[me], home_s, home_r, dev).start()
                return c

            lax.fori_loop(1 if dz == dx == 0 else 0, GA, home, 0)
    others = pl.ds(0, GA * GB - 1)
    tb[me] = wb[me]
    pltpu.make_async_copy(wb.at[others], tb.at[others], home_r).wait()
    panel_o[...] = dot(q_s[...], tb[...].reshape(SLOTS, LANES).astype(BF16)).astype(BF16)
    pltpu.make_async_copy(wb.at[others], tb.at[others], home_s).wait()

    for c in sends:
        c.wait_send()

    def b_done(k, c):
        b, dev = b_peer(k)
        rcopy(s2.at[b], r2.at[b_me], b1s.at[k], b1r.at[k], dev).wait_send()
        return c

    def a_done(k, c):
        a, dev = a_peer(k)
        rcopy(s1.at[a], r1.at[a_me], a1s.at[k], a1r.at[k], dev).wait_send()
        return c

    lax.fori_loop(1, GB, b_done, 0)
    lax.fori_loop(1, GA, a_done, 0)


def deliver(press, alpha, panel, press_o, alpha_o, panel_o, sem):
    pairs = ((press, press_o), (alpha, alpha_o), (panel, panel_o))
    copies = [pltpu.make_async_copy(s, d, sem.at[i]) for i, (s, d) in enumerate(pairs)]
    for c in copies:
        c.start()
    for c in copies:
        c.wait()


def body(alpha, vel_x, vel_z, divergence, press_guess, panel_records, panel_dest, panel_segment):
    padded = pltpu.VMEM((CX + 2, NB, PADZ, LANES), F32)
    plain = pltpu.VMEM((CX, NB, CZ, LANES), F32)
    hbm = pl.BlockSpec(memory_space=pltpu.HBM)
    vmem = pl.BlockSpec(memory_space=pltpu.VMEM)
    dma = lambda n: pltpu.SemaphoreType.DMA((n,))
    field = pltpu.VMEM((CX, CZ, BEAM), F32)
    outs = pl.pallas_call(
        kernel,
        out_shape=(field, field, pltpu.VMEM((PAN, LANES), BF16)),
        in_specs=[hbm] * 8,
        out_specs=(vmem, vmem, vmem),
        scratch_shapes=[
            pltpu.VMEM((3, CZ, BEAM), F32),
            pltpu.VMEM((PAN, LANES), BF16), pltpu.VMEM((1, PAN), I32), pltpu.VMEM((1, PAN), I32),
            padded,
            pltpu.VMEM((CX + 1, NB, CZ, LANES), F32),
            pltpu.VMEM((CX, NB, CZ + 8, LANES), F32),
            plain,
            padded, padded, padded, padded,
            plain, plain, plain, plain, plain, plain, plain,
            pltpu.VMEM((11, CX, NB, LANES), F32),
            pltpu.VMEM((11, CX, NB, LANES), F32),
            pltpu.VMEM((11, NB, CZ, LANES), BF16),
            pltpu.VMEM((11, NB, CZ, LANES), BF16),
            pltpu.VMEM((SLOTS, BEAM), F32),
            pltpu.VMEM((GA, REC_A + META, LANES), BF16),
            pltpu.VMEM((GA, REC_A + META, LANES), BF16),
            pltpu.VMEM((GB, REC_B + META, LANES), BF16),
            pltpu.VMEM((GB, REC_B + META, LANES), BF16),
            pltpu.VMEM((GA * GB, CAP, LANES), F32),
            pltpu.VMEM((GA * GB, CAP, LANES), F32),
            pltpu.VMEM((PAN, SLOTS), BF16),
            pltpu.VMEM((SLOTS, CX * CZ), BF16),
            pltpu.VMEM((SLOTS, SLOTS), BF16),
            pltpu.VMEM((SLOTS, GB * META), BF16),
            pltpu.VMEM((SLOTS, BEAM), BF16),
            pltpu.VMEM((CX * CZ, BEAM), BF16),
            dma(26), dma(11), dma(11), dma(11), dma(11),
            dma(GB), dma(GB), dma(GA), dma(GA), pltpu.SemaphoreType.DMA, pltpu.SemaphoreType.DMA,
        ],
        compiler_params=pltpu.CompilerParams(
            collective_id=0, has_side_effects=True, vmem_limit_bytes=50 * 1024 * 1024
        ),
    )(
        alpha, vel_x, vel_z, divergence, press_guess, panel_records,
        panel_dest.reshape(1, PAN), panel_segment.reshape(1, PAN),
    )
    outs = [pltpu.with_memory_space_constraint(o, pltpu.VMEM) for o in outs]
    return pl.pallas_call(
        deliver,
        out_shape=tuple(jax.ShapeDtypeStruct(o.shape, o.dtype) for o in outs),
        in_specs=[pl.BlockSpec(memory_space=pl.ANY)] * 3,
        out_specs=(hbm,) * 3,
        scratch_shapes=[dma(3)],
        compiler_params=pltpu.CompilerParams(vmem_limit_bytes=1024 * 1024),
    )(*outs)


def solution(mesh):
    field = P("slab", "depth", None)
    rows = P(("slab", "depth"), None)
    return jax.shard_map(
        body, mesh=mesh, in_specs=(field,) * 5 + (rows,) * 3,
        out_specs=(field, field, rows), check_vma=False,
    )
```

```python
import jax
import jax.numpy as jnp
from jax import lax
from jax.experimental import pallas as pl
from jax.experimental.pallas import tpu as pltpu
from jax.sharding import PartitionSpec as P

MESH = pl.DeviceIdType.MESH
F32, BF16, I32 = jnp.float32, jnp.bfloat16, jnp.int32
CX, CZ, BEAM, LANES = 16, 64, 512, 128
NB = BEAM // LANES
ROW0 = 8
PADZ = CZ + 16
SLABS, DEPTHS = 32, 4
GA, GB = 8, 16
CAP = 4
SLOTS = GA * GB * CAP
PAN = 256
REC_B, REC_A = GA * CAP, GB * CAP
META = 16


def iota(shape, dim):
    return lax.broadcasted_iota(I32, shape, dim)


def onehot(cond):
    return jnp.where(cond, 1.0, 0.0).astype(BF16)


def dot(a, b):
    return jnp.dot(a, b, preferred_element_type=F32)


def recip(d):
    r = pl.reciprocal(d, approx=True)
    return r * (2.0 - d * r)


def kernel(
    alpha_h, velx_h, velz_h, div_h, press_h, rec_h, dest_h, seg_h,
    press_o, alpha_o, panel_o,
    stage, rec_ref, dest_ref, seg_ref, al, vx, vz, div, rho, p0, p1, p2,
    axm, axp, azm, azp, aym, ayp, rr,
    zs, zr, xb, xr, acc,
    s1, r1, s2, r2, wb, tb,
    q_s, g_s, perm_s, spread, rmat, pb,
    load_sem, xs_sem, xr_sem, zs_sem, zr_sem,
    b1s, b1r, a1s, a1r, home_s, home_r,
):
    slab = lax.axis_index("slab")
    depth = lax.axis_index("depth")
    up_s, dn_s = (slab + 1) % SLABS, (slab + SLABS - 1) % SLABS
    up_d, dn_d = (depth + 1) % DEPTHS, (depth + DEPTHS - 1) % DEPTHS
    x_up, x_dn = (up_s, depth), (dn_s, depth)
    z_up, z_dn = (slab, up_d), (slab, dn_d)
    b_me, core = slab // 2, slab % 2
    a_me = core * DEPTHS + depth
    me = slab * DEPTHS + depth

    def b_peer(k):
        b = (b_me + k) % GB
        return b, (b * 2 + core, depth)

    def a_peer(k):
        a = (a_me + k) % GA
        return a, (b_me * 2 + a // DEPTHS, a % DEPTHS)

    loads = {}
    sem_i = 0

    def load(name, pairs):
        nonlocal sem_i
        loads[name] = []
        for src, dst in pairs:
            c = pltpu.make_async_copy(src, dst, load_sem.at[sem_i])
            c.start()
            sem_i += 1
            loads[name].append(c)

    def loaded(name):
        for c in loads[name]:
            c.wait()

    def field(src, dst):
        return [(src.at[:, :, pl.ds(y * LANES, LANES)], dst(y)) for y in range(NB)]

    load("panels", [(dest_h, dest_ref), (seg_h, seg_ref), (rec_h, rec_ref)])
    load("planes", [
        (alpha_h.at[CX - 1], stage.at[0]), (alpha_h.at[0], stage.at[1]), (velx_h.at[0], stage.at[2]),
    ])
    load("al", field(alpha_h, lambda y: al.at[pl.ds(1, CX), y, pl.ds(ROW0, CZ), :]))
    load("vz", field(velz_h, lambda y: vz.at[:, y, pl.ds(0, CZ), :]))
    load("vx", field(velx_h, lambda y: vx.at[pl.ds(0, CX), y, :, :]))
    load("p0", field(press_h, lambda y: p0.at[pl.ds(1, CX), y, pl.ds(ROW0, CZ), :]))
    load("div", field(div_h, lambda y: div.at[:, y, :, :]))

    barrier = pltpu.get_barrier_semaphore()
    for dev in (x_up, x_dn, z_up, z_dn):
        pl.semaphore_signal(barrier, inc=1, device_id=dev, device_id_type=MESH)

    def sig_b(k, c):
        pl.semaphore_signal(barrier, inc=1, device_id=b_peer(k)[1], device_id_type=MESH)
        return c

    def sig_a(k, c):
        pl.semaphore_signal(barrier, inc=1, device_id=a_peer(k)[1], device_id_type=MESH)
        return c

    lax.fori_loop(1, GB, sig_b, 0)
    lax.fori_loop(1, GA, sig_a, 0)

    def rcopy(src, dst, ss, rs, dev):
        return pltpu.make_async_remote_copy(
            src_ref=src, dst_ref=dst, send_sem=ss, recv_sem=rs,
            device_id=dev, device_id_type=MESH,
        )

    def xcopy(i, dev):
        return rcopy(xb.at[i], xr.at[i], xs_sem.at[i], xr_sem.at[i], dev)

    def zcopy(i, dev):
        return rcopy(zs.at[i], zr.at[i], zs_sem.at[i], zr_sem.at[i], dev)

    def xpair(i):
        return [xcopy(i, x_up), xcopy(i + 1, x_dn)]

    def pack_x(i, ref):
        xb[i] = ref[CX, :, ROW0 : ROW0 + CZ, :].astype(BF16)
        xb[i + 1] = ref[1, :, ROW0 : ROW0 + CZ, :].astype(BF16)

    def fill_x(i, ref):
        low, high = xr[i].astype(F32), xr[i + 1].astype(F32)
        ref[0, :, ROW0 : ROW0 + CZ, :] = jnp.where(slab == 0, 0.0, low)
        ref[CX + 1, :, ROW0 : ROW0 + CZ, :] = jnp.where(slab == SLABS - 1, 0.0, high)

    def zpair(i):
        return [zcopy(i, z_up), zcopy(i + 1, z_dn)]

    def pack_z(items):
        def step(g, c):
            for k in range(4):
                x = g * 4 + k
                for i, ref, xo, r in items:
                    zs[i, x] = ref[x + xo, :, r, :]
            return c

        lax.fori_loop(0, CX // 4, step, 0)

    def fill_z(items):
        def step(g, c):
            for k in range(4):
                x = g * 4 + k
                for i, ref, xo, r, edge in items:
                    ref[x + xo, :, r, :] = jnp.where(depth == edge, 0.0, zr[i, x])
            return c

        lax.fori_loop(0, CX // 4, step, 0)

    sends = []

    def start(copies):
        for c in copies:
            c.start()
        sends.extend(copies)

    loaded("panels")
    dest, seg = dest_ref[...], seg_ref[...]
    own = onehot(iota((GA * GB, PAN), 0) == dest)
    before = dot(own, onehot(iota((PAN, PAN), 0) < iota((PAN, PAN), 1)))
    slot = jnp.sum(own.astype(F32) * before, axis=0, keepdims=True)
    lane_of = (dest >> 3) * CAP + slot.astype(I32)
    place = (dest & (GA - 1)) * REC_A + lane_of
    packed = dot(onehot(iota((SLOTS, PAN), 0) == place), rec_ref[...]).astype(BF16)
    row = iota((LANES, PAN), 0)
    hi, lo = (seg >> 6).astype(F32), (seg & 63).astype(F32)
    bt = jnp.where(row == lane_of, hi, 0.0) + jnp.where(row == lane_of + REC_A, lo, 0.0)
    meta = lax.dot_general(
        onehot(iota((16, PAN), 0) == (dest & (GA - 1))), bt.astype(BF16),
        (((1,), (1,)), ((), ())), preferred_element_type=F32,
    )
    for a in range(GA):
        s1[a, 0:REC_A, :] = packed[a * REC_A : (a + 1) * REC_A]
        s1[a, REC_A:, :] = jnp.broadcast_to(meta[a : a + 1], (META, LANES)).astype(BF16)

    pl.semaphore_wait(barrier, 4 + (GB - 1) + (GA - 1))

    def a1_start(k, c):
        a, dev = a_peer(k)
        rcopy(s1.at[a], r1.at[a_me], a1s.at[k], a1r.at[k], dev).start()
        return c

    lax.fori_loop(1, GA, a1_start, 0)
    loaded("planes")
    for i in range(3):
        for y in range(NB):
            xb[i, y] = stage[i, :, y * LANES : (y + 1) * LANES].astype(BF16)
    e_al, e_vx = xpair(0), [xcopy(2, x_dn)]
    start(e_al + e_vx)

    r1[a_me] = s1[a_me]

    loaded("al")
    loaded("vz")
    pack_z([(0, al, 1, ROW0 + CZ - 1), (1, al, 1, ROW0), (2, vz, 0, 0)])
    ez_al, ez_vz = zpair(0), [zcopy(2, z_dn)]
    start(ez_al + ez_vz)
    loaded("vx")
    loaded("p0")
    pack_x(3, p0)
    pack_z([(3, p0, 1, ROW0 + CZ - 1), (4, p0, 1, ROW0)])
    e_p0, ez_p0 = xpair(3), zpair(3)
    start(e_p0 + ez_p0)

    answer = dest * CAP + slot.astype(I32)
    place_t = jnp.broadcast_to(answer.astype(F32), (LANES, PAN)).T
    for c in range(SLOTS // LANES):
        q_s[:, c * LANES : (c + 1) * LANES] = onehot(
            place_t == (iota((PAN, LANES), 1) + c * LANES).astype(F32)
        )
    pr, pc = iota((SLOTS, SLOTS), 0), iota((SLOTS, SLOTS), 1)
    perm_s[...] = onehot(
        pc == (((pr >> 2) & (GA - 1)) * REC_A + (pr >> 5) * CAP + (pr & 3))
    )

    lane = iota((NB, 8, LANES), 2)
    zero1 = jnp.zeros((1, 8, LANES), F32)

    def y_minus(v):
        r = pltpu.roll(v, 1, 2)
        return jnp.where(lane == 0, jnp.concatenate([zero1, r[: NB - 1]], axis=0), r)

    def y_plus(v):
        r = pltpu.roll(v, LANES - 1, 2)
        return jnp.where(lane == LANES - 1, jnp.concatenate([r[1:], zero1], axis=0), r)

    def at(ref, x, z, shift=0):
        return ref[x, :, pl.ds(ROW0 + z * 8 + shift, 8), :]

    def raw(ref, x, z, shift=0):
        return ref[x, :, pl.ds(z * 8 + shift, 8), :]

    def to_out(ref, x, z, v):
        for y in range(NB):
            ref[x, pl.ds(z * 8, 8), y * LANES : (y + 1) * LANES] = v[y]

    def advect(xs, z):
        a, right, fx1, u1 = at(al, xs[0] + 1, z), None, None, None
        left, u0 = at(al, xs[0], z), raw(vx, xs[0], z)
        fx0 = u0 * jnp.where(u0 > 0, left, a)
        for x in xs:
            right, u1 = at(al, x + 2, z), raw(vx, x + 1, z)
            w0, w1 = raw(vz, x, z), raw(vz, x, z, 1)
            fx1 = u1 * jnp.where(u1 > 0, a, right)
            fz0 = w0 * jnp.where(w0 > 0, at(al, x + 1, z, -1), a)
            fz1 = w1 * jnp.where(w1 > 0, a, at(al, x + 1, z, 1))
            new = a - 0.2 * (fx1 - fx0 + fz1 - fz0)
            to_out(alpha_o, x, z, new)
            rho[x + 1, :, pl.ds(ROW0 + z * 8, 8), :] = 1.0 + 9.0 * new
            a, fx0 = right, fx1

    def first(xs, z, also_sweep=True):
        d = at(rho, xs[0] + 1, z)
        cm = recip(d + at(rho, xs[0], z))
        left, mid = at(p0, xs[0], z), at(p0, xs[0] + 1, z)
        for x in xs:
            beyond, right = at(rho, x + 2, z), at(p0, x + 2, z) if also_sweep else None
            cp = recip(d + beyond)
            zm, zp = recip(d + at(rho, x + 1, z, -1)), recip(d + at(rho, x + 1, z, 1))
            ym = recip(d + y_minus(d))
            yp = y_plus(ym)
            wall = jnp.where(lane[:1] == LANES - 1, recip(d[NB - 1 :]), yp[NB - 1 :])
            yp = jnp.concatenate([yp[: NB - 1], wall], axis=0)
            inv = recip((cm + cp) + (zm + zp) + (ym + yp))
            c = [v * inv for v in (cm, cp, zm, zp, ym, yp)]
            for ref, v in zip((axm, axp, azm, azp, aym, ayp), c):
                ref[x, :, pl.ds(z * 8, 8), :] = v
            half = 0.5 * inv
            r = raw(div, x, z) * half
            rr[x, :, pl.ds(z * 8, 8), :] = r
            div[x, :, pl.ds(z * 8, 8), :] = half
            d, cm, before, now = beyond, cp, left, mid
            left, mid = mid, right
            if not also_sweep:
                continue
            p1[x + 1, :, pl.ds(ROW0 + z * 8, 8), :] = (
                (c[0] * before + c[1] * right)
                + (c[2] * at(p0, x + 1, z, -1) + c[3] * at(p0, x + 1, z, 1))
                + (c[4] * y_minus(now) + c[5] * y_plus(now) - r)
            )

    def sweep(p, store, xs, z):
        left, mid = at(p, xs[0], z), at(p, xs[0] + 1, z)
        for x in xs:
            right = at(p, x + 2, z)
            store(
                x, z,
                (raw(axm, x, z) * left + raw(axp, x, z) * right)
                + (raw(azm, x, z) * at(p, x + 1, z, -1) + raw(azp, x, z) * at(p, x + 1, z, 1))
                + (raw(aym, x, z) * y_minus(mid) + raw(ayp, x, z) * y_plus(mid) - raw(rr, x, z)),
            )
            left, mid = mid, right

    def into(ref):
        def store(x, z, v):
            ref[x + 1, :, pl.ds(ROW0 + z * 8, 8), :] = v

        return store

    def coefficients(xs, z):
        first(xs, z, also_sweep=False)

    def sweep1(xs, z):
        sweep(p0, into(p1), xs, z)

    def sweep2(xs, z):
        sweep(p1, into(p2), xs, z)

    def sweep3(xs, z):
        sweep(p2, lambda x, z, v: to_out(press_o, x, z, v), xs, z)

    tiles = CZ // 8
    middle = tuple(range(1, CX - 1))

    def interior(fn, first, count):
        def step(i, c):
            fn(middle, first + i)
            return c

        lax.fori_loop(0, count, step, 0)

    def edges(fn):
        def step(i, c):
            fn(middle, i * (tiles - 1))
            return c

        lax.fori_loop(0, 2, step, 0)

    def ends(fn):
        def step(i, c):
            for k in range(4):
                fn((0,), i * 4 + k)
                fn((CX - 1,), i * 4 + k)
            return c

        lax.fori_loop(0, tiles // 4, step, 0)

    inside, early, fused = tiles - 2, 5, 2

    def recv(copies):
        for c in copies:
            c.wait_recv()

    interior(advect, 1, inside)
    def a1_wait(k, c):
        src = (a_me + GA - k) % GA
        rcopy(s1.at[src], r1.at[src], a1s.at[k], a1r.at[k], a_peer(k)[1]).wait_recv()
        return c

    lax.fori_loop(1, GA, a1_wait, 0)
    got = dot(perm_s[...], r1[:, 0:REC_A, :].reshape(SLOTS, LANES)).astype(BF16)
    mrow = iota((META, LANES), 0)
    m1 = jnp.zeros((META, LANES), F32)
    for a in range(GA):
        m1 = jnp.where(mrow == a, r1[a, REC_A:, :].astype(F32), m1)
    m1 = m1.astype(BF16)
    for b in range(GB):
        s2[b, 0:REC_B, :] = got[b * REC_B : (b + 1) * REC_B]
        s2[b, REC_B:, :] = m1

    def b1_start(k, c):
        b, dev = b_peer(k)
        rcopy(s2.at[b], r2.at[b_me], b1s.at[k], b1r.at[k], dev).start()
        return c

    for first_k, last_k in ((5, 12), (1, 5), (12, GB)):
        lax.fori_loop(first_k, last_k, b1_start, 0)
    r2[b_me] = s2[b_me]

    recv(ez_al + ez_vz)
    fill_z([(0, al, 1, ROW0 - 1, 0), (1, al, 1, ROW0 + CZ, DEPTHS - 1), (2, vz, 0, CZ, DEPTHS - 1)])
    edges(advect)

    recv(e_al + e_vx)
    fill_x(0, al)
    vx[CX] = jnp.where(slab == SLABS - 1, 0.0, xr[2].astype(F32))
    ends(advect)
    pack_x(5, rho)
    e_rho, ez_rho = xpair(5), zpair(5)
    start(e_rho)
    pack_z([(5, rho, 1, ROW0 + CZ - 1), (6, rho, 1, ROW0)])
    start(ez_rho)

    srow, scol = iota((SLOTS, GB * META), 0), iota((SLOTS, GB * META), 1)
    spread[...] = onehot(scol == (srow >> 5) * META + ((srow >> 2) & (GA - 1)))
    loaded("div")
    interior(first, 1, fused)
    interior(coefficients, 1 + fused, inside - fused)
    recv(ez_p0 + ez_rho)
    fill_z([
        (3, p0, 1, ROW0 - 1, 0), (4, p0, 1, ROW0 + CZ, DEPTHS - 1),
        (5, rho, 1, ROW0 - 1, 0), (6, rho, 1, ROW0 + CZ, DEPTHS - 1),
    ])
    edges(first)
    recv(e_p0 + e_rho)
    fill_x(3, p0)
    fill_x(5, rho)
    ends(first)

    def b1_wait(k, c):
        src = (b_me + GB - k) % GB
        rcopy(s2.at[src], r2.at[src], b1s.at[k], b1r.at[k], b_peer(k)[1]).wait_recv()
        return c

    lax.fori_loop(1, GB, b1_wait, 0)

    m2 = r2[:, REC_B:, :].reshape(GB * META, LANES)
    wide = dot(spread[...], m2)
    pick = iota((SLOTS, LANES), 1) - (iota((SLOTS, LANES), 0) & 3) - b_me * CAP
    own_meta = jnp.where((pick == 0) | (pick == REC_A), wide, 0.0).astype(BF16)
    weight_c = jnp.where(iota((LANES, LANES), 0) < REC_A, 64.0, 1.0).astype(BF16)
    weight_r = jnp.where(iota((META, LANES), 1) < REC_A, 64.0, 1.0).astype(BF16)
    seg_c = dot(own_meta, weight_c).astype(I32)
    seg_r = lax.dot_general(
        weight_r, own_meta, (((1,), (1,)), ((), ())), preferred_element_type=F32
    )[0:1].astype(I32)
    block_c, key_f = seg_c & 3, (seg_c >> 2).astype(F32)
    key_r = (seg_r >> 2).astype(F32)
    recs = r2[:, 0:REC_B, :].reshape(SLOTS, LANES)
    for y in range(NB):
        rmat[:, y * LANES : (y + 1) * LANES] = jnp.where(
            block_c == y, recs.astype(F32), 0.0
        ).astype(BF16)

    def hull(planes):
        z = iota((CZ, SLOTS), 0)
        cells = jnp.concatenate([z + x * CZ for x in planes], axis=0).astype(F32)
        h = dot(onehot(cells == key_r), rmat[...])
        for k, x in enumerate(planes):
            for y in range(NB):
                part = h[k * CZ : (k + 1) * CZ, y * LANES : (y + 1) * LANES] * div[x, y]
                rr[x, y] += part
                p1[x + 1, y, ROW0 : ROW0 + CZ, :] -= part

    hull((0, CX - 1))
    pack_x(7, p1)
    e_p1, ez_p1 = xpair(7), zpair(7)
    start(e_p1)
    for i in range(1, CX - 1, 7):
        hull(tuple(range(i, i + 7)))
    pack_z([(7, p1, 1, ROW0 + CZ - 1), (8, p1, 1, ROW0)])
    start(ez_p1)
    interior(sweep1, 1 + fused, inside - fused)
    tail = (CX - 2) * CZ
    column = iota((SLOTS, LANES), 1)
    for c in range(tail // LANES):
        g_s[:, c * LANES : (c + 1) * LANES] = onehot(
            key_f == (column + (c * LANES + CZ)).astype(F32)
        )
    outer = jnp.where(column < CZ, column, column + tail)
    g_s[:, tail:] = onehot(key_f == outer.astype(F32))
    interior(sweep2, 1, early)
    recv(ez_p1)
    fill_z([(7, p1, 1, ROW0 - 1, 0), (8, p1, 1, ROW0 + CZ, DEPTHS - 1)])
    recv(e_p1)
    fill_x(7, p1)
    ends(sweep2)
    pack_x(9, p2)
    e_p2, ez_p2 = xpair(9), zpair(9)
    start(e_p2)
    edges(sweep2)
    pack_z([(9, p2, 1, ROW0 + CZ - 1), (10, p2, 1, ROW0)])
    start(ez_p2)
    interior(sweep2, 1 + early, inside - early)
    interior(sweep3, 1, inside)
    recv(ez_p2)
    fill_z([(9, p2, 1, ROW0 - 1, 0), (10, p2, 1, ROW0 + CZ, DEPTHS - 1)])
    edges(sweep3)
    for x in range(1, CX - 1):
        pb[(x - 1) * CZ : x * CZ, :] = press_o[x].astype(BF16)
    acc[...] = dot(g_s[:, 0:tail], pb[0:tail, :])
    recv(e_p2)
    fill_x(9, p2)
    ends(sweep3)

    pb[tail : tail + CZ, :] = press_o[0].astype(BF16)
    pb[tail + CZ :, :] = press_o[CX - 1].astype(BF16)
    wet = acc[...] + dot(g_s[:, tail:], pb[tail:, :])
    back = jnp.zeros((SLOTS, LANES), F32)
    for y in range(NB):
        back = jnp.where(block_c == y, wet[:, y * LANES : (y + 1) * LANES], back)
    back = back.astype(BF16).astype(F32)
    wb[...] = back.reshape(GA * GB, CAP, LANES)

    far = (2, 1, 3, 0)
    for dz in far:
        for dx in far:
            b = (b_me // 4 + dz) % 4 * 4 + (b_me % 4 + dx) % 4

            def home(k, c, b=b):
                a = (a_me + k) % GA
                d = b * GA + a
                dev = (b * 2 + a // DEPTHS, a % DEPTHS)
                rcopy(wb.at[d], tb.at[me], home_s, home_r, dev).start()
                return c

            lax.fori_loop(1 if dz == dx == 0 else 0, GA, home, 0)
    others = pl.ds(0, GA * GB - 1)
    tb[me] = wb[me]
    pltpu.make_async_copy(wb.at[others], tb.at[others], home_r).wait()
    panel_o[...] = dot(q_s[...], tb[...].reshape(SLOTS, LANES).astype(BF16)).astype(BF16)
    pltpu.make_async_copy(wb.at[others], tb.at[others], home_s).wait()

    for c in sends:
        c.wait_send()

    def b_done(k, c):
        b, dev = b_peer(k)
        rcopy(s2.at[b], r2.at[b_me], b1s.at[k], b1r.at[k], dev).wait_send()
        return c

    def a_done(k, c):
        a, dev = a_peer(k)
        rcopy(s1.at[a], r1.at[a_me], a1s.at[k], a1r.at[k], dev).wait_send()
        return c

    lax.fori_loop(1, GB, b_done, 0)
    lax.fori_loop(1, GA, a_done, 0)


def deliver(press, alpha, panel, press_o, alpha_o, panel_o, sem):
    pairs = ((press, press_o), (alpha, alpha_o), (panel, panel_o))
    copies = [pltpu.make_async_copy(s, d, sem.at[i]) for i, (s, d) in enumerate(pairs)]
    for c in copies:
        c.start()
    for c in copies:
        c.wait()


def body(alpha, vel_x, vel_z, divergence, press_guess, panel_records, panel_dest, panel_segment):
    padded = pltpu.VMEM((CX + 2, NB, PADZ, LANES), F32)
    plain = pltpu.VMEM((CX, NB, CZ, LANES), F32)
    hbm = pl.BlockSpec(memory_space=pltpu.HBM)
    vmem = pl.BlockSpec(memory_space=pltpu.VMEM)
    dma = lambda n: pltpu.SemaphoreType.DMA((n,))
    field = pltpu.VMEM((CX, CZ, BEAM), F32)
    outs = pl.pallas_call(
        kernel,
        out_shape=(field, field, pltpu.VMEM((PAN, LANES), BF16)),
        in_specs=[hbm] * 8,
        out_specs=(vmem, vmem, vmem),
        scratch_shapes=[
            pltpu.VMEM((3, CZ, BEAM), F32),
            pltpu.VMEM((PAN, LANES), BF16), pltpu.VMEM((1, PAN), I32), pltpu.VMEM((1, PAN), I32),
            padded,
            pltpu.VMEM((CX + 1, NB, CZ, LANES), F32),
            pltpu.VMEM((CX, NB, CZ + 8, LANES), F32),
            plain,
            padded, padded, padded, padded,
            plain, plain, plain, plain, plain, plain, plain,
            pltpu.VMEM((11, CX, NB, LANES), F32),
            pltpu.VMEM((11, CX, NB, LANES), F32),
            pltpu.VMEM((11, NB, CZ, LANES), BF16),
            pltpu.VMEM((11, NB, CZ, LANES), BF16),
            pltpu.VMEM((SLOTS, BEAM), F32),
            pltpu.VMEM((GA, REC_A + META, LANES), BF16),
            pltpu.VMEM((GA, REC_A + META, LANES), BF16),
            pltpu.VMEM((GB, REC_B + META, LANES), BF16),
            pltpu.VMEM((GB, REC_B + META, LANES), BF16),
            pltpu.VMEM((GA * GB, CAP, LANES), F32),
            pltpu.VMEM((GA * GB, CAP, LANES), F32),
            pltpu.VMEM((PAN, SLOTS), BF16),
            pltpu.VMEM((SLOTS, CX * CZ), BF16),
            pltpu.VMEM((SLOTS, SLOTS), BF16),
            pltpu.VMEM((SLOTS, GB * META), BF16),
            pltpu.VMEM((SLOTS, BEAM), BF16),
            pltpu.VMEM((CX * CZ, BEAM), BF16),
            dma(26), dma(11), dma(11), dma(11), dma(11),
            dma(GB), dma(GB), dma(GA), dma(GA), pltpu.SemaphoreType.DMA, pltpu.SemaphoreType.DMA,
        ],
        compiler_params=pltpu.CompilerParams(
            collective_id=0, has_side_effects=True, vmem_limit_bytes=50 * 1024 * 1024
        ),
    )(
        alpha, vel_x, vel_z, divergence, press_guess, panel_records,
        panel_dest.reshape(1, PAN), panel_segment.reshape(1, PAN),
    )
    outs = [pltpu.with_memory_space_constraint(o, pltpu.VMEM) for o in outs]
    return pl.pallas_call(
        deliver,
        out_shape=tuple(jax.ShapeDtypeStruct(o.shape, o.dtype) for o in outs),
        in_specs=[pl.BlockSpec(memory_space=pl.ANY)] * 3,
        out_specs=(hbm,) * 3,
        scratch_shapes=[dma(3)],
        compiler_params=pltpu.CompilerParams(vmem_limit_bytes=1024 * 1024),
    )(*outs)


def solution(mesh):
    field = P("slab", "depth", None)
    rows = P(("slab", "depth"), None)
    return jax.shard_map(
        body, mesh=mesh, in_specs=(field,) * 5 + (rows,) * 3,
        out_specs=(field, field, rows), check_vma=False,
    )
```

```python
import jax
import jax.numpy as jnp
from jax import lax
from jax.experimental import pallas as pl
from jax.experimental.pallas import tpu as pltpu
from jax.sharding import PartitionSpec as P

MESH = pl.DeviceIdType.MESH
F32, BF16, I32 = jnp.float32, jnp.bfloat16, jnp.int32
CX, CZ, BEAM, LANES = 16, 64, 512, 128
NB = BEAM // LANES
ROW0 = 8
PADZ = CZ + 16
SLABS, DEPTHS = 32, 4
GA, GB = 8, 16
CAP = 4
SLOTS = GA * GB * CAP
PAN = 256
REC_B, REC_A = GA * CAP, GB * CAP
META = 16


def iota(shape, dim):
    return lax.broadcasted_iota(I32, shape, dim)


def onehot(cond):
    return jnp.where(cond, 1.0, 0.0).astype(BF16)


def dot(a, b):
    return jnp.dot(a, b, preferred_element_type=F32)


def recip(d):
    r = pl.reciprocal(d, approx=True)
    return r * (2.0 - d * r)


def kernel(
    alpha_h, velx_h, velz_h, div_h, press_h, rec_h, dest_h, seg_h,
    press_o, alpha_o, panel_o,
    stage, rec_ref, dest_ref, seg_ref, al, vx, vz, div, rho, p0, p1, p2,
    axm, axp, azm, azp, aym, ayp, rr,
    zs, zr, xb, xr, acc,
    s1, r1, s2, r2, wb, tb,
    q_s, g_s, perm_s, spread, rmat, pb,
    load_sem, xs_sem, xr_sem, zs_sem, zr_sem,
    b1s, b1r, a1s, a1r, home_s, home_r,
):
    slab = lax.axis_index("slab")
    depth = lax.axis_index("depth")
    up_s, dn_s = (slab + 1) % SLABS, (slab + SLABS - 1) % SLABS
    up_d, dn_d = (depth + 1) % DEPTHS, (depth + DEPTHS - 1) % DEPTHS
    x_up, x_dn = (up_s, depth), (dn_s, depth)
    z_up, z_dn = (slab, up_d), (slab, dn_d)
    b_me, core = slab // 2, slab % 2
    a_me = core * DEPTHS + depth
    me = slab * DEPTHS + depth

    def b_peer(k):
        b = (b_me + k) % GB
        return b, (b * 2 + core, depth)

    def a_peer(k):
        a = (a_me + k) % GA
        return a, (b_me * 2 + a // DEPTHS, a % DEPTHS)

    loads = {}
    sem_i = 0

    def load(name, pairs):
        nonlocal sem_i
        loads[name] = []
        for src, dst in pairs:
            c = pltpu.make_async_copy(src, dst, load_sem.at[sem_i])
            c.start()
            sem_i += 1
            loads[name].append(c)

    def loaded(name):
        for c in loads[name]:
            c.wait()

    def field(src, dst):
        return [(src.at[:, :, pl.ds(y * LANES, LANES)], dst(y)) for y in range(NB)]

    load("panels", [(dest_h, dest_ref), (seg_h, seg_ref), (rec_h, rec_ref)])
    load("planes", [
        (alpha_h.at[CX - 1], stage.at[0]), (alpha_h.at[0], stage.at[1]), (velx_h.at[0], stage.at[2]),
    ])
    load("al", field(alpha_h, lambda y: al.at[pl.ds(1, CX), y, pl.ds(ROW0, CZ), :]))
    load("vz", field(velz_h, lambda y: vz.at[:, y, pl.ds(0, CZ), :]))
    load("vx", field(velx_h, lambda y: vx.at[pl.ds(0, CX), y, :, :]))
    load("p0", field(press_h, lambda y: p0.at[pl.ds(1, CX), y, pl.ds(ROW0, CZ), :]))
    load("div", field(div_h, lambda y: div.at[:, y, :, :]))

    barrier = pltpu.get_barrier_semaphore()
    for dev in (x_up, x_dn, z_up, z_dn):
        pl.semaphore_signal(barrier, inc=1, device_id=dev, device_id_type=MESH)

    def sig_b(k, c):
        pl.semaphore_signal(barrier, inc=1, device_id=b_peer(k)[1], device_id_type=MESH)
        return c

    def sig_a(k, c):
        pl.semaphore_signal(barrier, inc=1, device_id=a_peer(k)[1], device_id_type=MESH)
        return c

    lax.fori_loop(1, GB, sig_b, 0)
    lax.fori_loop(1, GA, sig_a, 0)

    def rcopy(src, dst, ss, rs, dev):
        return pltpu.make_async_remote_copy(
            src_ref=src, dst_ref=dst, send_sem=ss, recv_sem=rs,
            device_id=dev, device_id_type=MESH,
        )

    def xcopy(i, dev):
        return rcopy(xb.at[i], xr.at[i], xs_sem.at[i], xr_sem.at[i], dev)

    def zcopy(i, dev):
        return rcopy(zs.at[i], zr.at[i], zs_sem.at[i], zr_sem.at[i], dev)

    def xpair(i):
        return [xcopy(i, x_up), xcopy(i + 1, x_dn)]

    def pack_x(i, ref):
        xb[i] = ref[CX, :, ROW0 : ROW0 + CZ, :].astype(BF16)
        xb[i + 1] = ref[1, :, ROW0 : ROW0 + CZ, :].astype(BF16)

    def fill_x(i, ref):
        low, high = xr[i].astype(F32), xr[i + 1].astype(F32)
        ref[0, :, ROW0 : ROW0 + CZ, :] = jnp.where(slab == 0, 0.0, low)
        ref[CX + 1, :, ROW0 : ROW0 + CZ, :] = jnp.where(slab == SLABS - 1, 0.0, high)

    def zpair(i):
        return [zcopy(i, z_up), zcopy(i + 1, z_dn)]

    def pack_z(items):
        def step(g, c):
            for k in range(4):
                x = g * 4 + k
                for i, ref, xo, r in items:
                    zs[i, x] = ref[x + xo, :, r, :]
            return c

        lax.fori_loop(0, CX // 4, step, 0)

    def fill_z(items):
        def step(g, c):
            for k in range(4):
                x = g * 4 + k
                for i, ref, xo, r, edge in items:
                    ref[x + xo, :, r, :] = jnp.where(depth == edge, 0.0, zr[i, x])
            return c

        lax.fori_loop(0, CX // 4, step, 0)

    sends = []

    def start(copies):
        for c in copies:
            c.start()
        sends.extend(copies)

    loaded("panels")
    dest, seg = dest_ref[...], seg_ref[...]
    own = onehot(iota((GA * GB, PAN), 0) == dest)
    before = dot(own, onehot(iota((PAN, PAN), 0) < iota((PAN, PAN), 1)))
    slot = jnp.sum(own.astype(F32) * before, axis=0, keepdims=True)
    lane_of = (dest >> 3) * CAP + slot.astype(I32)
    place = (dest & (GA - 1)) * REC_A + lane_of
    packed = dot(onehot(iota((SLOTS, PAN), 0) == place), rec_ref[...]).astype(BF16)
    row = iota((LANES, PAN), 0)
    hi, lo = (seg >> 6).astype(F32), (seg & 63).astype(F32)
    bt = jnp.where(row == lane_of, hi, 0.0) + jnp.where(row == lane_of + REC_A, lo, 0.0)
    meta = lax.dot_general(
        onehot(iota((16, PAN), 0) == (dest & (GA - 1))), bt.astype(BF16),
        (((1,), (1,)), ((), ())), preferred_element_type=F32,
    )
    for a in range(GA):
        s1[a, 0:REC_A, :] = packed[a * REC_A : (a + 1) * REC_A]
        s1[a, REC_A:, :] = jnp.broadcast_to(meta[a : a + 1], (META, LANES)).astype(BF16)

    pl.semaphore_wait(barrier, 4 + (GB - 1) + (GA - 1))

    def a1_start(k, c):
        a, dev = a_peer(k)
        rcopy(s1.at[a], r1.at[a_me], a1s.at[k], a1r.at[k], dev).start()
        return c

    lax.fori_loop(1, GA, a1_start, 0)
    loaded("planes")
    for i in range(3):
        for y in range(NB):
            xb[i, y] = stage[i, :, y * LANES : (y + 1) * LANES].astype(BF16)
    e_al, e_vx = xpair(0), [xcopy(2, x_dn)]
    start(e_al + e_vx)

    r1[a_me] = s1[a_me]

    loaded("al")
    loaded("vz")
    pack_z([(0, al, 1, ROW0 + CZ - 1), (1, al, 1, ROW0), (2, vz, 0, 0)])
    ez_al, ez_vz = zpair(0), [zcopy(2, z_dn)]
    start(ez_al + ez_vz)
    loaded("vx")
    loaded("p0")
    pack_x(3, p0)
    pack_z([(3, p0, 1, ROW0 + CZ - 1), (4, p0, 1, ROW0)])
    e_p0, ez_p0 = xpair(3), zpair(3)
    start(e_p0 + ez_p0)

    answer = dest * CAP + slot.astype(I32)
    place_t = jnp.broadcast_to(answer.astype(F32), (LANES, PAN)).T
    for c in range(SLOTS // LANES):
        q_s[:, c * LANES : (c + 1) * LANES] = onehot(
            place_t == (iota((PAN, LANES), 1) + c * LANES).astype(F32)
        )
    pr, pc = iota((SLOTS, SLOTS), 0), iota((SLOTS, SLOTS), 1)
    perm_s[...] = onehot(
        pc == (((pr >> 2) & (GA - 1)) * REC_A + (pr >> 5) * CAP + (pr & 3))
    )

    lane = iota((NB, 8, LANES), 2)
    zero1 = jnp.zeros((1, 8, LANES), F32)

    def y_minus(v):
        r = pltpu.roll(v, 1, 2)
        return jnp.where(lane == 0, jnp.concatenate([zero1, r[: NB - 1]], axis=0), r)

    def y_plus(v):
        r = pltpu.roll(v, LANES - 1, 2)
        return jnp.where(lane == LANES - 1, jnp.concatenate([r[1:], zero1], axis=0), r)

    def at(ref, x, z, shift=0):
        return ref[x, :, pl.ds(ROW0 + z * 8 + shift, 8), :]

    def raw(ref, x, z, shift=0):
        return ref[x, :, pl.ds(z * 8 + shift, 8), :]

    def to_out(ref, x, z, v):
        for y in range(NB):
            ref[x, pl.ds(z * 8, 8), y * LANES : (y + 1) * LANES] = v[y]

    def advect(xs, z):
        a, right, fx1, u1 = at(al, xs[0] + 1, z), None, None, None
        left, u0 = at(al, xs[0], z), raw(vx, xs[0], z)
        fx0 = u0 * jnp.where(u0 > 0, left, a)
        for x in xs:
            right, u1 = at(al, x + 2, z), raw(vx, x + 1, z)
            w0, w1 = raw(vz, x, z), raw(vz, x, z, 1)
            fx1 = u1 * jnp.where(u1 > 0, a, right)
            fz0 = w0 * jnp.where(w0 > 0, at(al, x + 1, z, -1), a)
            fz1 = w1 * jnp.where(w1 > 0, a, at(al, x + 1, z, 1))
            new = a - 0.2 * (fx1 - fx0 + fz1 - fz0)
            to_out(alpha_o, x, z, new)
            rho[x + 1, :, pl.ds(ROW0 + z * 8, 8), :] = 1.0 + 9.0 * new
            a, fx0 = right, fx1

    def first(xs, z, also_sweep=True):
        d = at(rho, xs[0] + 1, z)
        cm = recip(d + at(rho, xs[0], z))
        left, mid = at(p0, xs[0], z), at(p0, xs[0] + 1, z)
        for x in xs:
            beyond, right = at(rho, x + 2, z), at(p0, x + 2, z) if also_sweep else None
            cp = recip(d + beyond)
            zm, zp = recip(d + at(rho, x + 1, z, -1)), recip(d + at(rho, x + 1, z, 1))
            ym = recip(d + y_minus(d))
            yp = y_plus(ym)
            wall = jnp.where(lane[:1] == LANES - 1, recip(d[NB - 1 :]), yp[NB - 1 :])
            yp = jnp.concatenate([yp[: NB - 1], wall], axis=0)
            inv = recip((cm + cp) + (zm + zp) + (ym + yp))
            c = [v * inv for v in (cm, cp, zm, zp, ym, yp)]
            for ref, v in zip((axm, axp, azm, azp, aym, ayp), c):
                ref[x, :, pl.ds(z * 8, 8), :] = v
            half = 0.5 * inv
            r = raw(div, x, z) * half
            rr[x, :, pl.ds(z * 8, 8), :] = r
            div[x, :, pl.ds(z * 8, 8), :] = half
            d, cm, before, now = beyond, cp, left, mid
            left, mid = mid, right
            if not also_sweep:
                continue
            p1[x + 1, :, pl.ds(ROW0 + z * 8, 8), :] = (
                (c[0] * before + c[1] * right)
                + (c[2] * at(p0, x + 1, z, -1) + c[3] * at(p0, x + 1, z, 1))
                + (c[4] * y_minus(now) + c[5] * y_plus(now) - r)
            )

    def sweep(p, store, xs, z):
        left, mid = at(p, xs[0], z), at(p, xs[0] + 1, z)
        for x in xs:
            right = at(p, x + 2, z)
            store(
                x, z,
                (raw(axm, x, z) * left + raw(axp, x, z) * right)
                + (raw(azm, x, z) * at(p, x + 1, z, -1) + raw(azp, x, z) * at(p, x + 1, z, 1))
                + (raw(aym, x, z) * y_minus(mid) + raw(ayp, x, z) * y_plus(mid) - raw(rr, x, z)),
            )
            left, mid = mid, right

    def into(ref):
        def store(x, z, v):
            ref[x + 1, :, pl.ds(ROW0 + z * 8, 8), :] = v

        return store

    def coefficients(xs, z):
        first(xs, z, also_sweep=False)

    def sweep1(xs, z):
        sweep(p0, into(p1), xs, z)

    def sweep2(xs, z):
        sweep(p1, into(p2), xs, z)

    def sweep3(xs, z):
        sweep(p2, lambda x, z, v: to_out(press_o, x, z, v), xs, z)

    tiles = CZ // 8
    middle = tuple(range(1, CX - 1))

    def interior(fn, first, count):
        def step(i, c):
            fn(middle, first + i)
            return c

        lax.fori_loop(0, count, step, 0)

    def edges(fn):
        def step(i, c):
            fn(middle, i * (tiles - 1))
            return c

        lax.fori_loop(0, 2, step, 0)

    def ends(fn):
        def step(i, c):
            for k in range(4):
                fn((0,), i * 4 + k)
                fn((CX - 1,), i * 4 + k)
            return c

        lax.fori_loop(0, tiles // 4, step, 0)

    inside, early, fused = tiles - 2, 3, 0

    def recv(copies):
        for c in copies:
            c.wait_recv()

    interior(advect, 1, inside)
    def a1_wait(k, c):
        src = (a_me + GA - k) % GA
        rcopy(s1.at[src], r1.at[src], a1s.at[k], a1r.at[k], a_peer(k)[1]).wait_recv()
        return c

    lax.fori_loop(1, GA, a1_wait, 0)
    got = dot(perm_s[...], r1[:, 0:REC_A, :].reshape(SLOTS, LANES)).astype(BF16)
    mrow = iota((META, LANES), 0)
    m1 = jnp.zeros((META, LANES), F32)
    for a in range(GA):
        m1 = jnp.where(mrow == a, r1[a, REC_A:, :].astype(F32), m1)
    m1 = m1.astype(BF16)
    for b in range(GB):
        s2[b, 0:REC_B, :] = got[b * REC_B : (b + 1) * REC_B]
        s2[b, REC_B:, :] = m1

    def b1_start(k, c):
        b, dev = b_peer(k)
        rcopy(s2.at[b], r2.at[b_me], b1s.at[k], b1r.at[k], dev).start()
        return c

    for first_k, last_k in ((5, 12), (1, 5), (12, GB)):
        lax.fori_loop(first_k, last_k, b1_start, 0)
    r2[b_me] = s2[b_me]

    recv(ez_al + ez_vz)
    fill_z([(0, al, 1, ROW0 - 1, 0), (1, al, 1, ROW0 + CZ, DEPTHS - 1), (2, vz, 0, CZ, DEPTHS - 1)])
    edges(advect)

    recv(e_al + e_vx)
    fill_x(0, al)
    vx[CX] = jnp.where(slab == SLABS - 1, 0.0, xr[2].astype(F32))
    ends(advect)
    pack_x(5, rho)
    e_rho, ez_rho = xpair(5), zpair(5)
    start(e_rho)
    pack_z([(5, rho, 1, ROW0 + CZ - 1), (6, rho, 1, ROW0)])
    start(ez_rho)

    srow, scol = iota((SLOTS, GB * META), 0), iota((SLOTS, GB * META), 1)
    spread[...] = onehot(scol == (srow >> 5) * META + ((srow >> 2) & (GA - 1)))
    loaded("div")
    interior(first, 1, fused)
    interior(coefficients, 1 + fused, inside - fused)
    recv(ez_p0 + ez_rho)
    fill_z([
        (3, p0, 1, ROW0 - 1, 0), (4, p0, 1, ROW0 + CZ, DEPTHS - 1),
        (5, rho, 1, ROW0 - 1, 0), (6, rho, 1, ROW0 + CZ, DEPTHS - 1),
    ])
    edges(first)
    recv(e_p0 + e_rho)
    fill_x(3, p0)
    fill_x(5, rho)
    ends(first)

    def b1_wait(k, c):
        src = (b_me + GB - k) % GB
        rcopy(s2.at[src], r2.at[src], b1s.at[k], b1r.at[k], b_peer(k)[1]).wait_recv()
        return c

    lax.fori_loop(1, GB, b1_wait, 0)

    m2 = r2[:, REC_B:, :].reshape(GB * META, LANES)
    wide = dot(spread[...], m2)
    pick = iota((SLOTS, LANES), 1) - (iota((SLOTS, LANES), 0) & 3) - b_me * CAP
    own_meta = jnp.where((pick == 0) | (pick == REC_A), wide, 0.0).astype(BF16)
    weight_c = jnp.where(iota((LANES, LANES), 0) < REC_A, 64.0, 1.0).astype(BF16)
    weight_r = jnp.where(iota((META, LANES), 1) < REC_A, 64.0, 1.0).astype(BF16)
    seg_c = dot(own_meta, weight_c).astype(I32)
    seg_r = lax.dot_general(
        weight_r, own_meta, (((1,), (1,)), ((), ())), preferred_element_type=F32
    )[0:1].astype(I32)
    block_c, key_f = seg_c & 3, (seg_c >> 2).astype(F32)
    key_r = (seg_r >> 2).astype(F32)
    recs = r2[:, 0:REC_B, :].reshape(SLOTS, LANES)
    for y in range(NB):
        rmat[:, y * LANES : (y + 1) * LANES] = jnp.where(
            block_c == y, recs.astype(F32), 0.0
        ).astype(BF16)

    def hull(planes):
        z = iota((CZ, SLOTS), 0)
        cells = jnp.concatenate([z + x * CZ for x in planes], axis=0).astype(F32)
        h = dot(onehot(cells == key_r), rmat[...])
        for k, x in enumerate(planes):
            for y in range(NB):
                part = h[k * CZ : (k + 1) * CZ, y * LANES : (y + 1) * LANES] * div[x, y]
                rr[x, y] += part
                p1[x + 1, y, ROW0 : ROW0 + CZ, :] -= part

    hull((0, CX - 1))
    pack_x(7, p1)
    e_p1, ez_p1 = xpair(7), zpair(7)
    start(e_p1)
    for i in range(1, CX - 1, 7):
        hull(tuple(range(i, i + 7)))
    pack_z([(7, p1, 1, ROW0 + CZ - 1), (8, p1, 1, ROW0)])
    start(ez_p1)
    interior(sweep1, 1 + fused, inside - fused)
    tail = (CX - 2) * CZ
    column = iota((SLOTS, LANES), 1)
    for c in range(tail // LANES):
        g_s[:, c * LANES : (c + 1) * LANES] = onehot(
            key_f == (column + (c * LANES + CZ)).astype(F32)
        )
    outer = jnp.where(column < CZ, column, column + tail)
    g_s[:, tail:] = onehot(key_f == outer.astype(F32))
    interior(sweep2, 1, early)
    recv(ez_p1)
    fill_z([(7, p1, 1, ROW0 - 1, 0), (8, p1, 1, ROW0 + CZ, DEPTHS - 1)])
    recv(e_p1)
    fill_x(7, p1)
    ends(sweep2)
    pack_x(9, p2)
    e_p2, ez_p2 = xpair(9), zpair(9)
    start(e_p2)
    edges(sweep2)
    pack_z([(9, p2, 1, ROW0 + CZ - 1), (10, p2, 1, ROW0)])
    start(ez_p2)
    interior(sweep2, 1 + early, inside - early)
    interior(sweep3, 1, inside)
    recv(ez_p2)
    fill_z([(9, p2, 1, ROW0 - 1, 0), (10, p2, 1, ROW0 + CZ, DEPTHS - 1)])
    edges(sweep3)
    for x in range(1, CX - 1):
        pb[(x - 1) * CZ : x * CZ, :] = press_o[x].astype(BF16)
    acc[...] = dot(g_s[:, 0:tail], pb[0:tail, :])
    recv(e_p2)
    fill_x(9, p2)
    ends(sweep3)

    pb[tail : tail + CZ, :] = press_o[0].astype(BF16)
    pb[tail + CZ :, :] = press_o[CX - 1].astype(BF16)
    wet = acc[...] + dot(g_s[:, tail:], pb[tail:, :])
    back = jnp.zeros((SLOTS, LANES), F32)
    for y in range(NB):
        back = jnp.where(block_c == y, wet[:, y * LANES : (y + 1) * LANES], back)
    back = back.astype(BF16).astype(F32)
    wb[...] = back.reshape(GA * GB, CAP, LANES)

    far = (2, 1, 3, 0)
    for dz in far:
        for dx in far:
            b = (b_me // 4 + dz) % 4 * 4 + (b_me % 4 + dx) % 4

            def home(k, c, b=b):
                a = (a_me + k) % GA
                d = b * GA + a
                dev = (b * 2 + a // DEPTHS, a % DEPTHS)
                rcopy(wb.at[d], tb.at[me], home_s, home_r, dev).start()
                return c

            lax.fori_loop(1 if dz == dx == 0 else 0, GA, home, 0)
    others = pl.ds(0, GA * GB - 1)
    tb[me] = wb[me]
    pltpu.make_async_copy(wb.at[others], tb.at[others], home_r).wait()
    panel_o[...] = dot(q_s[...], tb[...].reshape(SLOTS, LANES).astype(BF16)).astype(BF16)
    pltpu.make_async_copy(wb.at[others], tb.at[others], home_s).wait()

    for c in sends:
        c.wait_send()

    def b_done(k, c):
        b, dev = b_peer(k)
        rcopy(s2.at[b], r2.at[b_me], b1s.at[k], b1r.at[k], dev).wait_send()
        return c

    def a_done(k, c):
        a, dev = a_peer(k)
        rcopy(s1.at[a], r1.at[a_me], a1s.at[k], a1r.at[k], dev).wait_send()
        return c

    lax.fori_loop(1, GB, b_done, 0)
    lax.fori_loop(1, GA, a_done, 0)


def deliver(press, alpha, panel, press_o, alpha_o, panel_o, sem):
    pairs = ((press, press_o), (alpha, alpha_o), (panel, panel_o))
    copies = [pltpu.make_async_copy(s, d, sem.at[i]) for i, (s, d) in enumerate(pairs)]
    for c in copies:
        c.start()
    for c in copies:
        c.wait()


def body(alpha, vel_x, vel_z, divergence, press_guess, panel_records, panel_dest, panel_segment):
    padded = pltpu.VMEM((CX + 2, NB, PADZ, LANES), F32)
    plain = pltpu.VMEM((CX, NB, CZ, LANES), F32)
    hbm = pl.BlockSpec(memory_space=pltpu.HBM)
    vmem = pl.BlockSpec(memory_space=pltpu.VMEM)
    dma = lambda n: pltpu.SemaphoreType.DMA((n,))
    field = pltpu.VMEM((CX, CZ, BEAM), F32)
    outs = pl.pallas_call(
        kernel,
        out_shape=(field, field, pltpu.VMEM((PAN, LANES), BF16)),
        in_specs=[hbm] * 8,
        out_specs=(vmem, vmem, vmem),
        scratch_shapes=[
            pltpu.VMEM((3, CZ, BEAM), F32),
            pltpu.VMEM((PAN, LANES), BF16), pltpu.VMEM((1, PAN), I32), pltpu.VMEM((1, PAN), I32),
            padded,
            pltpu.VMEM((CX + 1, NB, CZ, LANES), F32),
            pltpu.VMEM((CX, NB, CZ + 8, LANES), F32),
            plain,
            padded, padded, padded, padded,
            plain, plain, plain, plain, plain, plain, plain,
            pltpu.VMEM((11, CX, NB, LANES), F32),
            pltpu.VMEM((11, CX, NB, LANES), F32),
            pltpu.VMEM((11, NB, CZ, LANES), BF16),
            pltpu.VMEM((11, NB, CZ, LANES), BF16),
            pltpu.VMEM((SLOTS, BEAM), F32),
            pltpu.VMEM((GA, REC_A + META, LANES), BF16),
            pltpu.VMEM((GA, REC_A + META, LANES), BF16),
            pltpu.VMEM((GB, REC_B + META, LANES), BF16),
            pltpu.VMEM((GB, REC_B + META, LANES), BF16),
            pltpu.VMEM((GA * GB, CAP, LANES), F32),
            pltpu.VMEM((GA * GB, CAP, LANES), F32),
            pltpu.VMEM((PAN, SLOTS), BF16),
            pltpu.VMEM((SLOTS, CX * CZ), BF16),
            pltpu.VMEM((SLOTS, SLOTS), BF16),
            pltpu.VMEM((SLOTS, GB * META), BF16),
            pltpu.VMEM((SLOTS, BEAM), BF16),
            pltpu.VMEM((CX * CZ, BEAM), BF16),
            dma(26), dma(11), dma(11), dma(11), dma(11),
            dma(GB), dma(GB), dma(GA), dma(GA), pltpu.SemaphoreType.DMA, pltpu.SemaphoreType.DMA,
        ],
        compiler_params=pltpu.CompilerParams(
            collective_id=0, has_side_effects=True, vmem_limit_bytes=50 * 1024 * 1024
        ),
    )(
        alpha, vel_x, vel_z, divergence, press_guess, panel_records,
        panel_dest.reshape(1, PAN), panel_segment.reshape(1, PAN),
    )
    outs = [pltpu.with_memory_space_constraint(o, pltpu.VMEM) for o in outs]
    return pl.pallas_call(
        deliver,
        out_shape=tuple(jax.ShapeDtypeStruct(o.shape, o.dtype) for o in outs),
        in_specs=[pl.BlockSpec(memory_space=pl.ANY)] * 3,
        out_specs=(hbm,) * 3,
        scratch_shapes=[dma(3)],
        compiler_params=pltpu.CompilerParams(vmem_limit_bytes=1024 * 1024),
    )(*outs)


def solution(mesh):
    field = P("slab", "depth", None)
    rows = P(("slab", "depth"), None)
    return jax.shard_map(
        body, mesh=mesh, in_specs=(field,) * 5 + (rows,) * 3,
        out_specs=(field, field, rows), check_vma=False,
    )
```
